32 devices in a mesh: row: 4 (over y, x), col: 8 (over z, core).
Axes of the slice: x: 2, y: 2, z: 4, core: 2. Of those that a mesh axis runs over, the one named last changes fastest.
Arguments:
- embed: bfloat16 [16384, 128], P(('row', 'col')), may hold values from -6 to 6
- degree: int32 [16384], P(('row', 'col')), may hold values from 1 to 256
- tile_row: int32 [4, 8, 256], P('row', 'col'), may hold values from 0 to 31
- tile_col: int32 [4, 8, 256], P('row', 'col'), may hold values from 0 to 15
- tile_count: int32 [4, 8], P('row', 'col'), may hold values from 64 to 256, as said below
- tile_values: bfloat16 [4, 8, 256, 128, 128], P('row', 'col'), may hold values from 0 to 1
- new_rows: int32 [8192], P(('row', 'col')), may hold values from 0 to 16383, as said below
- new_bucket: int32 [8192], P(('row', 'col')), may hold values from 0 to 15
- bucket_norm: float32 [16], replicated, may hold values from 0.5 to 4
Outputs:
- new_embed: float32 [8192, 128], P(('row', 'col'))
The draws below stay inside these ranges and needn't reach their ends.
Inputs may be any that keep to these rules, and one draw needn't show every extreme that they name: `tile_count`: at least 64 slots live on each device, and some device has all 256 live. `new_rows`: the new nodes of one device lie in that device's row block.
All inputs are finite; a program needn't handle non-finite values.
Results may differ from the reference program's by a relative error of at most 0.0026.
Values may be sent and summed in bfloat16 or wider, within the bound.
No kernel may reach another device: no remote copies, remote signals or barrier semaphores. Data moves between devices by JAX's collectives and lax.ppermute only.
A program may use at most 128 MiB of HBM per device.

```python
import math
import jax
import jax.numpy as jnp
from jax import lax

EMB = 128
TILE = 128
HOPS = 3
BUCKETS = 16
ROWS_DEV = 512
TILES_DEV = 256
NEW_DEV = 256
NODES = 16384
NEW = 8192
N_ROW = 4
N_COL = 8


def draw_tile_count(key, part):
    total = N_ROW * N_COL
    counts = jax.random.randint(key, (total,), TILES_DEV // 4, TILES_DEV + 1)
    where_full = jax.random.randint(jax.random.fold_in(key, 7), (), 0, total)
    counts = counts.at[where_full].set(TILES_DEV)
    return counts.reshape(N_ROW, N_COL).astype(jnp.int32)


def draw_new_rows(key, part):
    total = NEW_DEV * N_ROW * N_COL
    position = jnp.arange(total, dtype=jnp.int32)
    block = position // NEW_DEV // N_COL
    inside = jax.random.randint(key, (total,), 0, N_COL * ROWS_DEV)
    return (block * (N_COL * ROWS_DEV) + inside).astype(jnp.int32)


def with_ends(entries, own_key, smallest, high):
    longest = entries.shape.index(max(entries.shape))
    spots = []
    for shift in (0, 1):
        where = [jax.random.randint(jax.random.fold_in(own_key, axis), (), 0, length) for axis, length in enumerate(entries.shape)]
        where[longest] = (where[longest] + shift) % entries.shape[longest]
        spots.append(tuple(where))
    return entries.at[spots[0]].set(smallest).at[spots[1]].set(high)


def block_levels(rng, extent, pieces, low, largest):
    level = 1.0
    for dim, blocks in pieces:
        draws = jax.random.uniform(jax.random.fold_in(jax.random.fold_in(rng, 6), dim), (blocks,), jnp.float32, low / len(pieces), largest / len(pieces))
        level = level * jnp.repeat(jnp.exp(draws), extent[dim] // blocks).reshape((-1,) + (1,) * (len(extent) - 1 - dim))
    return level


def noise(stream_key, extent, deviation, reach, pieces=(), held_as=jnp.bfloat16):
    array = jax.random.normal(stream_key, extent, jnp.float32) * deviation
    if len(pieces) > 0:
        array = block_levels(stream_key, extent, pieces, -0.22, 0.18) * array
    return jnp.clip(array, min=-reach, max=reach).astype(held_as)


def setup_inputs(seed: int = 0) -> dict:
    seeds = jax.random.split(jax.random.key(seed), 10)
    embed = noise(seeds[0], (NODES, EMB), 1.0, 6.0, ((0, 32),))
    degree = with_ends(jax.random.randint(seeds[1], (NODES,), 1, 257), jax.random.fold_in(seeds[1], 1), 1, 256).astype(jnp.int32)
    tile_row = with_ends(jax.random.randint(seeds[2], (N_ROW, N_COL, TILES_DEV), 0, N_COL * ROWS_DEV // TILE), jax.random.fold_in(seeds[2], 1), 0, (N_COL * ROWS_DEV // TILE) - 1).astype(jnp.int32)
    tile_col = with_ends(jax.random.randint(seeds[3], (N_ROW, N_COL, TILES_DEV), 0, N_ROW * ROWS_DEV // TILE), jax.random.fold_in(seeds[3], 1), 0, (N_ROW * ROWS_DEV // TILE) - 1).astype(jnp.int32)
    tile_count = draw_tile_count(jax.random.fold_in(seeds[9], 71), 0)
    tile_values = jnp.clip(1.0 * jax.random.uniform(seeds[5], (N_ROW, N_COL, TILES_DEV, TILE, TILE), jnp.float32) ** block_levels(seeds[5], (N_ROW, N_COL, TILES_DEV, TILE, TILE), ((0, 4), (1, 8)), -0.2, 0.2), 0.0, 1.0).astype(jnp.bfloat16)
    new_rows = draw_new_rows(jax.random.fold_in(seeds[9], 71), 0)
    new_bucket = with_ends(jax.random.randint(seeds[7], (NEW,), 0, BUCKETS), jax.random.fold_in(seeds[7], 1), 0, BUCKETS - 1).astype(jnp.int32)
    bucket_norm = jnp.clip(jnp.exp(jax.random.uniform(seeds[8], (BUCKETS,), jnp.float32, math.log(0.5), math.log(4.0))), 0.5, 4.0)
    return dict(embed=embed, degree=degree, tile_row=tile_row, tile_col=tile_col, tile_count=tile_count, tile_values=tile_values, new_rows=new_rows, new_bucket=new_bucket, bucket_norm=bucket_norm)


def one_hop(state, tile_row, tile_col, tile_count, tile_values):
    grid = state.reshape(N_ROW, N_COL, ROWS_DEV, EMB)
    block_rows = N_COL * ROWS_DEV
    slots = jnp.arange(TILES_DEV, dtype=jnp.int32)

    def per_row(r):

        def per_col(total, c):
            cols = grid[:, c].reshape(N_ROW * ROWS_DEV // TILE, TILE, EMB)
            picked = cols[tile_col[r, c]].astype(jnp.float32)
            weights = tile_values[r, c].astype(jnp.float32)
            prod = jnp.einsum('tij,tjk->tik', weights, picked)
            live = slots < tile_count[r, c]
            prod = jnp.where(live[:, None, None], prod, jnp.float32(0.0))
            sums = jax.ops.segment_sum(prod, tile_row[r, c], num_segments=block_rows // TILE)
            return (total + sums.reshape(block_rows, EMB), None)
        total, _ = lax.scan(per_col, jnp.zeros((block_rows, EMB), jnp.float32), jnp.arange(N_COL, dtype=jnp.int32))
        return total
    return lax.map(per_row, jnp.arange(N_ROW, dtype=jnp.int32)).reshape(N_ROW * N_COL * ROWS_DEV, EMB)

def reference(embed, degree, tile_row, tile_col, tile_count, tile_values, new_rows, new_bucket, bucket_norm):
    scale = lax.rsqrt(degree.astype(jnp.float32))
    state = (scale[:, None] * embed.astype(jnp.float32)).astype(jnp.bfloat16)
    for hop in range(HOPS - 1):
        summed = one_hop(state, tile_row, tile_col, tile_count, tile_values)
        state = ((scale * scale)[:, None] * summed).astype(jnp.bfloat16)
    last = one_hop(state, tile_row, tile_col, tile_count, tile_values)
    picked = last[new_rows]
    target = bucket_norm[new_bucket]
    return target[:, None] * picked * lax.rsqrt(lax.optimization_barrier(jnp.sum(picked * picked, axis=1, keepdims=True)) + 1e-06)
```

```python
import functools

import jax
import jax.numpy as jnp
from jax import lax
from jax.experimental import pallas as pl
from jax.experimental.pallas import tpu as pltpu
from jax.sharding import PartitionSpec as P

HOPS = 3
GROUP = 4
SHIFT = 256
MIB = 1024 * 1024


def iota(shape, dim):
    return lax.broadcasted_iota(jnp.int32, shape, dim)


def to_column(row):
    n = row.shape[1]
    return jnp.sum(jnp.where(iota((n, n), 0) == iota((n, n), 1), row, 0.0), axis=1, keepdims=True)


def to_row(column):
    n = column.shape[0]
    return jnp.sum(jnp.where(iota((n, n), 0) == iota((n, n), 1), column, 0.0), axis=0, keepdims=True)


def plan_kernel(row_tiles, per_group, zero_tile, info_ref, tile_row_ref, tile_col_ref, plan_ref):
    slots = tile_row_ref.shape[1]
    length = plan_ref.shape[1]
    count, my_row, my_col = info_ref[0], info_ref[1], info_ref[2]
    half = row_tiles // 2
    row = tile_row_ref[...]
    rel = (row // per_group) ^ my_col
    order = (1 - rel % 2) * half + (rel // 2) * per_group + row % per_group
    order = jnp.where(iota((1, slots), 1) < count, order, row_tiles).astype(jnp.float32)
    col = tile_col_ref[...]
    source = ((col // per_group) ^ my_row) * per_group + col % per_group
    entry = (iota((1, slots), 1) * SHIFT + source).astype(jnp.float32)
    order_c = to_column(order)
    entry_c = to_column(entry)
    same = jnp.where((order_c == order) & (iota((slots, slots), 1) < iota((slots, slots), 0)), 1.0, 0.0)
    within = jnp.sum(same, axis=1, keepdims=True)
    tiles_r = iota((row_tiles, slots), 0).astype(jnp.float32)
    held = jnp.sum(jnp.where(tiles_r == order, 1.0, 0.0), axis=1, keepdims=True).astype(jnp.int32)
    steps = jnp.maximum((held + GROUP - 1) // GROUP, 1).astype(jnp.float32)
    square = (row_tiles, row_tiles)
    first_c = jnp.sum(jnp.where(iota(square, 1) < iota(square, 0), to_row(steps), 0.0), axis=1, keepdims=True)
    first_r = to_row(first_c)
    lanes = iota((slots, row_tiles), 1).astype(jnp.float32)
    start = jnp.sum(jnp.where(order_c == lanes, first_r, 0.0), axis=1, keepdims=True)
    place = jnp.where(order_c < row_tiles, GROUP * start + within, -1.0)
    hit = place == iota((slots, length), 1).astype(jnp.float32)
    listed = jnp.sum(jnp.where(hit, entry_c - zero_tile, 0.0), axis=0, keepdims=True) + zero_tile
    ends = first_c + steps
    step_no = iota((row_tiles, length), 1).astype(jnp.float32)
    owner = jnp.sum(jnp.where(ends <= step_no, 1.0, 0.0), axis=0, keepdims=True)
    odd_steps = jnp.sum(jnp.where(iota((row_tiles, 1), 0) == half, first_c, 0.0))
    all_steps = jnp.sum(steps)
    lane = iota((1, length), 1)
    sizes = jnp.where(lane == 0, odd_steps, jnp.where(lane == 1, all_steps, 0.0))
    plan_ref[0:1, :] = listed.astype(jnp.int32)
    plan_ref[1:2, :] = owner.astype(jnp.int32)
    plan_ref[2:3, :] = sizes.astype(jnp.int32)
    plan_ref[3:8, :] = jnp.zeros((5, length), jnp.int32)


def fill_state(pieces, state):
    at = 0
    for piece in pieces:
        state[at : at + piece.shape[0], :] = piece[...]
        at += piece.shape[0]
    state[at:, :] = jnp.zeros((state.shape[0] - at, state.shape[1]), state.dtype)


def multiply(plan_ref, weights_ref, state, total, first, last, base):
    tile = weights_ref.shape[1]

    def step(s, carry):
        left, right = [], []
        for j in range(GROUP):
            entry = plan_ref[0, s * GROUP + j]
            left.append(weights_ref[entry // SHIFT])
            right.append(state[pl.ds(pl.multiple_of((entry % SHIFT) * tile, tile), tile), :])
        prod = jnp.dot(
            jnp.concatenate(left, axis=1),
            jnp.concatenate(right, axis=0),
            preferred_element_type=jnp.float32,
        )
        at = pl.ds(pl.multiple_of((plan_ref[1, s] - base) * tile, tile), tile)
        total[at, :] += prod
        return carry

    lax.fori_loop(first, last, step, 0)


def half_kernel(pieces, part, plan_ref, *refs):
    state_refs, weights_ref, total, state = refs[:pieces], refs[pieces], refs[pieces + 1], refs[pieces + 2]
    half = total.shape[0] // weights_ref.shape[1]
    fill_state(state_refs, state)
    total[...] = jnp.zeros_like(total)
    first = plan_ref[2, 0] if part else 0
    last = plan_ref[2, 1] if part else plan_ref[2, 0]
    multiply(plan_ref, weights_ref, state, total, first, last, half * part)


def pick_kernel(pieces, plan_ref, place_ref, *refs):
    state_refs, weights_ref = refs[:pieces], refs[pieces]
    odd_ref, even_ref, state, total = refs[pieces + 1 :]
    fill_state(state_refs, state)
    total[...] = jnp.zeros_like(total)
    multiply(plan_ref, weights_ref, state, total, 0, plan_ref[2, 1], 0)
    rows = odd_ref.shape[0]
    for part, out in ((0, odd_ref), (1, even_ref)):

        def some(i, carry, part=part, out=out):
            for j in range(8):
                at = i * 8 + j
                out[pl.ds(at, 1), :] = total[pl.ds(place_ref[part, at], 1), :]
            return carry

        lax.fori_loop(0, rows // 8, some, 0)


VMEM_SPEC = pl.BlockSpec(memory_space=pltpu.VMEM)


def local(
    embed, degree, tile_row, tile_col, tile_count, tile_values, new_rows, new_bucket, bucket_norm
):
    rows_here, width = embed.shape
    ncols, nrows = lax.axis_size("col"), lax.axis_size("row")
    my_col, my_row = lax.axis_index("col"), lax.axis_index("row")
    weights = tile_values[0, 0]
    slots, tile = weights.shape[:2]
    block_rows = ncols * rows_here
    row_tiles = block_rows // tile
    per_group = rows_here // tile
    zero_tile = nrows * per_group
    half_rows = block_rows // 2
    length = -(-(slots + GROUP * row_tiles) // 128) * 128

    def swap(array, axis, size, mask):
        return lax.ppermute(array, axis, [(i, i ^ mask) for i in range(size)])

    near = jnp.stack([new_rows, swap(new_rows, "col", ncols, 1)])
    picks = jnp.concatenate([near] + [swap(near, "col", ncols, 2 * k) for k in range(1, ncols // 2)])
    inside = picks - my_row * block_rows
    rel = (inside // rows_here) ^ my_col
    place = (1 - rel % 2) * half_rows + (rel // 2) * rows_here + inside % rows_here
    place = place.reshape(ncols // 2, 2, -1).transpose(1, 0, 2)[::-1].reshape(2, -1)

    info = jnp.stack([tile_count[0, 0], my_row, my_col])
    plan = pl.pallas_call(
        functools.partial(plan_kernel, row_tiles, per_group, zero_tile),
        out_shape=jax.ShapeDtypeStruct((8, length), jnp.int32),
        in_specs=[pl.BlockSpec(memory_space=pltpu.SMEM), VMEM_SPEC, VMEM_SPEC],
        out_specs=VMEM_SPEC,
        name="plan",
    )(info, tile_row[0], tile_col[0])
    weights = pltpu.with_memory_space_constraint(weights, pltpu.VMEM)

    state_scratch = pltpu.VMEM(((zero_tile + 1) * tile, width), jnp.bfloat16)
    half_cost = pl.CostEstimate(
        flops=slots * tile * tile * width, bytes_accessed=slots * tile * tile, transcendentals=0
    )
    params = pltpu.CompilerParams(vmem_limit_bytes=24 * MIB)

    def products(pieces, part):
        return pl.pallas_call(
            functools.partial(half_kernel, nrows, part),
            out_shape=jax.ShapeDtypeStruct((half_rows, width), jnp.float32),
            grid_spec=pltpu.PrefetchScalarGridSpec(
                num_scalar_prefetch=1,
                grid=(),
                in_specs=[VMEM_SPEC] * (nrows + 1),
                out_specs=VMEM_SPEC,
                scratch_shapes=[state_scratch],
            ),
            compiler_params=params,
            cost_estimate=half_cost,
            name=("odd", "even")[part],
        )(plan, *pieces, weights)

    def picked_products(pieces):
        shape = jax.ShapeDtypeStruct((place.shape[1], width), jnp.float32)
        return pl.pallas_call(
            functools.partial(pick_kernel, nrows),
            out_shape=(shape, shape),
            grid_spec=pltpu.PrefetchScalarGridSpec(
                num_scalar_prefetch=2,
                grid=(),
                in_specs=[VMEM_SPEC] * (nrows + 1),
                out_specs=(VMEM_SPEC, VMEM_SPEC),
                scratch_shapes=[state_scratch, pltpu.VMEM((block_rows, width), jnp.float32)],
            ),
            compiler_params=params,
            cost_estimate=half_cost,
            name="last",
        )(plan, place, *pieces, weights)

    def spread(state):
        return [state] + [swap(state, "row", nrows, k) for k in range(1, nrows)]

    def collect(odd, even):
        rows = even.shape[0] // (ncols // 2)
        other = swap(odd, "col", ncols, 1)
        own = even[:rows] + other[:rows]
        for k in range(1, ncols // 2):
            at = slice(k * rows, (k + 1) * rows)
            sent = (even[at] + other[at]).astype(jnp.bfloat16)
            own = own + swap(sent, "col", ncols, 2 * k).astype(jnp.float32)
        return own

    scale = lax.rsqrt(degree.astype(jnp.float32))
    state = (scale[:, None] * embed.astype(jnp.float32)).astype(jnp.bfloat16)
    for hop in range(HOPS - 1):
        pieces = spread(state)
        summed = collect(products(pieces, 0), products(pieces, 1))
        state = ((scale * scale)[:, None] * summed).astype(jnp.bfloat16)
    picked = collect(*picked_products(spread(state)))
    buckets = jnp.arange(bucket_norm.shape[0], dtype=jnp.int32)
    target = jnp.sum(
        jnp.where(new_bucket[:, None] == buckets[None, :], bucket_norm[None, :], jnp.float32(0.0)),
        axis=1,
    )
    return (
        target[:, None]
        * picked
        * lax.rsqrt(jnp.sum(picked * picked, axis=1, keepdims=True) + 1e-06)
    )


def solution(mesh):
    in_specs = (
        P(("row", "col"), None),
        P(("row", "col")),
        P("row", "col", None),
        P("row", "col", None),
        P("row", "col"),
        P("row", "col", None, None, None),
        P(("row", "col")),
        P(("row", "col")),
        P(),
    )
    out_specs = P(("row", "col"), None)
    return jax.shard_map(local, mesh=mesh, in_specs=in_specs, out_specs=out_specs, check_vma=False)
```

```python
import functools

import jax
import jax.numpy as jnp
from jax import lax
from jax.experimental import pallas as pl
from jax.experimental.pallas import tpu as pltpu
from jax.sharding import PartitionSpec as P

HOPS = 3
GROUP = 4
UNROLL = 4
UNPICK = 16
BITS = 8
SHIFT = 1 << BITS
BYTE = 256
LANES = 128
PACK = 16
MIB = 1024 * 1024


def iota(shape, dim):
    return lax.broadcasted_iota(jnp.int32, shape, dim)


def to_column(row):
    n = row.shape[1]
    return jnp.sum(jnp.where(iota((n, n), 0) == iota((n, n), 1), row, 0.0), axis=1, keepdims=True)


def to_row(column):
    n = column.shape[0]
    return jnp.sum(jnp.where(iota((n, n), 0) == iota((n, n), 1), column, 0.0), axis=0, keepdims=True)


def plan_kernel(
    row_tiles, per_group, zero_tile, info_ref, tile_row_ref, tile_col_ref, weights_ref, plan_ref, held_ref, sem
):
    load = pltpu.make_async_copy(weights_ref, held_ref, sem)
    load.start()
    slots = tile_row_ref.shape[1]
    length = plan_ref.shape[1]
    count, my_row, my_col = info_ref[0], info_ref[1], info_ref[2]
    half = row_tiles // 2
    row = tile_row_ref[...]
    rel = (row // per_group) ^ my_col
    order = (1 - rel % 2) * half + (rel // 2) * per_group + row % per_group
    order = jnp.where(iota((1, slots), 1) < count, order, row_tiles).astype(jnp.float32)
    col = tile_col_ref[...]
    source = ((col // per_group) ^ my_row) * per_group + col % per_group
    entry = (iota((1, slots), 1) * SHIFT + source).astype(jnp.float32)
    order_c = to_column(order)
    entry_c = to_column(entry)
    same = jnp.where((order_c == order) & (iota((slots, slots), 1) < iota((slots, slots), 0)), 1.0, 0.0)
    within = jnp.sum(same, axis=1, keepdims=True)
    tiles_r = iota((row_tiles, slots), 0).astype(jnp.float32)
    held = jnp.sum(jnp.where(tiles_r == order, 1.0, 0.0), axis=1, keepdims=True).astype(jnp.int32)
    steps = (held + GROUP - 1) // GROUP
    upper = iota((row_tiles, 1), 0) < half
    odd_steps = jnp.sum(jnp.where(upper, steps, 0).astype(jnp.float32))
    even_steps = jnp.sum(jnp.where(upper, 0, steps).astype(jnp.float32))
    odd_end = pl.cdiv(odd_steps.astype(jnp.int32), UNROLL) * UNROLL
    all_end = odd_end + pl.cdiv(even_steps.astype(jnp.int32), UNROLL) * UNROLL
    steps = steps.astype(jnp.float32)
    square = (row_tiles, row_tiles)
    first_c = jnp.sum(jnp.where(iota(square, 1) < iota(square, 0), to_row(steps), 0.0), axis=1, keepdims=True)
    first_c = first_c + jnp.where(upper, 0.0, odd_end.astype(jnp.float32) - odd_steps)
    first_r = to_row(first_c)
    lanes = iota((slots, row_tiles), 1).astype(jnp.float32)
    start = jnp.sum(jnp.where(order_c == lanes, first_r, 0.0), axis=1, keepdims=True)
    place = jnp.where(order_c < row_tiles, GROUP * start + within, -1.0)
    hit = place == iota((slots, length), 1).astype(jnp.float32)
    listed = jnp.sum(jnp.where(hit, entry_c - zero_tile, 0.0), axis=0, keepdims=True) + zero_tile
    ends = first_c + steps
    step_no = iota((row_tiles, length), 1)
    owner = jnp.sum(jnp.where(ends <= step_no.astype(jnp.float32), 1.0, 0.0), axis=0, keepdims=True)
    owner = owner.astype(jnp.int32)
    lane = iota((1, length), 1)
    owner = jnp.where(lane < odd_end, jnp.minimum(owner, half - 1), jnp.minimum(owner, row_tiles - 1))
    plan_ref[0:1, :] = listed.astype(jnp.int32)
    plan_ref[1:2, :] = owner
    plan_ref[2:3, :] = jnp.where(lane == 0, odd_end // UNROLL, all_end // UNROLL)
    plan_ref[3:8, :] = jnp.zeros((5, length), jnp.int32)
    load.wait()


def fill_state(pieces, state):
    at = 0
    for piece in pieces:
        state[at : at + piece.shape[0], :] = piece[...]
        at += piece.shape[0]
    state[at:, :] = jnp.zeros((state.shape[0] - at, state.shape[1]), state.dtype)


def multiply(plan_ref, weights_ref, state, total, first, last, base):
    tile = weights_ref.shape[1]

    def turn(i, carry):
        prods = []
        for u in range(UNROLL):
            left, right = [], []
            for j in range(GROUP):
                entry = plan_ref[0, (i * UNROLL + u) * GROUP + j]
                left.append(weights_ref[entry >> BITS])
                right.append(state[pl.ds(pl.multiple_of((entry & (SHIFT - 1)) * tile, tile), tile), :])
            prods.append(
                jnp.dot(
                    jnp.concatenate(left, axis=1),
                    jnp.concatenate(right, axis=0),
                    preferred_element_type=jnp.float32,
                )
            )
        for u in range(UNROLL):
            at = pl.ds(pl.multiple_of((plan_ref[1, i * UNROLL + u] - base) * tile, tile), tile)
            total[at, :] += prods[u]
        return carry

    lax.fori_loop(first, last, turn, 0)


def half_kernel(pieces, part, extra, plan_ref, *refs):
    state_refs, weights_ref = refs[:pieces], refs[pieces]
    total, state = refs[-2:]
    rows = total.shape[0] - extra
    half = rows // weights_ref.shape[1]
    fill_state(state_refs, state)
    total[0:rows, :] = jnp.zeros((rows, total.shape[1]), total.dtype)
    first = plan_ref[2, 0] if part else 0
    last = plan_ref[2, 1] if part else plan_ref[2, 0]
    multiply(plan_ref, weights_ref, state, total, first, last, half * part)
    if extra:
        total[rows:, :] = refs[pieces + 1][...]


def merge_kernel(extra, even_ref, other_ref, *refs):
    own_ref, sent_refs = refs[-1 - extra[1]], refs[len(refs) - extra[1] :]
    rows = own_ref.shape[0]
    own_ref[...] = even_ref[0:rows, :] + other_ref[0:rows, :]
    for k, sent in enumerate(sent_refs):
        at = pl.ds((k + 1) * rows, rows)
        sent[0:rows, :] = (even_ref[at, :] + other_ref[at, :]).astype(sent.dtype)
        if extra[0]:
            sent[rows:, :] = refs[0][...]


def pick_rows(place_ref, part, total, out):
    def some(i, carry):
        for j in range(UNPICK):
            at = i * UNPICK + j
            out[pl.ds(at, 1), :] = total[pl.ds(place_ref[part, at], 1), :]
        return carry

    lax.fori_loop(0, out.shape[0] // UNPICK, some, 0)


def last_kernel(pieces, plan_ref, place_ref, *refs):
    state_refs, weights_ref = refs[:pieces], refs[pieces]
    odd_ref, total, state = refs[pieces + 1 :]
    fill_state(state_refs, state)
    total[...] = jnp.zeros_like(total)
    multiply(plan_ref, weights_ref, state, total, 0, plan_ref[2, 1], 0)
    pick_rows(place_ref, 0, total, odd_ref)


def pick_kernel(place_ref, total, even_ref):
    pick_rows(place_ref, 1, total, even_ref)


VMEM_SPEC = pl.BlockSpec(memory_space=pltpu.VMEM)


def local(
    embed, degree, tile_row, tile_col, tile_count, tile_values, new_rows, new_bucket, bucket_norm
):
    rows_here, width = embed.shape
    ncols, nrows = lax.axis_size("col"), lax.axis_size("row")
    my_col, my_row = lax.axis_index("col"), lax.axis_index("row")
    weights = tile_values[0, 0]
    slots, tile = weights.shape[:2]
    block_rows = ncols * rows_here
    row_tiles = block_rows // tile
    per_group = rows_here // tile
    zero_tile = nrows * per_group
    half_rows = block_rows // 2
    length = -(-(slots + GROUP * (row_tiles + 2 * UNROLL)) // LANES) * LANES

    def swap(array, axis, size, mask):
        return lax.ppermute(array, axis, [(i, i ^ mask) for i in range(size)])

    params = pltpu.CompilerParams(vmem_limit_bytes=24 * MIB)
    info = jnp.stack([tile_count[0, 0], my_row, my_col])
    plan, weights = pl.pallas_call(
        functools.partial(plan_kernel, row_tiles, per_group, zero_tile),
        out_shape=(
            jax.ShapeDtypeStruct((8, length), jnp.int32),
            pltpu.VMEM(weights.shape, weights.dtype),
        ),
        in_specs=[
            pl.BlockSpec(memory_space=pltpu.SMEM),
            VMEM_SPEC,
            VMEM_SPEC,
            pl.BlockSpec(memory_space=pltpu.HBM),
        ],
        out_specs=(VMEM_SPEC, VMEM_SPEC),
        scratch_shapes=[pltpu.SemaphoreType.DMA],
        compiler_params=params,
        name="plan",
    )(info, tile_row[0], tile_col[0], pltpu.with_memory_space_constraint(weights, pltpu.HBM))
    weights = pltpu.with_memory_space_constraint(weights, pltpu.VMEM)

    state_scratch = pltpu.VMEM(((zero_tile + 1) * tile, width), jnp.bfloat16)
    half_cost = pl.CostEstimate(
        flops=slots * tile * tile * width, bytes_accessed=slots * tile * tile, transcendentals=0
    )

    def products(pieces, part, extra=None):
        more = 0 if extra is None else extra.shape[0]
        return pl.pallas_call(
            functools.partial(half_kernel, nrows, part, more),
            out_shape=jax.ShapeDtypeStruct((half_rows + more, width), jnp.float32),
            grid_spec=pltpu.PrefetchScalarGridSpec(
                num_scalar_prefetch=1,
                grid=(),
                in_specs=[VMEM_SPEC] * (nrows + 1 + (more > 0)),
                out_specs=VMEM_SPEC,
                scratch_shapes=[state_scratch],
            ),
            compiler_params=params,
            cost_estimate=half_cost,
            name=("odd", "even")[part],
        )(plan, *pieces, weights, *(() if extra is None else (extra,)))

    def picked_products(pieces, place):
        picks = jax.ShapeDtypeStruct((place.shape[1], width), jnp.float32)
        odd, total = pl.pallas_call(
            functools.partial(last_kernel, nrows),
            out_shape=(picks, jax.ShapeDtypeStruct((block_rows, width), jnp.float32)),
            grid_spec=pltpu.PrefetchScalarGridSpec(
                num_scalar_prefetch=2,
                grid=(),
                in_specs=[VMEM_SPEC] * (nrows + 1),
                out_specs=(VMEM_SPEC, VMEM_SPEC),
                scratch_shapes=[state_scratch],
            ),
            compiler_params=params,
            cost_estimate=half_cost,
            name="last",
        )(plan, place, *pieces, weights)
        even = pl.pallas_call(
            pick_kernel,
            out_shape=picks,
            grid_spec=pltpu.PrefetchScalarGridSpec(
                num_scalar_prefetch=1, grid=(), in_specs=[VMEM_SPEC], out_specs=VMEM_SPEC
            ),
            compiler_params=params,
            cost_estimate=half_cost,
            name="pick",
        )(place, total)
        return odd, even

    def spread(state):
        return [state] + [swap(state, "row", nrows, k) for k in range(1, nrows)]

    def collect(other, even, extra=None):
        chips = ncols // 2
        rows = even.shape[0] // chips
        more = 0 if extra is None else extra.shape[0]
        own, *sent = pl.pallas_call(
            functools.partial(merge_kernel, (more, chips - 1)),
            out_shape=[jax.ShapeDtypeStruct((rows, width), jnp.float32)]
            + [jax.ShapeDtypeStruct((rows + more, width), jnp.bfloat16)] * (chips - 1),
            in_specs=[VMEM_SPEC] * (2 + (more > 0)),
            out_specs=[VMEM_SPEC] * chips,
            compiler_params=params,
            name="merge",
        )(even, other, *(() if extra is None else (extra,)))
        came = [swap(part, "col", ncols, 2 * k) for k, part in enumerate(sent, 1)]
        for part in came:
            own = own + part[:rows].astype(jnp.float32)
        return own, [part[rows:] for part in came]

    def swap_cores(odd):
        return swap(odd, "col", ncols, 1)

    inside = new_rows - my_row * block_rows
    new_here = inside.shape[0]
    id_rows = new_here // LANES
    as_rows = inside.astype(jnp.float32).reshape(id_rows, LANES)
    as_rows = jnp.pad(as_rows, ((0, -id_rows % 8), (0, 0)))

    def to_bytes(ids):
        return jnp.concatenate([ids // BYTE, ids % BYTE]).astype(jnp.bfloat16)

    def from_bytes(rows):
        high, low = rows[:id_rows].astype(jnp.int32), rows[id_rows : 2 * id_rows].astype(jnp.int32)
        return (high * BYTE + low).reshape(1, new_here)

    scale = lax.rsqrt(degree.astype(jnp.float32))
    state = (scale[:, None] * embed.astype(jnp.float32)).astype(jnp.bfloat16)
    for hop in range(HOPS - 1):
        pieces = spread(state)
        if hop == 0:
            other = swap_cores(products(pieces, 0, as_rows))
            near = other[half_rows : half_rows + id_rows].astype(jnp.int32)
            both = jnp.concatenate([to_bytes(inside.reshape(id_rows, LANES)), to_bytes(near)])
            both = jnp.pad(both, ((0, -both.shape[0] % PACK), (0, 0)))
            own, far = collect(other, products(pieces, 1), both)
            picks = [inside.reshape(1, new_here), near.reshape(1, new_here)]
            for rows in far:
                picks += [from_bytes(rows), from_bytes(rows[2 * id_rows :])]
            picks = jnp.concatenate(picks)
            rel = (picks // rows_here) ^ my_col
            place = (1 - rel % 2) * half_rows + (rel // 2) * rows_here + picks % rows_here
            place = place.reshape(ncols // 2, 2, -1).transpose(1, 0, 2)[::-1].reshape(2, -1)
        else:
            own, _ = collect(swap_cores(products(pieces, 0)), products(pieces, 1))
        state = ((scale * scale)[:, None] * own).astype(jnp.bfloat16)
    odd, even = picked_products(spread(state), place)
    picked, _ = collect(swap_cores(odd), even)
    buckets = jnp.arange(bucket_norm.shape[0], dtype=jnp.int32)
    target = jnp.sum(
        jnp.where(new_bucket[:, None] == buckets[None, :], bucket_norm[None, :], jnp.float32(0.0)),
        axis=1,
    )
    return (
        target[:, None]
        * picked
        * lax.rsqrt(jnp.sum(picked * picked, axis=1, keepdims=True) + 1e-06)
    )


def solution(mesh):
    in_specs = (
        P(("row", "col"), None),
        P(("row", "col")),
        P("row", "col", None),
        P("row", "col", None),
        P("row", "col"),
        P("row", "col", None, None, None),
        P(("row", "col")),
        P(("row", "col")),
        P(),
    )
    out_specs = P(("row", "col"), None)
    return jax.shard_map(local, mesh=mesh, in_specs=in_specs, out_specs=out_specs, check_vma=False)
```

```python
import functools

import jax
import jax.numpy as jnp
from jax import lax
from jax.experimental import pallas as pl
from jax.experimental.pallas import tpu as pltpu
from jax.sharding import PartitionSpec as P

HOPS = 3
HALVES = 2
CHUNKS = 2 * HALVES
GROUP = 4
UNROLL = 4
UNPICK = 16
BITS = 8
SHIFT = 1 << BITS
BYTE = 256
LANES = 128
PACK = 16
MIB = 1024 * 1024

VMEM_SPEC = pl.BlockSpec(memory_space=pltpu.VMEM)
SMEM_SPEC = pl.BlockSpec(memory_space=pltpu.SMEM)
HBM_SPEC = pl.BlockSpec(memory_space=pltpu.HBM)
PARAMS = pltpu.CompilerParams(vmem_limit_bytes=16 * MIB)


def iota(shape, dim):
    return lax.broadcasted_iota(jnp.int32, shape, dim)


def to_column(row):
    n = row.shape[1]
    return jnp.sum(jnp.where(iota((n, n), 0) == iota((n, n), 1), row, 0.0), axis=1, keepdims=True)


def to_row(column):
    n = column.shape[0]
    return jnp.sum(jnp.where(iota((n, n), 0) == iota((n, n), 1), column, 0.0), axis=0, keepdims=True)


def plan_kernel(
    row_tiles, per_group, zero_tile, count_ref, tile_row_hbm, tile_col_hbm, weights_hbm,
    plan_ref, weights_ref, tile_row_ref, tile_col_ref, sems,
):
    load = pltpu.make_async_copy(weights_hbm, weights_ref, sems.at[0])
    lists = (
        pltpu.make_async_copy(tile_row_hbm, tile_row_ref, sems.at[1]),
        pltpu.make_async_copy(tile_col_hbm, tile_col_ref, sems.at[2]),
    )
    for copy in lists:
        copy.start()
    load.start()
    for copy in lists:
        copy.wait()
    slots = tile_row_ref.shape[1]
    length = plan_ref.shape[1]
    my_row, my_col = lax.axis_index("row"), lax.axis_index("col")
    chunk_tiles = row_tiles // CHUNKS
    per_half = per_group // HALVES
    row = tile_row_ref[...]
    rel = (row // per_group) ^ my_col
    chunk = (1 - rel % 2) * HALVES + (row % per_group) // per_half
    order = chunk * chunk_tiles + (rel // 2) * per_half + row % per_half
    order = jnp.where(iota((1, slots), 1) < count_ref[0, 0], order, row_tiles).astype(jnp.float32)
    col = tile_col_ref[...]
    source = ((col // per_group) ^ my_row) * per_group + col % per_group
    entry = (iota((1, slots), 1) * SHIFT + source).astype(jnp.float32)
    order_c = to_column(order)
    entry_c = to_column(entry)
    same = jnp.where((order_c == order) & (iota((slots, slots), 1) < iota((slots, slots), 0)), 1.0, 0.0)
    within = jnp.sum(same, axis=1, keepdims=True)
    tiles_r = iota((row_tiles, slots), 0).astype(jnp.float32)
    held = jnp.sum(jnp.where(tiles_r == order, 1.0, 0.0), axis=1, keepdims=True).astype(jnp.int32)
    steps = (held + GROUP - 1) // GROUP
    steps_f = steps.astype(jnp.float32)
    square = (row_tiles, row_tiles)
    first = jnp.sum(jnp.where(iota(square, 1) < iota(square, 0), to_row(steps_f), 0.0), axis=1, keepdims=True)
    tile_no, step_no = iota((row_tiles, 1), 0), iota((1, length), 1)
    raw, begin, ends = jnp.int32(0), jnp.int32(0), []
    limit = jnp.full((1, length), row_tiles - 1, jnp.int32)
    shift = jnp.zeros((row_tiles, 1), jnp.int32)
    for c in range(CHUNKS):
        mine = (tile_no >= c * chunk_tiles) & (tile_no < (c + 1) * chunk_tiles)
        size = jnp.sum(jnp.where(mine, steps_f, 0.0)).astype(jnp.int32)
        shift = shift + jnp.where(mine, begin - raw, 0)
        end = begin + (size + UNROLL - 1) // UNROLL * UNROLL
        limit = jnp.where((step_no >= begin) & (step_no < end), (c + 1) * chunk_tiles - 1, limit)
        raw, begin = raw + size, end
        ends.append(end // UNROLL)
    first = first + shift.astype(jnp.float32)
    lanes = iota((slots, row_tiles), 1).astype(jnp.float32)
    start = jnp.sum(jnp.where(order_c == lanes, to_row(first), 0.0), axis=1, keepdims=True)
    place = jnp.where(order_c < row_tiles, GROUP * start + within, -1.0)
    hit = place == iota((slots, length), 1).astype(jnp.float32)
    listed = jnp.sum(jnp.where(hit, entry_c - zero_tile, 0.0), axis=0, keepdims=True) + zero_tile
    done = (first + steps_f) <= iota((row_tiles, length), 1).astype(jnp.float32)
    owner = jnp.sum(jnp.where(done, 1.0, 0.0), axis=0, keepdims=True).astype(jnp.int32)
    bounds = jnp.zeros((1, length), jnp.int32)
    for c, end in enumerate(ends):
        bounds = jnp.where(step_no == c + 1, end, bounds)
    plan_ref[0:1, :] = listed.astype(jnp.int32)
    plan_ref[1:2, :] = jnp.minimum(owner, limit)
    plan_ref[2:3, :] = bounds
    plan_ref[3:8, :] = jnp.zeros((5, length), jnp.int32)
    load.wait()


def fill_state(pieces, state, halves, tile):
    rows = pieces[0].shape[0]
    devices = (state.shape[0] - tile) // (rows * halves)
    for i, piece in enumerate(pieces):
        half, device = halves - 1 - i // devices, i % devices
        at = (device * halves + half) * rows
        state[at : at + rows, :] = piece[...]
    state[len(pieces) * rows :, :] = jnp.zeros((tile, state.shape[1]), state.dtype)


def multiply(plan_ref, weights_ref, state, total, chunk, chunks, chunk_tiles):
    tile = weights_ref.shape[1]
    total[...] = jnp.zeros_like(total)

    def turn(i, carry):
        prods = []
        for u in range(UNROLL):
            left, right = [], []
            for j in range(GROUP):
                entry = plan_ref[0, (i * UNROLL + u) * GROUP + j]
                left.append(weights_ref[entry >> BITS])
                right.append(state[pl.ds(pl.multiple_of((entry & (SHIFT - 1)) * tile, tile), tile), :])
            prods.append(
                jnp.dot(
                    jnp.concatenate(left, axis=1),
                    jnp.concatenate(right, axis=0),
                    preferred_element_type=jnp.float32,
                )
            )
        for u in range(UNROLL):
            row = plan_ref[1, i * UNROLL + u] - chunk * chunk_tiles
            at = pl.ds(pl.multiple_of(row * tile, tile), tile)
            total[at, :] += prods[u]
        return carry

    lax.fori_loop(plan_ref[2, chunk], plan_ref[2, chunk + chunks], turn, 0)


def odd_kernel(pieces, halves, plan_ref, *refs):
    weights_ref, extra_refs = refs[pieces], refs[pieces + 1 : -3]
    odd_ref, state, total = refs[-3:]
    rows = total.shape[0]
    fill_state(refs[:pieces], state, halves, weights_ref.shape[1])
    multiply(plan_ref, weights_ref, state, total, 0, HALVES, 0)
    odd_ref[0:rows, :] = total[...].astype(odd_ref.dtype)
    for extra in extra_refs:
        odd_ref[rows:, :] = extra[...]


def even0_kernel(plan_ref, state, weights_ref, even_ref):
    multiply(plan_ref, weights_ref, state, even_ref, HALVES, 1, even_ref.shape[0] // weights_ref.shape[1])


def even1_kernel(chips, plan_ref, state, weights_ref, after_ref, other_ref, *refs):
    extra_refs, own_ref, sent_refs, total = refs[: -chips - 1], refs[-chips - 1], refs[-chips:-1], refs[-1]
    rows = total.shape[0]
    multiply(plan_ref, weights_ref, state, total, HALVES + 1, 1, rows // weights_ref.shape[1])
    add_cores(chips, rows, total, other_ref, own_ref, sent_refs)
    for extra in extra_refs:
        size = extra.shape[0]
        far = other_ref[other_ref.shape[0] - size :, :].astype(jnp.float32)
        both = (extra[...].astype(jnp.float32) + pltpu.roll(far, size // 2, 0)).astype(extra.dtype)
        for sent in sent_refs:
            sent[own_ref.shape[0] :, :] = both


def add_cores(chips, offset, even_ref, other_ref, own_ref, sent_refs):
    rows = own_ref.shape[0]
    for k, out in enumerate((own_ref, *sent_refs)):
        other = other_ref[pl.ds(offset + k * rows, rows), :].astype(jnp.float32)
        out[0:rows, :] = (even_ref[pl.ds(k * rows, rows), :] + other).astype(out.dtype)


def merge_kernel(chips, even_ref, other_ref, own_ref, *sent_refs):
    add_cores(chips, 0, even_ref, other_ref, own_ref, sent_refs)


def place_kernel(chips, rows_here, block_rows, id_rows, mine_ref, other_ref, *refs):
    far_refs, place_ref = refs[:-1], refs[-1]
    my_col = lax.axis_index("col")
    half = rows_here // HALVES
    chunk_rows = block_rows // CHUNKS
    extra = mine_ref.shape[0]

    def places(rows):
        ids = (rows[:id_rows] * BYTE + rows[id_rows : 2 * id_rows]).astype(jnp.int32)
        rel = (ids // rows_here) ^ my_col
        chunk = (1 - rel % 2) * HALVES + ids % rows_here // half
        return chunk * chunk_rows + rel // 2 * half + ids % half

    def tail(ref):
        return ref[ref.shape[0] - extra :, :].astype(jnp.float32)

    even, odd = [mine_ref[...].astype(jnp.float32)], [tail(other_ref)]
    for ref in far_refs:
        rows = tail(ref)
        even.append(rows)
        odd.append(pltpu.roll(rows, extra - extra // 2, 0))
    for k in range(chips):
        place_ref[k * id_rows : (k + 1) * id_rows, :] = places(odd[k])
        place_ref[(chips + k) * id_rows : (chips + k + 1) * id_rows, :] = places(even[k])


def pick_rows(place_ref, part, total, picked, out):
    count = picked.shape[0]

    def some(i, carry):
        base = pl.multiple_of(i * UNPICK, UNPICK)
        row = (part * count + base) // LANES
        lane = base % LANES
        for j in range(UNPICK):
            picked[pl.ds(base + j, 1), :] = total[pl.ds(place_ref[row, lane + j], 1), :]
        return carry

    lax.fori_loop(0, count // UNPICK, some, 0)
    if out is not picked:
        out[...] = picked[...].astype(out.dtype)


def last_kernel(pieces, halves, plan_ref, place_ref, *refs):
    weights_ref = refs[pieces]
    odd_ref, total, state, picked = refs[pieces + 1 :]
    fill_state(refs[:pieces], state, halves, weights_ref.shape[1])
    multiply(plan_ref, weights_ref, state, total, 0, CHUNKS, 0)
    pick_rows(place_ref, 0, total, picked, odd_ref)


def pick_kernel(place_ref, total, even_ref):
    pick_rows(place_ref, 1, total, even_ref, even_ref)


def local(
    embed, degree, tile_row, tile_col, tile_count, tile_values, new_rows, new_bucket, bucket_norm
):
    rows_here, width = embed.shape
    ncols, nrows = lax.axis_size("col"), lax.axis_size("row")
    weights = tile_values[0, 0]
    slots, tile = weights.shape[:2]
    chips = ncols // 2
    block_rows = ncols * rows_here
    row_tiles = block_rows // tile
    per_group = rows_here // tile
    half_here = rows_here // HALVES
    chunk_rows = block_rows // CHUNKS
    zero_tile = nrows * per_group
    new_here = new_rows.shape[0]
    id_rows = new_here // LANES
    id_block = -(-4 * id_rows // PACK) * PACK
    length = -(-(slots + GROUP * (row_tiles + CHUNKS * UNROLL)) // LANES) * LANES
    f32, bf16 = jnp.float32, jnp.bfloat16
    array = jax.ShapeDtypeStruct
    in_hbm = lambda x: pltpu.with_memory_space_constraint(x, pltpu.HBM)
    in_vmem = lambda x: pltpu.with_memory_space_constraint(x, pltpu.VMEM)

    def call(kernel, name, out_shape, args, scalars=0, in_specs=None, scratch=(), turns=0.0):
        many = isinstance(out_shape, (list, tuple))
        cost = pl.CostEstimate(
            flops=int(turns * 2 * slots * tile * tile * width),
            bytes_accessed=int(turns * 2 * slots * tile * tile),
            transcendentals=0,
        )
        return pl.pallas_call(
            kernel,
            out_shape=out_shape,
            grid_spec=pltpu.PrefetchScalarGridSpec(
                num_scalar_prefetch=scalars,
                grid=(),
                in_specs=in_specs or [VMEM_SPEC] * (len(args) - scalars),
                out_specs=[VMEM_SPEC] * len(out_shape) if many else VMEM_SPEC,
                scratch_shapes=list(scratch),
            ),
            compiler_params=PARAMS,
            cost_estimate=cost if turns else None,
            name=name,
        )(*args)

    def swap(array, axis, size, mask):
        return lax.ppermute(array, axis, [(i, i ^ mask) for i in range(size)])

    def swap_cores(odd):
        return swap(odd, "col", ncols, 1)

    def spread(state):
        return [state] + [swap(state, "row", nrows, k) for k in range(1, nrows)]

    scale = lax.rsqrt(degree.astype(f32))
    state = (scale[:, None] * embed.astype(f32)).astype(bf16)
    pieces = spread(state)

    plan, weights = call(
        functools.partial(plan_kernel, row_tiles, per_group, zero_tile),
        "plan",
        [array((8, length), jnp.int32), pltpu.VMEM(weights.shape, weights.dtype)],
        (tile_count, in_hbm(tile_row[0]), in_hbm(tile_col[0]), in_hbm(weights)),
        in_specs=[SMEM_SPEC, HBM_SPEC, HBM_SPEC, HBM_SPEC],
        scratch=[
            pltpu.VMEM((1, slots), jnp.int32),
            pltpu.VMEM((1, slots), jnp.int32),
            pltpu.SemaphoreType.DMA((3,)),
        ],
    )
    weights = in_vmem(weights)

    inside = (new_rows - lax.axis_index("row") * block_rows).reshape(id_rows, LANES)
    mine = jnp.concatenate([inside // BYTE, inside % BYTE]).astype(bf16)
    mine = jnp.pad(mine, ((0, id_block - 2 * id_rows), (0, 0)))

    state_shape = ((zero_tile + 1) * tile, width)

    def sums_shape(rows, more=0):
        return [array((rows, width), f32)] + [array((rows + more, width), bf16)] * (chips - 1)

    def send(sent):
        return [swap(part, "col", ncols, 2 * k) for k, part in enumerate(sent, 1)]

    def merge(even, other):
        own, *sent = call(
            functools.partial(merge_kernel, chips), "merge", sums_shape(even.shape[0] // chips), (even, other)
        )
        return own, send(sent)

    def add(own, came):
        for part in came:
            own = own + part[: own.shape[0]].astype(f32)
        return own

    for hop in range(HOPS - 1):
        extra = (mine,) if hop == 0 else ()
        odd, held = call(
            functools.partial(odd_kernel, len(pieces), len(pieces) // nrows),
            "odd",
            [
                array((HALVES * chunk_rows + len(extra) * id_block, width), bf16),
                array(state_shape, bf16),
            ],
            (plan, *pieces, weights, *extra),
            scalars=1,
            scratch=[pltpu.VMEM((HALVES * chunk_rows, width), f32)],
            turns=0.5,
        )
        other = swap_cores(odd)
        even0 = call(
            even0_kernel, "even0", array((chunk_rows, width), f32), (plan, held, weights), scalars=1, turns=0.25
        )
        own0, came0 = merge(even0, other)
        own1, *sent1 = call(
            functools.partial(even1_kernel, chips),
            "even1",
            sums_shape(half_here, len(extra) * id_block),
            (plan, held, weights, own0, other, *extra),
            scalars=1,
            scratch=[pltpu.VMEM((chunk_rows, width), f32)],
            turns=0.25,
        )
        came1 = send(sent1)
        if hop == 0:
            place = call(
                functools.partial(place_kernel, chips, rows_here, block_rows, id_rows),
                "place",
                array((2 * chips * id_rows, LANES), jnp.int32),
                (mine, other, *came1),
            )
        parts = {}
        for half, (own, came) in reversed(tuple(enumerate(((own0, came0), (own1, came1))))):
            here = scale[half * half_here : (half + 1) * half_here]
            parts[half] = spread(((here * here)[:, None] * add(own, came)).astype(bf16))
        pieces = [parts[half][r] for half in reversed(range(HALVES)) for r in range(nrows)]

    odd, total = call(
        functools.partial(last_kernel, len(pieces), len(pieces) // nrows),
        "last",
        [array((chips * new_here, width), bf16), array((block_rows, width), f32)],
        (plan, place, *pieces, weights),
        scalars=2,
        scratch=[pltpu.VMEM(state_shape, bf16), pltpu.VMEM((chips * new_here, width), f32)],
        turns=1.0,
    )
    other = swap_cores(odd)
    even = call(pick_kernel, "pick", array((chips * new_here, width), f32), (place, total), scalars=1, turns=0.2)
    picked = add(*merge(even, other))
    buckets = jnp.arange(bucket_norm.shape[0], dtype=jnp.int32)
    target = jnp.sum(
        jnp.where(new_bucket[:, None] == buckets[None, :], bucket_norm[None, :], jnp.float32(0.0)),
        axis=1,
    )
    return (
        target[:, None]
        * picked
        * lax.rsqrt(jnp.sum(picked * picked, axis=1, keepdims=True) + 1e-06)
    )


def solution(mesh):
    in_specs = (
        P(("row", "col"), None),
        P(("row", "col")),
        P("row", "col", None),
        P("row", "col", None),
        P("row", "col"),
        P("row", "col", None, None, None),
        P(("row", "col")),
        P(("row", "col")),
        P(),
    )
    out_specs = P(("row", "col"), None)
    return jax.shard_map(local, mesh=mesh, in_specs=in_specs, out_specs=out_specs, check_vma=False)
```

```python
import functools

import jax
import jax.numpy as jnp
from jax import lax
from jax.experimental import pallas as pl
from jax.experimental.pallas import tpu as pltpu
from jax.sharding import PartitionSpec as P

HOPS = 3
CHUNKS = 2
GROUP = 4
UNROLL = 4
UNPICK = 16
BITS = 8
SHIFT = 1 << BITS
BYTE = 256
LANES = 128
PACK = 16
MIB = 1024 * 1024

VMEM_SPEC = pl.BlockSpec(memory_space=pltpu.VMEM)
SMEM_SPEC = pl.BlockSpec(memory_space=pltpu.SMEM)
HBM_SPEC = pl.BlockSpec(memory_space=pltpu.HBM)
PARAMS = pltpu.CompilerParams(vmem_limit_bytes=16 * MIB)


def iota(shape, dim):
    return lax.broadcasted_iota(jnp.int32, shape, dim)


def to_column(row):
    n = row.shape[1]
    return jnp.sum(jnp.where(iota((n, n), 0) == iota((n, n), 1), row, 0.0), axis=1, keepdims=True)


def to_row(column):
    n = column.shape[0]
    return jnp.sum(jnp.where(iota((n, n), 0) == iota((n, n), 1), column, 0.0), axis=0, keepdims=True)


def plan_kernel(
    row_tiles, per_group, zero_tile, count_ref, tile_row_hbm, tile_col_hbm, weights_hbm,
    plan_ref, weights_ref, tile_row_ref, tile_col_ref, sems,
):
    load = pltpu.make_async_copy(weights_hbm, weights_ref, sems.at[0])
    lists = (
        pltpu.make_async_copy(tile_row_hbm, tile_row_ref, sems.at[1]),
        pltpu.make_async_copy(tile_col_hbm, tile_col_ref, sems.at[2]),
    )
    for copy in lists:
        copy.start()
    load.start()
    for copy in lists:
        copy.wait()
    slots = tile_row_ref.shape[1]
    length = plan_ref.shape[1]
    my_core = lax.axis_index("col") % 2
    chunk_tiles = row_tiles // CHUNKS
    row = tile_row_ref[...]
    group = row // per_group
    chunk = 1 - (group ^ my_core) % 2
    order = chunk * chunk_tiles + group // 2 * per_group + row % per_group
    order = jnp.where(iota((1, slots), 1) < count_ref[0, 0], order, row_tiles).astype(jnp.float32)
    entry = (iota((1, slots), 1) * SHIFT + tile_col_ref[...]).astype(jnp.float32)
    order_c = to_column(order)
    entry_c = to_column(entry)
    same = jnp.where((order_c == order) & (iota((slots, slots), 1) < iota((slots, slots), 0)), 1.0, 0.0)
    within = jnp.sum(same, axis=1, keepdims=True)
    tiles_r = iota((row_tiles, slots), 0).astype(jnp.float32)
    held = jnp.sum(jnp.where(tiles_r == order, 1.0, 0.0), axis=1, keepdims=True).astype(jnp.int32)
    steps = (held + GROUP - 1) // GROUP
    steps_f = steps.astype(jnp.float32)
    square = (row_tiles, row_tiles)
    first = jnp.sum(jnp.where(iota(square, 1) < iota(square, 0), to_row(steps_f), 0.0), axis=1, keepdims=True)
    tile_no, step_no = iota((row_tiles, 1), 0), iota((1, length), 1)
    raw, begin, ends = jnp.int32(0), jnp.int32(0), []
    limit = jnp.full((1, length), row_tiles - 1, jnp.int32)
    shift = jnp.zeros((row_tiles, 1), jnp.int32)
    for c in range(CHUNKS):
        mine = (tile_no >= c * chunk_tiles) & (tile_no < (c + 1) * chunk_tiles)
        size = jnp.sum(jnp.where(mine, steps_f, 0.0)).astype(jnp.int32)
        shift = shift + jnp.where(mine, begin - raw, 0)
        end = begin + (size + UNROLL - 1) // UNROLL * UNROLL
        limit = jnp.where((step_no >= begin) & (step_no < end), (c + 1) * chunk_tiles - 1, limit)
        raw, begin = raw + size, end
        ends.append(end // UNROLL)
    first = first + shift.astype(jnp.float32)
    lanes = iota((slots, row_tiles), 1).astype(jnp.float32)
    start = jnp.sum(jnp.where(order_c == lanes, to_row(first), 0.0), axis=1, keepdims=True)
    place = jnp.where(order_c < row_tiles, GROUP * start + within, -1.0)
    hit = place == iota((slots, length), 1).astype(jnp.float32)
    listed = jnp.sum(jnp.where(hit, entry_c - zero_tile, 0.0), axis=0, keepdims=True) + zero_tile
    done = (first + steps_f) <= iota((row_tiles, length), 1).astype(jnp.float32)
    owner = jnp.sum(jnp.where(done, 1.0, 0.0), axis=0, keepdims=True).astype(jnp.int32)
    bounds = jnp.zeros((1, length), jnp.int32)
    for c, end in enumerate(ends):
        bounds = jnp.where(step_no == c + 1, end, bounds)
    plan_ref[0:1, :] = listed.astype(jnp.int32)
    plan_ref[1:2, :] = jnp.minimum(owner, limit)
    plan_ref[2:3, :] = bounds
    plan_ref[3:8, :] = jnp.zeros((5, length), jnp.int32)
    load.wait()


def multiply(plan_ref, weights_ref, state, total, chunk, chunks, chunk_tiles):
    tile = weights_ref.shape[1]
    total[...] = jnp.zeros_like(total)

    def turn(i, carry):
        prods = []
        for u in range(UNROLL):
            left, right = [], []
            for j in range(GROUP):
                entry = plan_ref[0, (i * UNROLL + u) * GROUP + j]
                left.append(weights_ref[entry >> BITS])
                right.append(state[pl.ds(pl.multiple_of((entry & (SHIFT - 1)) * tile, tile), tile), :])
            prods.append(
                jnp.dot(
                    jnp.concatenate(left, axis=1),
                    jnp.concatenate(right, axis=0),
                    preferred_element_type=jnp.float32,
                )
            )
        for u in range(UNROLL):
            row = plan_ref[1, i * UNROLL + u] - chunk * chunk_tiles
            at = pl.ds(pl.multiple_of(row * tile, tile), tile)
            total[at, :] += prods[u]
        return carry

    lax.fori_loop(plan_ref[2, chunk], plan_ref[2, chunk + chunks], turn, 0)


def fill_state(gathered_ref, state):
    rows = gathered_ref.shape[0]
    state[0:rows, :] = gathered_ref[...]
    state[rows:, :] = jnp.zeros((state.shape[0] - rows, state.shape[1]), state.dtype)


def odd_kernel(plan_ref, gathered_ref, weights_ref, *refs):
    extra_refs, (odd_ref, state, total) = refs[:-3], refs[-3:]
    rows = total.shape[0]
    fill_state(gathered_ref, state)
    multiply(plan_ref, weights_ref, state, total, 0, 1, 0)
    odd_ref[0:rows, :] = total[...].astype(odd_ref.dtype)
    for extra in extra_refs:
        odd_ref[rows:, :] = extra[...]


def even_kernel(plan_ref, state, weights_ref, even_ref):
    multiply(plan_ref, weights_ref, state, even_ref, 1, 1, even_ref.shape[0] // weights_ref.shape[1])


def merge_kernel(chips, even_ref, other_ref, *refs):
    extra_refs, sent_ref = refs[:-1], refs[-1]
    rows, block = even_ref.shape[0] // chips, sent_ref.shape[0] // chips
    for k in range(chips):
        part = even_ref[pl.ds(k * rows, rows), :] + other_ref[pl.ds(k * rows, rows), :].astype(jnp.float32)
        sent_ref[k * block : k * block + rows, :] = part.astype(sent_ref.dtype)
    for extra in extra_refs:
        size = extra.shape[0]
        far = other_ref[chips * rows :, :].astype(jnp.float32)
        both = (extra[...].astype(jnp.float32) + pltpu.roll(far, size // 2, 0)).astype(sent_ref.dtype)
        for k in range(chips):
            sent_ref[k * block + rows : (k + 1) * block, :] = both


def state_kernel(chips, came_ref, square_ref, state_ref):
    rows, block = square_ref.shape[0], came_ref.shape[0] // chips
    total = came_ref[0:rows, :].astype(jnp.float32)
    for k in range(1, chips):
        total = total + came_ref[k * block : k * block + rows, :].astype(jnp.float32)
    state = (square_ref[...] * total).astype(state_ref.dtype)
    for r in range(state_ref.shape[0] // rows):
        state_ref[r * rows : (r + 1) * rows, :] = state


def place_kernel(chips, rows_here, block_rows, id_rows, extra, came_ref, place_ref):
    my_core = lax.axis_index("col") % 2
    chunk_rows = block_rows // CHUNKS
    block = came_ref.shape[0] // chips

    def places(rows):
        ids = (rows[:id_rows] * BYTE + rows[id_rows : 2 * id_rows]).astype(jnp.int32)
        group = ids // rows_here
        return (1 - (group ^ my_core) % 2) * chunk_rows + group // 2 * rows_here + ids % rows_here

    for k in range(chips):
        rows = came_ref[(k + 1) * block - extra : (k + 1) * block, :].astype(jnp.float32)
        odd = pltpu.roll(rows, extra - extra // 2, 0)
        place_ref[k * id_rows : (k + 1) * id_rows, :] = places(odd)
        place_ref[(chips + k) * id_rows : (chips + k + 1) * id_rows, :] = places(rows)


def pick_rows(place_ref, part, total, picked, out):
    count = picked.shape[0]

    def some(i, carry):
        base = pl.multiple_of(i * UNPICK, UNPICK)
        row = (part * count + base) // LANES
        lane = base % LANES
        for j in range(UNPICK):
            picked[pl.ds(base + j, 1), :] = total[pl.ds(place_ref[row, lane + j], 1), :]
        return carry

    lax.fori_loop(0, count // UNPICK, some, 0)
    if out is not picked:
        out[...] = picked[...].astype(out.dtype)


def last_kernel(plan_ref, place_ref, gathered_ref, weights_ref, odd_ref, total, state, picked):
    fill_state(gathered_ref, state)
    multiply(plan_ref, weights_ref, state, total, 0, CHUNKS, 0)
    pick_rows(place_ref, 0, total, picked, odd_ref)


def pick_kernel(place_ref, total, even_ref):
    pick_rows(place_ref, 1, total, even_ref, even_ref)


def local(
    embed, degree, tile_row, tile_col, tile_count, tile_values, new_rows, new_bucket, bucket_norm
):
    rows_here, width = embed.shape
    ncols, nrows = lax.axis_size("col"), lax.axis_size("row")
    weights = tile_values[0, 0]
    slots, tile = weights.shape[:2]
    chips = ncols // 2
    block_rows = ncols * rows_here
    row_tiles = block_rows // tile
    per_group = rows_here // tile
    chunk_rows = block_rows // CHUNKS
    zero_tile = nrows * per_group
    new_here = new_rows.shape[0]
    id_rows = new_here // LANES
    id_block = -(-4 * id_rows // PACK) * PACK
    length = -(-(slots + GROUP * (row_tiles + CHUNKS * UNROLL)) // LANES) * LANES
    f32, bf16 = jnp.float32, jnp.bfloat16
    array = jax.ShapeDtypeStruct
    in_hbm = lambda x: pltpu.with_memory_space_constraint(x, pltpu.HBM)
    in_vmem = lambda x: pltpu.with_memory_space_constraint(x, pltpu.VMEM)

    def call(kernel, name, out_shape, args, scalars=0, in_specs=None, scratch=(), turns=0.0):
        many = isinstance(out_shape, (list, tuple))
        cost = pl.CostEstimate(
            flops=int(turns * 2 * slots * tile * tile * width),
            bytes_accessed=int(turns * 2 * slots * tile * tile),
            transcendentals=0,
        )
        return pl.pallas_call(
            kernel,
            out_shape=out_shape,
            grid_spec=pltpu.PrefetchScalarGridSpec(
                num_scalar_prefetch=scalars,
                grid=(),
                in_specs=in_specs or [VMEM_SPEC] * (len(args) - scalars),
                out_specs=[VMEM_SPEC] * len(out_shape) if many else VMEM_SPEC,
                scratch_shapes=list(scratch),
            ),
            compiler_params=PARAMS,
            cost_estimate=cost if turns else None,
            name=name,
        )(*args)

    def swap_cores(odd):
        return lax.ppermute(odd, "col", [(i, i ^ 1) for i in range(ncols)])

    def to_chips(blocks):
        cores = [[2 * z + core for z in range(chips)] for core in range(2)]
        return lax.all_to_all(blocks, "col", 0, 0, axis_index_groups=cores, tiled=True)

    def spread(copies):
        return lax.all_to_all(copies, "row", 0, 0, tiled=True)

    scale = lax.rsqrt(degree.astype(f32))
    state = (scale[:, None] * embed.astype(f32)).astype(bf16)
    gathered = spread(jnp.tile(state, (nrows, 1)))
    square = jnp.broadcast_to((scale * scale)[:, None], (rows_here, width))

    plan, weights = call(
        functools.partial(plan_kernel, row_tiles, per_group, zero_tile),
        "plan",
        [array((8, length), jnp.int32), pltpu.VMEM(weights.shape, weights.dtype)],
        (tile_count, in_hbm(tile_row[0]), in_hbm(tile_col[0]), in_hbm(weights)),
        in_specs=[SMEM_SPEC, HBM_SPEC, HBM_SPEC, HBM_SPEC],
        scratch=[
            pltpu.VMEM((1, slots), jnp.int32),
            pltpu.VMEM((1, slots), jnp.int32),
            pltpu.SemaphoreType.DMA((3,)),
        ],
    )
    weights = in_vmem(weights)

    inside = (new_rows - lax.axis_index("row") * block_rows).reshape(id_rows, LANES)
    mine = jnp.concatenate([inside // BYTE, inside % BYTE]).astype(bf16)
    mine = jnp.pad(mine, ((0, id_block - 2 * id_rows), (0, 0)))

    state_shape = ((zero_tile + 1) * tile, width)

    def collect(even, other, extra=()):
        more = sum(e.shape[0] for e in extra)
        sent = call(
            functools.partial(merge_kernel, chips),
            "merge",
            array((even.shape[0] + chips * more, width), bf16),
            (even, other, *extra),
        )
        return to_chips(sent)

    for hop in range(HOPS - 1):
        extra = (mine,) if hop == 0 else ()
        odd, held = call(
            odd_kernel,
            "odd",
            [array((chunk_rows + len(extra) * id_block, width), bf16), array(state_shape, bf16)],
            (plan, gathered, weights, *extra),
            scalars=1,
            scratch=[pltpu.VMEM((chunk_rows, width), f32)],
            turns=0.5,
        )
        other = swap_cores(odd)
        even = call(
            even_kernel, "even", array((chunk_rows, width), f32), (plan, held, weights), scalars=1, turns=0.5
        )
        came = collect(even, other, extra)
        if hop == 0:
            place = call(
                functools.partial(place_kernel, chips, rows_here, block_rows, id_rows, id_block),
                "place",
                array((2 * chips * id_rows, LANES), jnp.int32),
                (came,),
            )
        copies = call(
            functools.partial(state_kernel, chips),
            "state",
            array((nrows * rows_here, width), bf16),
            (came, square),
        )
        gathered = spread(copies)

    odd, total = call(
        last_kernel,
        "last",
        [array((chips * new_here, width), bf16), array((block_rows, width), f32)],
        (plan, place, gathered, weights),
        scalars=2,
        scratch=[pltpu.VMEM(state_shape, bf16), pltpu.VMEM((chips * new_here, width), f32)],
        turns=1.0,
    )
    other = swap_cores(odd)
    even = call(pick_kernel, "pick", array((chips * new_here, width), f32), (place, total), scalars=1, turns=0.2)
    picked = jnp.sum(collect(even, other).reshape(chips, new_here, width).astype(f32), axis=0)
    buckets = jnp.arange(bucket_norm.shape[0], dtype=jnp.int32)
    target = jnp.sum(
        jnp.where(new_bucket[:, None] == buckets[None, :], bucket_norm[None, :], jnp.float32(0.0)),
        axis=1,
    )
    return (
        target[:, None]
        * picked
        * lax.rsqrt(jnp.sum(picked * picked, axis=1, keepdims=True) + 1e-06)
    )


def solution(mesh):
    in_specs = (
        P(("row", "col"), None),
        P(("row", "col")),
        P("row", "col", None),
        P("row", "col", None),
        P("row", "col"),
        P("row", "col", None, None, None),
        P(("row", "col")),
        P(("row", "col")),
        P(),
    )
    out_specs = P(("row", "col"), None)
    return jax.shard_map(local, mesh=mesh, in_specs=in_specs, out_specs=out_specs, check_vma=False)
```

```python
import functools

import jax
import jax.numpy as jnp
from jax import lax
from jax.experimental import pallas as pl
from jax.experimental.pallas import tpu as pltpu
from jax.sharding import PartitionSpec as P

HOPS = 3
CHUNKS = 4
GROUP = 4
UNROLL = 4
UNPICK = 16
BITS = 8
SHIFT = 1 << BITS
BYTE = 256
LANES = 128
PACK = 16
MIB = 1024 * 1024

VMEM_SPEC = pl.BlockSpec(memory_space=pltpu.VMEM)
SMEM_SPEC = pl.BlockSpec(memory_space=pltpu.SMEM)
HBM_SPEC = pl.BlockSpec(memory_space=pltpu.HBM)
PARAMS = pltpu.CompilerParams(vmem_limit_bytes=16 * MIB)


def far_first(k, chips):
    return k ^ (chips // 2)


def iota(shape, dim):
    return lax.broadcasted_iota(jnp.int32, shape, dim)


def to_column(row):
    n = row.shape[1]
    return jnp.sum(jnp.where(iota((n, n), 0) == iota((n, n), 1), row, 0.0), axis=1, keepdims=True)


def to_row(column):
    n = column.shape[0]
    return jnp.sum(jnp.where(iota((n, n), 0) == iota((n, n), 1), column, 0.0), axis=0, keepdims=True)


def plan_kernel(
    row_tiles, per_group, zero_tile, count_ref, tile_row_hbm, tile_col_hbm, weights_hbm,
    plan_ref, weights_ref, tile_row_ref, tile_col_ref, sems,
):
    load = pltpu.make_async_copy(weights_hbm, weights_ref, sems.at[0])
    lists = (
        pltpu.make_async_copy(tile_row_hbm, tile_row_ref, sems.at[1]),
        pltpu.make_async_copy(tile_col_hbm, tile_col_ref, sems.at[2]),
    )
    for copy in lists:
        copy.start()
    load.start()
    for copy in lists:
        copy.wait()
    slots = tile_row_ref.shape[1]
    length = plan_ref.shape[1]
    my_row, my_col = lax.axis_index("row"), lax.axis_index("col")
    chunk_tiles = row_tiles // CHUNKS
    row = tile_row_ref[...]
    rel = (row // per_group) ^ my_col
    chips = 2 * chunk_tiles // per_group
    place = (1 - rel % 2) * chips + far_first(rel // 2, chips)
    order = place * per_group + row % per_group
    order = jnp.where(iota((1, slots), 1) < count_ref[0, 0], order, row_tiles).astype(jnp.float32)
    col = tile_col_ref[...]
    source = ((col // per_group) ^ my_row) * per_group + col % per_group
    entry = (iota((1, slots), 1) * SHIFT + source).astype(jnp.float32)
    order_c = to_column(order)
    entry_c = to_column(entry)
    same = jnp.where((order_c == order) & (iota((slots, slots), 1) < iota((slots, slots), 0)), 1.0, 0.0)
    within = jnp.sum(same, axis=1, keepdims=True)
    tiles_r = iota((row_tiles, slots), 0).astype(jnp.float32)
    held = jnp.sum(jnp.where(tiles_r == order, 1.0, 0.0), axis=1, keepdims=True).astype(jnp.int32)
    steps = (held + GROUP - 1) // GROUP
    steps_f = steps.astype(jnp.float32)
    square = (row_tiles, row_tiles)
    first = jnp.sum(jnp.where(iota(square, 1) < iota(square, 0), to_row(steps_f), 0.0), axis=1, keepdims=True)
    tile_no, step_no = iota((row_tiles, 1), 0), iota((1, length), 1)
    raw, begin, ends = jnp.int32(0), jnp.int32(0), []
    limit = jnp.full((1, length), row_tiles - 1, jnp.int32)
    shift = jnp.zeros((row_tiles, 1), jnp.int32)
    for c in range(CHUNKS):
        mine = (tile_no >= c * chunk_tiles) & (tile_no < (c + 1) * chunk_tiles)
        size = jnp.sum(jnp.where(mine, steps_f, 0.0)).astype(jnp.int32)
        shift = shift + jnp.where(mine, begin - raw, 0)
        end = begin + (size + UNROLL - 1) // UNROLL * UNROLL
        limit = jnp.where((step_no >= begin) & (step_no < end), (c + 1) * chunk_tiles - 1, limit)
        raw, begin = raw + size, end
        ends.append(end // UNROLL)
    first = first + shift.astype(jnp.float32)
    lanes = iota((slots, row_tiles), 1).astype(jnp.float32)
    start = jnp.sum(jnp.where(order_c == lanes, to_row(first), 0.0), axis=1, keepdims=True)
    place = jnp.where(order_c < row_tiles, GROUP * start + within, -1.0)
    hit = place == iota((slots, length), 1).astype(jnp.float32)
    listed = jnp.sum(jnp.where(hit, entry_c - zero_tile, 0.0), axis=0, keepdims=True) + zero_tile
    done = (first + steps_f) <= iota((row_tiles, length), 1).astype(jnp.float32)
    owner = jnp.sum(jnp.where(done, 1.0, 0.0), axis=0, keepdims=True).astype(jnp.int32)
    bounds = jnp.zeros((1, length), jnp.int32)
    for c, end in enumerate(ends):
        bounds = jnp.where(step_no == c + 1, end, bounds)
    plan_ref[0:1, :] = listed.astype(jnp.int32)
    plan_ref[1:2, :] = jnp.minimum(owner, limit)
    plan_ref[2:3, :] = bounds
    plan_ref[3:8, :] = jnp.zeros((5, length), jnp.int32)
    load.wait()


def begin_kernel(degree_hbm, embed_hbm, state_ref, square_ref, degree_ref, embed_ref, sems):
    copies = (
        pltpu.make_async_copy(degree_hbm, degree_ref, sems.at[0]),
        pltpu.make_async_copy(embed_hbm, embed_ref, sems.at[1]),
    )
    for copy in copies:
        copy.start()
    for copy in copies:
        copy.wait()
    lanes = degree_ref.shape[1]
    for i in range(degree_ref.shape[0]):
        scale = to_column(lax.rsqrt(degree_ref[i : i + 1, :].astype(jnp.float32)))
        at = slice(i * lanes, (i + 1) * lanes)
        state_ref[at, :] = (scale * embed_ref[at, :].astype(jnp.float32)).astype(state_ref.dtype)
        square_ref[at, :] = jnp.broadcast_to(scale * scale, (lanes, square_ref.shape[1]))


def fill_state(pieces, state):
    rows = pieces[0].shape[0]
    for i, piece in enumerate(pieces):
        state[i * rows : (i + 1) * rows, :] = piece[...]
    at = len(pieces) * rows
    state[at:, :] = jnp.zeros((state.shape[0] - at, state.shape[1]), state.dtype)


def multiply(plan_ref, weights_ref, state, total, chunk, chunks, chunk_tiles):
    tile = weights_ref.shape[1]
    total[...] = jnp.zeros_like(total)

    def turn(i, carry):
        prods = []
        for u in range(UNROLL):
            left, right = [], []
            for j in range(GROUP):
                entry = plan_ref[0, (i * UNROLL + u) * GROUP + j]
                left.append(weights_ref[entry >> BITS])
                right.append(state[pl.ds(pl.multiple_of((entry & (SHIFT - 1)) * tile, tile), tile), :])
            prods.append(
                jnp.dot(
                    jnp.concatenate(left, axis=1),
                    jnp.concatenate(right, axis=0),
                    preferred_element_type=jnp.float32,
                )
            )
        for u in range(UNROLL):
            row = plan_ref[1, i * UNROLL + u] - chunk * chunk_tiles
            at = pl.ds(pl.multiple_of(row * tile, tile), tile)
            total[at, :] += prods[u]
        return carry

    lax.fori_loop(plan_ref[2, chunk], plan_ref[2, chunk + chunks], turn, 0)


def odd_kernel(pieces, plan_ref, *refs):
    weights_ref, extra_refs = refs[pieces], refs[pieces + 1 : -3]
    odd_ref, state, total = refs[-3:]
    rows = total.shape[0]
    fill_state(refs[:pieces], state)
    multiply(plan_ref, weights_ref, state, total, 0, 2, 0)
    odd_ref[0:rows, :] = total[...].astype(odd_ref.dtype)
    for extra in extra_refs:
        odd_ref[rows:, :] = extra[...]


def add_cores(offset, even_ref, other_ref, extra_refs, out_refs):
    rows = even_ref.shape[0] // len(out_refs)
    for i, out in enumerate(out_refs):
        other = other_ref[offset + i * rows : offset + (i + 1) * rows, :].astype(jnp.float32)
        out[0:rows, :] = (even_ref[i * rows : (i + 1) * rows, :] + other).astype(out.dtype)
        for extra in extra_refs:
            if out.shape[0] > rows:
                size = extra.shape[0]
                tail = other_ref[other_ref.shape[0] - size :, :].astype(jnp.float32)
                both = extra[...].astype(jnp.float32) + pltpu.roll(tail, size // 2, 0)
                out[rows:, :] = both.astype(out.dtype)


def even_far_kernel(plan_ref, state, weights_ref, even_ref):
    multiply(plan_ref, weights_ref, state, even_ref, 2, 1, even_ref.shape[0] // weights_ref.shape[1])


def merge_kernel(outs, even_ref, other_ref, *refs):
    add_cores(0, even_ref, other_ref, refs[:-outs], refs[-outs:])


def even_near_kernel(outs, plan_ref, state, weights_ref, after_ref, other_ref, *refs):
    extra_refs, out_refs, total = refs[: -outs - 1], refs[-outs - 1 : -1], refs[-1]
    rows = total.shape[0]
    multiply(plan_ref, weights_ref, state, total, 3, 1, rows // weights_ref.shape[1])
    add_cores(rows, total, other_ref, extra_refs, out_refs)


def add_kernel(own_ref, *refs):
    out_ref = refs[-1]
    rows = out_ref.shape[0]
    total = own_ref[...]
    for ref in refs[:-1]:
        total = total + ref[0:rows, :].astype(jnp.float32)
    out_ref[...] = total


def place_kernel(chips, rows_here, block_rows, id_rows, mine_ref, other_ref, *refs):
    far_refs, place_ref = refs[:-1], refs[-1]
    my_col = lax.axis_index("col")
    extra = mine_ref.shape[0]

    def places(rows):
        ids = (rows[:id_rows] * BYTE + rows[id_rows : 2 * id_rows]).astype(jnp.int32)
        rel = (ids // rows_here) ^ my_col
        return ((1 - rel % 2) * chips + far_first(rel // 2, chips)) * rows_here + ids % rows_here

    def tail(ref):
        return ref[ref.shape[0] - extra :, :].astype(jnp.float32)

    even, odd = [mine_ref[...].astype(jnp.float32)], [tail(other_ref)]
    for ref in far_refs:
        rows = tail(ref)
        even.append(rows)
        odd.append(pltpu.roll(rows, extra - extra // 2, 0))
    for k in range(chips):
        at = far_first(k, chips) * id_rows
        place_ref[at : at + id_rows, :] = places(odd[k])
        at = at + chips * id_rows
        place_ref[at : at + id_rows, :] = places(even[k])


def pick_rows(place_ref, first, total, picked):
    def some(i, carry):
        base = pl.multiple_of(i * UNPICK, UNPICK)
        row = (first + base) // LANES
        lane = (first + base) % LANES
        rows = [total[pl.ds(place_ref[row, lane + j], 1), :] for j in range(UNPICK)]
        for j in range(UNPICK):
            picked[pl.ds(base + j, 1), :] = rows[j]
        return carry

    lax.fori_loop(0, picked.shape[0] // UNPICK, some, 0)


def last_kernel(pieces, plan_ref, place_ref, *refs):
    weights_ref = refs[pieces]
    odd_ref, total, state, picked = refs[pieces + 1 :]
    fill_state(refs[:pieces], state)
    multiply(plan_ref, weights_ref, state, total, 0, CHUNKS, 0)
    pick_rows(place_ref, 0, total, picked)
    odd_ref[...] = picked[...].astype(odd_ref.dtype)


def pick_far_kernel(place_ref, total, even_ref):
    pick_rows(place_ref, 2 * even_ref.shape[0], total, even_ref)


def pick_near_kernel(outs, place_ref, total, after_ref, other_ref, *refs):
    out_refs, picked = refs[:-1], refs[-1]
    rows = picked.shape[0]
    pick_rows(place_ref, 3 * rows, total, picked)
    add_cores(rows, picked, other_ref, (), out_refs)


def local(
    embed, degree, tile_row, tile_col, tile_count, tile_values, new_rows, new_bucket, bucket_norm
):
    rows_here, width = embed.shape
    ncols, nrows = lax.axis_size("col"), lax.axis_size("row")
    weights = tile_values[0, 0]
    slots, tile = weights.shape[:2]
    chips = ncols // 2
    block_rows = ncols * rows_here
    row_tiles = block_rows // tile
    per_group = rows_here // tile
    chunk_rows = block_rows // CHUNKS
    zero_tile = nrows * per_group
    new_here = new_rows.shape[0]
    id_rows = new_here // LANES
    id_block = -(-4 * id_rows // PACK) * PACK
    length = -(-(slots + GROUP * (row_tiles + CHUNKS * UNROLL)) // LANES) * LANES
    f32, bf16 = jnp.float32, jnp.bfloat16
    array = jax.ShapeDtypeStruct
    in_hbm = lambda x: pltpu.with_memory_space_constraint(x, pltpu.HBM)
    in_vmem = lambda x: pltpu.with_memory_space_constraint(x, pltpu.VMEM)

    def call(kernel, name, out_shape, args, scalars=0, in_specs=None, scratch=(), turns=0.0):
        many = isinstance(out_shape, (list, tuple))
        cost = pl.CostEstimate(
            flops=int(turns * 2 * slots * tile * tile * width),
            bytes_accessed=int(turns * 2 * slots * tile * tile),
            transcendentals=0,
        )
        return pl.pallas_call(
            kernel,
            out_shape=out_shape,
            grid_spec=pltpu.PrefetchScalarGridSpec(
                num_scalar_prefetch=scalars,
                grid=(),
                in_specs=in_specs or [VMEM_SPEC] * (len(args) - scalars),
                out_specs=[VMEM_SPEC] * len(out_shape) if many else VMEM_SPEC,
                scratch_shapes=list(scratch),
            ),
            compiler_params=PARAMS,
            cost_estimate=cost if turns else None,
            name=name,
        )(*args)

    def swap(array, axis, size, mask):
        return lax.ppermute(array, axis, [(i, i ^ mask) for i in range(size)])

    def swap_cores(odd):
        return swap(odd, "col", ncols, 1)

    def spread(state):
        return [state] + [swap(state, "row", nrows, k) for k in range(1, nrows)]

    state, square = call(
        begin_kernel,
        "begin",
        [array(embed.shape, bf16), array(embed.shape, f32)],
        (in_hbm(degree.reshape(rows_here // LANES, LANES)), in_hbm(embed)),
        in_specs=[HBM_SPEC, HBM_SPEC],
        scratch=[
            pltpu.VMEM((rows_here // LANES, LANES), jnp.int32),
            pltpu.VMEM(embed.shape, bf16),
            pltpu.SemaphoreType.DMA((2,)),
        ],
    )
    pieces = spread(state)

    plan, weights = call(
        functools.partial(plan_kernel, row_tiles, per_group, zero_tile),
        "plan",
        [array((8, length), jnp.int32), pltpu.VMEM(weights.shape, weights.dtype)],
        (tile_count, in_hbm(tile_row[0]), in_hbm(tile_col[0]), in_hbm(weights)),
        in_specs=[SMEM_SPEC, HBM_SPEC, HBM_SPEC, HBM_SPEC],
        scratch=[
            pltpu.VMEM((1, slots), jnp.int32),
            pltpu.VMEM((1, slots), jnp.int32),
            pltpu.SemaphoreType.DMA((3,)),
        ],
    )
    weights = in_vmem(weights)

    inside = (new_rows - lax.axis_index("row") * block_rows).reshape(id_rows, LANES)
    mine = jnp.concatenate([inside // BYTE, inside % BYTE]).astype(bf16)
    mine = jnp.pad(mine, ((0, id_block - 2 * id_rows), (0, 0)))

    state_shape = ((zero_tile + 1) * tile, width)

    half_chips = chips // 2

    def send(sent, first):
        return [swap(part, "col", ncols, 2 * (first + i)) for i, part in enumerate(sent)]

    def collect(other, far_part, near_kernel, near_args, near_scalars, rows, turns, extra=()):
        more = sum(e.shape[0] for e in extra)
        blocks = [array((rows + more, width), bf16)] * half_chips
        far = call(functools.partial(merge_kernel, half_chips), "merge", blocks, (far_part, other, *extra))
        own, *near = call(
            functools.partial(near_kernel, half_chips),
            "near",
            [array((rows, width), f32)] + blocks[1:],
            (*near_args, far[0], other, *extra),
            scalars=near_scalars,
            scratch=[pltpu.VMEM((half_chips * rows, width), f32)],
            turns=turns,
        )
        came_far, came_near = send(far, half_chips), send(near, 1)
        return call(add_kernel, "add", array((rows, width), f32), (own, *came_far)), came_near, came_far

    def add(total, came):
        for part in came:
            total = total + part[: total.shape[0]].astype(f32)
        return total

    for hop in range(HOPS - 1):
        extra = (mine,) if hop == 0 else ()
        odd, held = call(
            functools.partial(odd_kernel, nrows),
            "odd",
            [array((2 * chunk_rows + len(extra) * id_block, width), bf16), array(state_shape, bf16)],
            (plan, *pieces, weights, *extra),
            scalars=1,
            scratch=[pltpu.VMEM((2 * chunk_rows, width), f32)],
            turns=0.5,
        )
        other = swap_cores(odd)
        far_part = call(
            even_far_kernel, "far", array((chunk_rows, width), f32), (plan, held, weights), scalars=1, turns=0.25
        )
        total, near, far = collect(
            other, far_part, even_near_kernel, (plan, held, weights), 1, rows_here, 0.25, extra
        )
        if hop == 0:
            place = call(
                functools.partial(place_kernel, chips, rows_here, block_rows, id_rows),
                "place",
                array((2 * chips * id_rows, LANES), jnp.int32),
                (mine, other, *near, *far),
            )
        pieces = spread((square * add(total, near)).astype(bf16))

    odd, total = call(
        functools.partial(last_kernel, nrows),
        "last",
        [array((chips * new_here, width), bf16), array((block_rows, width), f32)],
        (plan, place, *pieces, weights),
        scalars=2,
        scratch=[pltpu.VMEM(state_shape, bf16), pltpu.VMEM((chips * new_here, width), f32)],
        turns=1.0,
    )
    other = swap_cores(odd)
    far_part = call(
        pick_far_kernel, "pick", array((half_chips * new_here, width), f32), (place, total), scalars=1, turns=0.25
    )
    summed, near, _ = collect(other, far_part, pick_near_kernel, (place, total), 1, new_here, 0.25)
    picked = add(summed, near)
    buckets = jnp.arange(bucket_norm.shape[0], dtype=jnp.int32)
    target = jnp.sum(
        jnp.where(new_bucket[:, None] == buckets[None, :], bucket_norm[None, :], jnp.float32(0.0)),
        axis=1,
    )
    return (
        target[:, None]
        * picked
        * lax.rsqrt(jnp.sum(picked * picked, axis=1, keepdims=True) + 1e-06)
    )


def solution(mesh):
    in_specs = (
        P(("row", "col"), None),
        P(("row", "col")),
        P("row", "col", None),
        P("row", "col", None),
        P("row", "col"),
        P("row", "col", None, None, None),
        P(("row", "col")),
        P(("row", "col")),
        P(),
    )
    out_specs = P(("row", "col"), None)
    return jax.shard_map(local, mesh=mesh, in_specs=in_specs, out_specs=out_specs, check_vma=False)
```

```python
import functools

import jax
import jax.numpy as jnp
from jax import lax
from jax.experimental import pallas as pl
from jax.experimental.pallas import tpu as pltpu
from jax.sharding import PartitionSpec as P

HOPS = 3
CHUNKS = 4
GROUP = 4
UNROLL = 4
UNPICK = 16
BITS = 8
SHIFT = 1 << BITS
BYTE = 256
LANES = 128
PACK = 16
MIB = 1024 * 1024

VMEM_SPEC = pl.BlockSpec(memory_space=pltpu.VMEM)
SMEM_SPEC = pl.BlockSpec(memory_space=pltpu.SMEM)
HBM_SPEC = pl.BlockSpec(memory_space=pltpu.HBM)
PARAMS = pltpu.CompilerParams(vmem_limit_bytes=16 * MIB)


def block_place(k, chips):
    place, last = 0, chips.bit_length() - 2
    for j in range(last + 1):
        place = place + (1 - (k >> j) % 2) * (1 << (last - j))
    return place


def iota(shape, dim):
    return lax.broadcasted_iota(jnp.int32, shape, dim)


def to_column(row):
    n = row.shape[1]
    return jnp.sum(jnp.where(iota((n, n), 0) == iota((n, n), 1), row, 0.0), axis=1, keepdims=True)


def to_row(column):
    n = column.shape[0]
    return jnp.sum(jnp.where(iota((n, n), 0) == iota((n, n), 1), column, 0.0), axis=0, keepdims=True)


def plan_kernel(
    row_tiles, per_group, zero_tile, count_ref, tile_row_hbm, tile_col_hbm, weights_hbm,
    plan_ref, weights_ref, tile_row_ref, tile_col_ref, sems,
):
    load = pltpu.make_async_copy(weights_hbm, weights_ref, sems.at[0])
    lists = (
        pltpu.make_async_copy(tile_row_hbm, tile_row_ref, sems.at[1]),
        pltpu.make_async_copy(tile_col_hbm, tile_col_ref, sems.at[2]),
    )
    for copy in lists:
        copy.start()
    load.start()
    for copy in lists:
        copy.wait()
    slots = tile_row_ref.shape[1]
    length = plan_ref.shape[1]
    my_row, my_col = lax.axis_index("row"), lax.axis_index("col")
    chunk_tiles = row_tiles // CHUNKS
    row = tile_row_ref[...]
    rel = (row // per_group) ^ my_col
    chips = 2 * chunk_tiles // per_group
    place = (1 - rel % 2) * chips + block_place(rel // 2, chips)
    order = place * per_group + row % per_group
    order = jnp.where(iota((1, slots), 1) < count_ref[0, 0], order, row_tiles).astype(jnp.float32)
    col = tile_col_ref[...]
    source = ((col // per_group) ^ my_row) * per_group + col % per_group
    entry = (iota((1, slots), 1) * SHIFT + source).astype(jnp.float32)
    order_c = to_column(order)
    entry_c = to_column(entry)
    same = jnp.where((order_c == order) & (iota((slots, slots), 1) < iota((slots, slots), 0)), 1.0, 0.0)
    within = jnp.sum(same, axis=1, keepdims=True)
    tiles_r = iota((row_tiles, slots), 0).astype(jnp.float32)
    held = jnp.sum(jnp.where(tiles_r == order, 1.0, 0.0), axis=1, keepdims=True).astype(jnp.int32)
    steps = (held + GROUP - 1) // GROUP
    steps_f = steps.astype(jnp.float32)
    square = (row_tiles, row_tiles)
    first = jnp.sum(jnp.where(iota(square, 1) < iota(square, 0), to_row(steps_f), 0.0), axis=1, keepdims=True)
    tile_no, step_no = iota((row_tiles, 1), 0), iota((1, length), 1)
    raw, begin, ends = jnp.int32(0), jnp.int32(0), []
    limit = jnp.full((1, length), row_tiles - 1, jnp.int32)
    shift = jnp.zeros((row_tiles, 1), jnp.int32)
    for c in range(CHUNKS):
        mine = (tile_no >= c * chunk_tiles) & (tile_no < (c + 1) * chunk_tiles)
        size = jnp.sum(jnp.where(mine, steps_f, 0.0)).astype(jnp.int32)
        shift = shift + jnp.where(mine, begin - raw, 0)
        end = begin + (size + UNROLL - 1) // UNROLL * UNROLL
        limit = jnp.where((step_no >= begin) & (step_no < end), (c + 1) * chunk_tiles - 1, limit)
        raw, begin = raw + size, end
        ends.append(end // UNROLL)
    first = first + shift.astype(jnp.float32)
    lanes = iota((slots, row_tiles), 1).astype(jnp.float32)
    start = jnp.sum(jnp.where(order_c == lanes, to_row(first), 0.0), axis=1, keepdims=True)
    place = jnp.where(order_c < row_tiles, GROUP * start + within, -1.0)
    hit = place == iota((slots, length), 1).astype(jnp.float32)
    listed = jnp.sum(jnp.where(hit, entry_c - zero_tile, 0.0), axis=0, keepdims=True) + zero_tile
    done = (first + steps_f) <= iota((row_tiles, length), 1).astype(jnp.float32)
    owner = jnp.sum(jnp.where(done, 1.0, 0.0), axis=0, keepdims=True).astype(jnp.int32)
    bounds = jnp.zeros((1, length), jnp.int32)
    for c, end in enumerate(ends):
        bounds = jnp.where(step_no == c + 1, end, bounds)
    plan_ref[0:1, :] = listed.astype(jnp.int32)
    plan_ref[1:2, :] = jnp.minimum(owner, limit)
    plan_ref[2:3, :] = bounds
    plan_ref[3:8, :] = jnp.zeros((5, length), jnp.int32)
    load.wait()


def begin_kernel(degree_hbm, embed_hbm, state_ref, square_ref, degree_ref, embed_ref, sems):
    copies = (
        pltpu.make_async_copy(degree_hbm, degree_ref, sems.at[0]),
        pltpu.make_async_copy(embed_hbm, embed_ref, sems.at[1]),
    )
    for copy in copies:
        copy.start()
    for copy in copies:
        copy.wait()
    lanes = degree_ref.shape[1]
    for i in range(degree_ref.shape[0]):
        scale = to_column(lax.rsqrt(degree_ref[i : i + 1, :].astype(jnp.float32)))
        at = slice(i * lanes, (i + 1) * lanes)
        state_ref[at, :] = (scale * embed_ref[at, :].astype(jnp.float32)).astype(state_ref.dtype)
        square_ref[at, :] = jnp.broadcast_to(scale * scale, (lanes, square_ref.shape[1]))


def fill_state(pieces, state):
    rows = pieces[0].shape[0]
    for i, piece in enumerate(pieces):
        state[i * rows : (i + 1) * rows, :] = piece[...]
    at = len(pieces) * rows
    state[at:, :] = jnp.zeros((state.shape[0] - at, state.shape[1]), state.dtype)


def multiply(plan_ref, weights_ref, state, total, chunk, chunks, chunk_tiles):
    tile = weights_ref.shape[1]
    total[...] = jnp.zeros_like(total)

    def turn(i, carry):
        prods = []
        for u in range(UNROLL):
            left, right = [], []
            for j in range(GROUP):
                entry = plan_ref[0, (i * UNROLL + u) * GROUP + j]
                left.append(weights_ref[entry >> BITS])
                right.append(state[pl.ds(pl.multiple_of((entry & (SHIFT - 1)) * tile, tile), tile), :])
            prods.append(
                jnp.dot(
                    jnp.concatenate(left, axis=1),
                    jnp.concatenate(right, axis=0),
                    preferred_element_type=jnp.float32,
                )
            )
        for u in range(UNROLL):
            row = plan_ref[1, i * UNROLL + u] - chunk * chunk_tiles
            at = pl.ds(pl.multiple_of(row * tile, tile), tile)
            total[at, :] += prods[u]
        return carry

    lax.fori_loop(plan_ref[2, chunk], plan_ref[2, chunk + chunks], turn, 0)


def odd_kernel(pieces, plan_ref, *refs):
    weights_ref, extra_refs = refs[pieces], refs[pieces + 1 : -3]
    odd_ref, state, total = refs[-3:]
    rows = total.shape[0]
    fill_state(refs[:pieces], state)
    multiply(plan_ref, weights_ref, state, total, 0, 2, 0)
    odd_ref[0:rows, :] = total[...].astype(odd_ref.dtype)
    for extra in extra_refs:
        odd_ref[rows:, :] = extra[...]


def even_sent_kernel(plan_ref, state, weights_ref, even_ref):
    multiply(plan_ref, weights_ref, state, even_ref, 2, 1, even_ref.shape[0] // weights_ref.shape[1])


def merge_kernel(even_ref, other_ref, *refs):
    extra_refs, sent_ref = refs[:-1], refs[-1]
    rows = even_ref.shape[0]
    sent_ref[0:rows, :] = (even_ref[...] + other_ref[0:rows, :].astype(jnp.float32)).astype(sent_ref.dtype)
    for extra in extra_refs:
        size = extra.shape[0]
        tail = other_ref[2 * rows :, :].astype(jnp.float32)
        both = extra[...].astype(jnp.float32) + pltpu.roll(tail, size // 4, 0)
        sent_ref[rows:, :] = both.astype(sent_ref.dtype)


def even_kept_kernel(plan_ref, state, weights_ref, after_ref, other_ref, kept_ref):
    rows = kept_ref.shape[0]
    multiply(plan_ref, weights_ref, state, kept_ref, 3, 1, rows // weights_ref.shape[1])
    kept_ref[...] += other_ref[rows : 2 * rows, :].astype(jnp.float32)


def round_kernel(ids, kept_ref, before_ref, came_ref, sent_ref, left_ref):
    rows = left_ref.shape[0]
    sent_ref[0:rows, :] = (kept_ref[0:rows, :] + came_ref[0:rows, :].astype(jnp.float32)).astype(sent_ref.dtype)
    left_ref[...] = kept_ref[rows:, :] + came_ref[rows : 2 * rows, :].astype(jnp.float32)
    if ids:
        known = [r[2 * rows :, :].astype(jnp.float32)[:ids] for r in (before_ref, came_ref)]
        sent_ref[rows:, :] = jnp.concatenate(known).astype(sent_ref.dtype)


def place_kernel(chips, rows_here, id_rows, sent_ref, came_ref, place_ref):
    my_col = lax.axis_index("col")
    half = chips // 2
    step = 4 * id_rows
    rows = (sent_ref.shape[0] // rows_here) * rows_here

    for k in range(chips):
        ref = came_ref if k >= half else sent_ref
        tail = ref[rows:, :].astype(jnp.float32)[k % half * step : (k % half + 1) * step]
        for part in range(2):
            own = tail[(1 - part) * 2 * id_rows :]
            ids = (own[:id_rows] * BYTE + own[id_rows : 2 * id_rows]).astype(jnp.int32)
            rel = (ids // rows_here) ^ my_col
            place = (1 - rel % 2) * chips + block_place(rel // 2, chips)
            place = place * rows_here + ids % rows_here
            for r in range(id_rows):
                at = ((part * chips + block_place(k, chips)) * id_rows + r) * LANES
                place_ref[0:1, at : at + LANES] = place[r : r + 1, :]


def pick_rows(place_ref, first, total, picked):
    def some(i, carry):
        for j in range(UNPICK):
            at = i * UNPICK + j
            picked[pl.ds(at, 1), :] = total[pl.ds(place_ref[0, first + at], 1), :]
        return carry

    lax.fori_loop(0, picked.shape[0] // UNPICK, some, 0)


def last_kernel(pieces, plan_ref, place_ref, *refs):
    weights_ref = refs[pieces]
    odd_ref, total, state, picked = refs[pieces + 1 :]
    fill_state(refs[:pieces], state)
    multiply(plan_ref, weights_ref, state, total, 0, CHUNKS, 0)
    pick_rows(place_ref, 0, total, picked)
    odd_ref[...] = picked[...].astype(odd_ref.dtype)


def pick_sent_kernel(place_ref, total, even_ref):
    pick_rows(place_ref, 2 * even_ref.shape[0], total, even_ref)


def pick_kept_kernel(place_ref, total, after_ref, other_ref, kept_ref):
    rows = kept_ref.shape[0]
    pick_rows(place_ref, 3 * rows, total, kept_ref)
    kept_ref[...] += other_ref[rows : 2 * rows, :].astype(jnp.float32)


def local(
    embed, degree, tile_row, tile_col, tile_count, tile_values, new_rows, new_bucket, bucket_norm
):
    rows_here, width = embed.shape
    ncols, nrows = lax.axis_size("col"), lax.axis_size("row")
    weights = tile_values[0, 0]
    slots, tile = weights.shape[:2]
    chips = ncols // 2
    block_rows = ncols * rows_here
    row_tiles = block_rows // tile
    per_group = rows_here // tile
    chunk_rows = block_rows // CHUNKS
    zero_tile = nrows * per_group
    new_here = new_rows.shape[0]
    id_rows = new_here // LANES
    id_block = -(-4 * id_rows // PACK) * PACK
    length = -(-(slots + GROUP * (row_tiles + CHUNKS * UNROLL)) // LANES) * LANES
    f32, bf16 = jnp.float32, jnp.bfloat16
    array = jax.ShapeDtypeStruct
    in_hbm = lambda x: pltpu.with_memory_space_constraint(x, pltpu.HBM)
    in_vmem = lambda x: pltpu.with_memory_space_constraint(x, pltpu.VMEM)

    def call(kernel, name, out_shape, args, scalars=0, in_specs=None, scratch=(), turns=0.0):
        many = isinstance(out_shape, (list, tuple))
        cost = pl.CostEstimate(
            flops=int(turns * 2 * slots * tile * tile * width),
            bytes_accessed=int(turns * 2 * slots * tile * tile),
            transcendentals=0,
        )
        return pl.pallas_call(
            kernel,
            out_shape=out_shape,
            grid_spec=pltpu.PrefetchScalarGridSpec(
                num_scalar_prefetch=scalars,
                grid=(),
                in_specs=in_specs or [VMEM_SPEC] * (len(args) - scalars),
                out_specs=[VMEM_SPEC] * len(out_shape) if many else VMEM_SPEC,
                scratch_shapes=list(scratch),
            ),
            compiler_params=PARAMS,
            cost_estimate=cost if turns else None,
            name=name,
        )(*args)

    def swap(array, axis, size, mask):
        return lax.ppermute(array, axis, [(i, i ^ mask) for i in range(size)])

    def swap_cores(odd):
        return swap(odd, "col", ncols, 1)

    def spread(state):
        return [state] + [swap(state, "row", nrows, k) for k in range(1, nrows)]

    state, square = call(
        begin_kernel,
        "begin",
        [array(embed.shape, bf16), array(embed.shape, f32)],
        (in_hbm(degree.reshape(rows_here // LANES, LANES)), in_hbm(embed)),
        in_specs=[HBM_SPEC, HBM_SPEC],
        scratch=[
            pltpu.VMEM((rows_here // LANES, LANES), jnp.int32),
            pltpu.VMEM(embed.shape, bf16),
            pltpu.SemaphoreType.DMA((2,)),
        ],
    )
    pieces = spread(state)

    plan, weights = call(
        functools.partial(plan_kernel, row_tiles, per_group, zero_tile),
        "plan",
        [array((8, length), jnp.int32), pltpu.VMEM(weights.shape, weights.dtype)],
        (tile_count, in_hbm(tile_row[0]), in_hbm(tile_col[0]), in_hbm(weights)),
        in_specs=[SMEM_SPEC, HBM_SPEC, HBM_SPEC, HBM_SPEC],
        scratch=[
            pltpu.VMEM((1, slots), jnp.int32),
            pltpu.VMEM((1, slots), jnp.int32),
            pltpu.SemaphoreType.DMA((3,)),
        ],
    )
    weights = in_vmem(weights)

    inside = (new_rows - lax.axis_index("row") * block_rows).reshape(id_rows, LANES)
    mine = jnp.concatenate([inside // BYTE, inside % BYTE]).astype(bf16)
    mine = jnp.pad(mine, ((0, id_block - 2 * id_rows), (0, 0)))

    state_shape = ((zero_tile + 1) * tile, width)

    def collect(other, even, kept_kernel, kept_args, turns, extra=()):
        rows = even.shape[0]
        more = sum(e.shape[0] for e in extra)
        sent = call(merge_kernel, "merge", array((rows + more, width), bf16), (even, other, *extra))
        kept = call(
            kept_kernel, "kept", array((rows, width), f32), (*kept_args, sent, other), scalars=1, turns=turns
        )
        apart, ids = 1, 4 * id_rows if extra else 0
        while True:
            came = swap(sent, "col", ncols, 2 * apart)
            apart *= 2
            if apart == chips:
                return kept, sent, came
            rows //= 2
            sent, kept = call(
                functools.partial(round_kernel, ids),
                "round",
                [array((rows + 2 * ids, width), bf16), array((rows, width), f32)],
                (kept, sent, came),
            )
            ids *= 2

    for hop in range(HOPS - 1):
        extra = (mine,) if hop == 0 else ()
        odd, held = call(
            functools.partial(odd_kernel, nrows),
            "odd",
            [array((2 * chunk_rows + len(extra) * id_block, width), bf16), array(state_shape, bf16)],
            (plan, *pieces, weights, *extra),
            scalars=1,
            scratch=[pltpu.VMEM((2 * chunk_rows, width), f32)],
            turns=0.5,
        )
        other = swap_cores(odd)
        even = call(
            even_sent_kernel, "even", array((chunk_rows, width), f32), (plan, held, weights), scalars=1, turns=0.25
        )
        kept, sent, came = collect(other, even, even_kept_kernel, (plan, held, weights), 0.25, extra)
        if hop == 0:
            place = call(
                functools.partial(place_kernel, chips, rows_here, id_rows),
                "place",
                array((1, ncols * new_here), jnp.int32),
                (sent, came),
            )
        pieces = spread((square * (kept + came[:rows_here].astype(f32))).astype(bf16))

    odd, total = call(
        functools.partial(last_kernel, nrows),
        "last",
        [array((chips * new_here, width), bf16), array((block_rows, width), f32)],
        (plan, place, *pieces, weights),
        scalars=2,
        scratch=[pltpu.VMEM(state_shape, bf16), pltpu.VMEM((chips * new_here, width), f32)],
        turns=1.0,
    )
    other = swap_cores(odd)
    even = call(
        pick_sent_kernel, "pick", array((chips * new_here // 2, width), f32), (place, total), scalars=1, turns=0.25
    )
    kept, _, came = collect(other, even, pick_kept_kernel, (place, total), 0.25)
    picked = kept + came.astype(f32)
    buckets = jnp.arange(bucket_norm.shape[0], dtype=jnp.int32)
    target = jnp.sum(
        jnp.where(new_bucket[:, None] == buckets[None, :], bucket_norm[None, :], jnp.float32(0.0)),
        axis=1,
    )
    return (
        target[:, None]
        * picked
        * lax.rsqrt(jnp.sum(picked * picked, axis=1, keepdims=True) + 1e-06)
    )


def solution(mesh):
    in_specs = (
        P(("row", "col"), None),
        P(("row", "col")),
        P("row", "col", None),
        P("row", "col", None),
        P("row", "col"),
        P("row", "col", None, None, None),
        P(("row", "col")),
        P(("row", "col")),
        P(),
    )
    out_specs = P(("row", "col"), None)
    return jax.shard_map(local, mesh=mesh, in_specs=in_specs, out_specs=out_specs, check_vma=False)
```

```python
import functools

import jax
import jax.numpy as jnp
from jax import lax
from jax.experimental import pallas as pl
from jax.experimental.pallas import tpu as pltpu
from jax.sharding import PartitionSpec as P

HOPS = 3
HALVES = 2
CHUNKS = 2 * HALVES
GROUP = 4
UNROLL = 4
UNPICK = 16
BITS = 8
SHIFT = 1 << BITS
BYTE = 256
LANES = 128
PACK = 16
MIB = 1024 * 1024

VMEM_SPEC = pl.BlockSpec(memory_space=pltpu.VMEM)
SMEM_SPEC = pl.BlockSpec(memory_space=pltpu.SMEM)
HBM_SPEC = pl.BlockSpec(memory_space=pltpu.HBM)
PARAMS = pltpu.CompilerParams(vmem_limit_bytes=16 * MIB)


def iota(shape, dim):
    return lax.broadcasted_iota(jnp.int32, shape, dim)


def to_column(row):
    n = row.shape[1]
    return jnp.sum(jnp.where(iota((n, n), 0) == iota((n, n), 1), row, 0.0), axis=1, keepdims=True)


def to_row(column):
    n = column.shape[0]
    return jnp.sum(jnp.where(iota((n, n), 0) == iota((n, n), 1), column, 0.0), axis=0, keepdims=True)


def plan_kernel(
    row_tiles, per_group, zero_tile, count_ref, tile_row_hbm, tile_col_hbm, weights_hbm,
    plan_ref, weights_ref, tile_row_ref, tile_col_ref, sems,
):
    load = pltpu.make_async_copy(weights_hbm, weights_ref, sems.at[0])
    lists = (
        pltpu.make_async_copy(tile_row_hbm, tile_row_ref, sems.at[1]),
        pltpu.make_async_copy(tile_col_hbm, tile_col_ref, sems.at[2]),
    )
    for copy in lists:
        copy.start()
    load.start()
    for copy in lists:
        copy.wait()
    slots = tile_row_ref.shape[1]
    length = plan_ref.shape[1]
    my_row, my_col = lax.axis_index("row"), lax.axis_index("col")
    chunk_tiles = row_tiles // CHUNKS
    per_half = per_group // HALVES
    row = tile_row_ref[...]
    rel = (row // per_group) ^ my_col
    chunk = (1 - rel % 2) * HALVES + (row % per_group) // per_half
    order = chunk * chunk_tiles + (rel // 2) * per_half + row % per_half
    order = jnp.where(iota((1, slots), 1) < count_ref[0, 0], order, row_tiles).astype(jnp.float32)
    col = tile_col_ref[...]
    source = ((col // per_group) ^ my_row) * per_group + col % per_group
    entry = (iota((1, slots), 1) * SHIFT + source).astype(jnp.float32)
    order_c = to_column(order)
    entry_c = to_column(entry)
    same = jnp.where((order_c == order) & (iota((slots, slots), 1) < iota((slots, slots), 0)), 1.0, 0.0)
    within = jnp.sum(same, axis=1, keepdims=True)
    tiles_r = iota((row_tiles, slots), 0).astype(jnp.float32)
    held = jnp.sum(jnp.where(tiles_r == order, 1.0, 0.0), axis=1, keepdims=True).astype(jnp.int32)
    steps = (held + GROUP - 1) // GROUP
    steps_f = steps.astype(jnp.float32)
    square = (row_tiles, row_tiles)
    first = jnp.sum(jnp.where(iota(square, 1) < iota(square, 0), to_row(steps_f), 0.0), axis=1, keepdims=True)
    tile_no, step_no = iota((row_tiles, 1), 0), iota((1, length), 1)
    raw, begin, ends = jnp.int32(0), jnp.int32(0), []
    limit = jnp.full((1, length), row_tiles - 1, jnp.int32)
    shift = jnp.zeros((row_tiles, 1), jnp.int32)
    for c in range(CHUNKS):
        mine = (tile_no >= c * chunk_tiles) & (tile_no < (c + 1) * chunk_tiles)
        size = jnp.sum(jnp.where(mine, steps_f, 0.0)).astype(jnp.int32)
        shift = shift + jnp.where(mine, begin - raw, 0)
        end = begin + (size + UNROLL - 1) // UNROLL * UNROLL
        limit = jnp.where((step_no >= begin) & (step_no < end), (c + 1) * chunk_tiles - 1, limit)
        raw, begin = raw + size, end
        ends.append(end // UNROLL)
    first = first + shift.astype(jnp.float32)
    lanes = iota((slots, row_tiles), 1).astype(jnp.float32)
    start = jnp.sum(jnp.where(order_c == lanes, to_row(first), 0.0), axis=1, keepdims=True)
    place = jnp.where(order_c < row_tiles, GROUP * start + within, -1.0)
    hit = place == iota((slots, length), 1).astype(jnp.float32)
    listed = jnp.sum(jnp.where(hit, entry_c - zero_tile, 0.0), axis=0, keepdims=True) + zero_tile
    done = (first + steps_f) <= iota((row_tiles, length), 1).astype(jnp.float32)
    owner = jnp.sum(jnp.where(done, 1.0, 0.0), axis=0, keepdims=True).astype(jnp.int32)
    bounds = jnp.zeros((1, length), jnp.int32)
    for c, end in enumerate(ends):
        bounds = jnp.where(step_no == c + 1, end, bounds)
    plan_ref[0:1, :] = listed.astype(jnp.int32)
    plan_ref[1:2, :] = jnp.minimum(owner, limit)
    plan_ref[2:3, :] = bounds
    plan_ref[3:8, :] = jnp.zeros((5, length), jnp.int32)
    load.wait()


def begin_kernel(degree_hbm, embed_hbm, state_ref, *refs):
    square_refs, (degree_ref, embed_ref, sems) = refs[:HALVES], refs[HALVES:]
    half = embed_ref.shape[0] // HALVES
    copies = (
        pltpu.make_async_copy(degree_hbm, degree_ref, sems.at[0]),
        pltpu.make_async_copy(embed_hbm, embed_ref, sems.at[1]),
    )
    for copy in copies:
        copy.start()
    for copy in copies:
        copy.wait()
    lanes = degree_ref.shape[1]
    for i in range(degree_ref.shape[0]):
        scale = to_column(lax.rsqrt(degree_ref[i : i + 1, :].astype(jnp.float32)))
        at = slice(i * lanes, (i + 1) * lanes)
        state_ref[at, :] = (scale * embed_ref[at, :].astype(jnp.float32)).astype(state_ref.dtype)
        inside = i * lanes % half
        square = jnp.broadcast_to(scale * scale, (lanes, embed_ref.shape[1]))
        square_refs[i * lanes // half][inside : inside + lanes, :] = square


def fill_state(pieces, state, halves, tile):
    rows = pieces[0].shape[0]
    devices = (state.shape[0] - tile) // (rows * halves)
    for i, piece in enumerate(pieces):
        half, device = halves - 1 - i // devices, i % devices
        at = (device * halves + half) * rows
        state[at : at + rows, :] = piece[...]
    state[len(pieces) * rows :, :] = jnp.zeros((tile, state.shape[1]), state.dtype)


def multiply(plan_ref, weights_ref, state, total, chunk, chunks, chunk_tiles):
    tile = weights_ref.shape[1]
    total[...] = jnp.zeros_like(total)

    def turn(i, carry):
        prods = []
        for u in range(UNROLL):
            left, right = [], []
            for j in range(GROUP):
                entry = plan_ref[0, (i * UNROLL + u) * GROUP + j]
                left.append(weights_ref[entry >> BITS])
                right.append(state[pl.ds(pl.multiple_of((entry & (SHIFT - 1)) * tile, tile), tile), :])
            prods.append(
                jnp.dot(
                    jnp.concatenate(left, axis=1),
                    jnp.concatenate(right, axis=0),
                    preferred_element_type=jnp.float32,
                )
            )
        for u in range(UNROLL):
            row = plan_ref[1, i * UNROLL + u] - chunk * chunk_tiles
            at = pl.ds(pl.multiple_of(row * tile, tile), tile)
            total[at, :] += prods[u]
        return carry

    lax.fori_loop(plan_ref[2, chunk], plan_ref[2, chunk + chunks], turn, 0)


def odd_kernel(pieces, halves, plan_ref, *refs):
    weights_ref, extra_refs = refs[pieces], refs[pieces + 1 : -3]
    odd_ref, state, total = refs[-3:]
    rows = total.shape[0]
    fill_state(refs[:pieces], state, halves, weights_ref.shape[1])
    multiply(plan_ref, weights_ref, state, total, 0, HALVES, 0)
    odd_ref[0:rows, :] = total[...].astype(odd_ref.dtype)
    for extra in extra_refs:
        odd_ref[rows:, :] = extra[...]


def even0_kernel(plan_ref, state, weights_ref, even_ref):
    multiply(plan_ref, weights_ref, state, even_ref, HALVES, 1, even_ref.shape[0] // weights_ref.shape[1])


def even1_kernel(chips, plan_ref, state, weights_ref, after_ref, other_ref, *refs):
    extra_refs, own_ref, sent_refs, total = refs[: -chips - 1], refs[-chips - 1], refs[-chips:-1], refs[-1]
    rows = total.shape[0]
    multiply(plan_ref, weights_ref, state, total, HALVES + 1, 1, rows // weights_ref.shape[1])
    add_cores(chips, rows, total, other_ref, own_ref, sent_refs)
    for extra in extra_refs:
        size = extra.shape[0]
        far = other_ref[other_ref.shape[0] - size :, :].astype(jnp.float32)
        both = (extra[...].astype(jnp.float32) + pltpu.roll(far, size // 2, 0)).astype(extra.dtype)
        for sent in sent_refs:
            sent[own_ref.shape[0] :, :] = both


def add_cores(chips, offset, even_ref, other_ref, own_ref, sent_refs):
    rows = own_ref.shape[0]
    for k, out in enumerate((own_ref, *sent_refs)):
        other = other_ref[pl.ds(offset + k * rows, rows), :].astype(jnp.float32)
        out[0:rows, :] = (even_ref[pl.ds(k * rows, rows), :] + other).astype(out.dtype)


def merge_kernel(chips, even_ref, other_ref, own_ref, *sent_refs):
    add_cores(chips, 0, even_ref, other_ref, own_ref, sent_refs)


def state_kernel(parts, square_ref, own_ref, *refs):
    state_ref = refs[-1]
    total = own_ref[...]
    for ref in refs[:parts]:
        total = total + ref[0 : total.shape[0], :].astype(jnp.float32)
    state_ref[...] = (square_ref[...] * total).astype(state_ref.dtype)


def place_kernel(chips, rows_here, block_rows, id_rows, mine_ref, other_ref, *refs):
    far_refs, place_ref = refs[:-1], refs[-1]
    my_col = lax.axis_index("col")
    half = rows_here // HALVES
    chunk_rows = block_rows // CHUNKS
    extra = mine_ref.shape[0]

    def places(rows):
        ids = (rows[:id_rows] * BYTE + rows[id_rows : 2 * id_rows]).astype(jnp.int32)
        rel = (ids // rows_here) ^ my_col
        chunk = (1 - rel % 2) * HALVES + ids % rows_here // half
        return chunk * chunk_rows + rel // 2 * half + ids % half

    def tail(ref):
        return ref[ref.shape[0] - extra :, :].astype(jnp.float32)

    even, odd = [mine_ref[...].astype(jnp.float32)], [tail(other_ref)]
    for ref in far_refs:
        rows = tail(ref)
        even.append(rows)
        odd.append(pltpu.roll(rows, extra - extra // 2, 0))
    for k in range(chips):
        for part, rows in enumerate((places(odd[k]), places(even[k]))):
            for r in range(id_rows):
                at = ((part * chips + k) * id_rows + r) * LANES
                place_ref[0:1, at : at + LANES] = rows[r : r + 1, :]


def pick_rows(place_ref, first, total, picked):
    def some(i, carry):
        for j in range(UNPICK):
            at = i * UNPICK + j
            picked[pl.ds(at, 1), :] = total[pl.ds(place_ref[0, first + at], 1), :]
        return carry

    lax.fori_loop(0, picked.shape[0] // UNPICK, some, 0)


def last_kernel(pieces, halves, plan_ref, place_ref, *refs):
    weights_ref = refs[pieces]
    odd_ref, total, state, picked = refs[pieces + 1 :]
    fill_state(refs[:pieces], state, halves, weights_ref.shape[1])
    multiply(plan_ref, weights_ref, state, total, 0, CHUNKS, 0)
    pick_rows(place_ref, 0, total, picked)
    odd_ref[...] = picked[...].astype(odd_ref.dtype)


def pick_kernel(place_ref, total, even_ref):
    pick_rows(place_ref, even_ref.shape[0], total, even_ref)


def local(
    embed, degree, tile_row, tile_col, tile_count, tile_values, new_rows, new_bucket, bucket_norm
):
    rows_here, width = embed.shape
    ncols, nrows = lax.axis_size("col"), lax.axis_size("row")
    weights = tile_values[0, 0]
    slots, tile = weights.shape[:2]
    chips = ncols // 2
    block_rows = ncols * rows_here
    row_tiles = block_rows // tile
    per_group = rows_here // tile
    half_here = rows_here // HALVES
    chunk_rows = block_rows // CHUNKS
    zero_tile = nrows * per_group
    new_here = new_rows.shape[0]
    id_rows = new_here // LANES
    id_block = -(-4 * id_rows // PACK) * PACK
    length = -(-(slots + GROUP * (row_tiles + CHUNKS * UNROLL)) // LANES) * LANES
    f32, bf16 = jnp.float32, jnp.bfloat16
    array = jax.ShapeDtypeStruct
    in_hbm = lambda x: pltpu.with_memory_space_constraint(x, pltpu.HBM)
    in_vmem = lambda x: pltpu.with_memory_space_constraint(x, pltpu.VMEM)

    def call(kernel, name, out_shape, args, scalars=0, in_specs=None, scratch=(), turns=0.0):
        many = isinstance(out_shape, (list, tuple))
        cost = pl.CostEstimate(
            flops=int(turns * 2 * slots * tile * tile * width),
            bytes_accessed=int(turns * 2 * slots * tile * tile),
            transcendentals=0,
        )
        return pl.pallas_call(
            kernel,
            out_shape=out_shape,
            grid_spec=pltpu.PrefetchScalarGridSpec(
                num_scalar_prefetch=scalars,
                grid=(),
                in_specs=in_specs or [VMEM_SPEC] * (len(args) - scalars),
                out_specs=[VMEM_SPEC] * len(out_shape) if many else VMEM_SPEC,
                scratch_shapes=list(scratch),
            ),
            compiler_params=PARAMS,
            cost_estimate=cost if turns else None,
            name=name,
        )(*args)

    def swap(array, axis, size, mask):
        return lax.ppermute(array, axis, [(i, i ^ mask) for i in range(size)])

    def swap_cores(odd):
        return swap(odd, "col", ncols, 1)

    def spread(state):
        return [state] + [swap(state, "row", nrows, k) for k in range(1, nrows)]

    state, *squares = call(
        begin_kernel,
        "begin",
        [array(embed.shape, bf16)] + [array((half_here, width), f32)] * HALVES,
        (in_hbm(degree.reshape(rows_here // LANES, LANES)), in_hbm(embed)),
        in_specs=[HBM_SPEC, HBM_SPEC],
        scratch=[
            pltpu.VMEM((rows_here // LANES, LANES), jnp.int32),
            pltpu.VMEM(embed.shape, bf16),
            pltpu.SemaphoreType.DMA((2,)),
        ],
    )
    pieces = spread(state)

    plan, weights = call(
        functools.partial(plan_kernel, row_tiles, per_group, zero_tile),
        "plan",
        [array((8, length), jnp.int32), pltpu.VMEM(weights.shape, weights.dtype)],
        (tile_count, in_hbm(tile_row[0]), in_hbm(tile_col[0]), in_hbm(weights)),
        in_specs=[SMEM_SPEC, HBM_SPEC, HBM_SPEC, HBM_SPEC],
        scratch=[
            pltpu.VMEM((1, slots), jnp.int32),
            pltpu.VMEM((1, slots), jnp.int32),
            pltpu.SemaphoreType.DMA((3,)),
        ],
    )
    weights = in_vmem(weights)

    inside = (new_rows - lax.axis_index("row") * block_rows).reshape(id_rows, LANES)
    mine = jnp.concatenate([inside // BYTE, inside % BYTE]).astype(bf16)
    mine = jnp.pad(mine, ((0, id_block - 2 * id_rows), (0, 0)))

    state_shape = ((zero_tile + 1) * tile, width)

    def sums_shape(rows, more=0):
        return [array((rows, width), f32)] + [array((rows + more, width), bf16)] * (chips - 1)

    def send(sent):
        return [swap(part, "col", ncols, 2 * k) for k, part in enumerate(sent, 1)]

    def merge(even, other):
        own, *sent = call(
            functools.partial(merge_kernel, chips), "merge", sums_shape(even.shape[0] // chips), (even, other)
        )
        return own, send(sent)

    def add(own, came):
        for part in came:
            own = own + part[: own.shape[0]].astype(f32)
        return own

    for hop in range(HOPS - 1):
        extra = (mine,)
        odd, held = call(
            functools.partial(odd_kernel, len(pieces), len(pieces) // nrows),
            "odd",
            [
                array((HALVES * chunk_rows + len(extra) * id_block, width), bf16),
                array(state_shape, bf16),
            ],
            (plan, *pieces, weights, *extra),
            scalars=1,
            scratch=[pltpu.VMEM((HALVES * chunk_rows, width), f32)],
            turns=0.5,
        )
        other = swap_cores(odd)
        even0 = call(
            even0_kernel, "even0", array((chunk_rows, width), f32), (plan, held, weights), scalars=1, turns=0.25
        )
        own0, came0 = merge(even0, other)
        own1, *sent1 = call(
            functools.partial(even1_kernel, chips),
            "even1",
            sums_shape(half_here, len(extra) * id_block),
            (plan, held, weights, own0, other, *extra),
            scalars=1,
            scratch=[pltpu.VMEM((chunk_rows, width), f32)],
            turns=0.25,
        )
        came1 = send(sent1)
        if hop == 0:
            place = call(
                functools.partial(place_kernel, chips, rows_here, block_rows, id_rows),
                "place",
                array((1, ncols * new_here), jnp.int32),
                (mine, other, *came1),
            )
        parts, after = [], ()
        for square, own, came in zip(squares, (own0, own1), (came0, came1)):
            half_state = call(
                functools.partial(state_kernel, len(came)),
                "state",
                array(square.shape, bf16),
                (square, own, *came, *after),
            )
            parts.append(spread(half_state))
            after = (half_state,)
        pieces = [parts[half][r] for half in reversed(range(HALVES)) for r in range(nrows)]

    odd, total = call(
        functools.partial(last_kernel, len(pieces), len(pieces) // nrows),
        "last",
        [array((chips * new_here, width), bf16), array((block_rows, width), f32)],
        (plan, place, *pieces, weights),
        scalars=2,
        scratch=[pltpu.VMEM(state_shape, bf16), pltpu.VMEM((chips * new_here, width), f32)],
        turns=1.0,
    )
    other = swap_cores(odd)
    even = call(pick_kernel, "pick", array((chips * new_here, width), f32), (place, total), scalars=1, turns=0.2)
    picked = add(*merge(even, other))
    buckets = jnp.arange(bucket_norm.shape[0], dtype=jnp.int32)
    target = jnp.sum(
        jnp.where(new_bucket[:, None] == buckets[None, :], bucket_norm[None, :], jnp.float32(0.0)),
        axis=1,
    )
    return (
        target[:, None]
        * picked
        * lax.rsqrt(jnp.sum(picked * picked, axis=1, keepdims=True) + 1e-06)
    )


def solution(mesh):
    in_specs = (
        P(("row", "col"), None),
        P(("row", "col")),
        P("row", "col", None),
        P("row", "col", None),
        P("row", "col"),
        P("row", "col", None, None, None),
        P(("row", "col")),
        P(("row", "col")),
        P(),
    )
    out_specs = P(("row", "col"), None)
    return jax.shard_map(local, mesh=mesh, in_specs=in_specs, out_specs=out_specs, check_vma=False)
```

```python
import functools

import jax
import jax.numpy as jnp
from jax import lax
from jax.experimental import pallas as pl
from jax.experimental.pallas import tpu as pltpu
from jax.sharding import PartitionSpec as P

HOPS = 3
HALVES = 2
CHUNKS = 2 * HALVES
GROUP = 4
UNROLL = 8
UNPICK = 16
BITS = 8
SHIFT = 1 << BITS
BYTE = 256
LANES = 128
PACK = 16
MIB = 1024 * 1024

VMEM_SPEC = pl.BlockSpec(memory_space=pltpu.VMEM)
SMEM_SPEC = pl.BlockSpec(memory_space=pltpu.SMEM)
HBM_SPEC = pl.BlockSpec(memory_space=pltpu.HBM)
PARAMS = pltpu.CompilerParams(vmem_limit_bytes=16 * MIB)


def iota(shape, dim):
    return lax.broadcasted_iota(jnp.int32, shape, dim)


def to_column(row):
    n = row.shape[1]
    return jnp.sum(jnp.where(iota((n, n), 0) == iota((n, n), 1), row, 0.0), axis=1, keepdims=True)


def to_row(column):
    n = column.shape[0]
    return jnp.sum(jnp.where(iota((n, n), 0) == iota((n, n), 1), column, 0.0), axis=0, keepdims=True)


def plan_kernel(
    row_tiles, per_group, zero_tile, count_ref, tile_row_hbm, tile_col_hbm, weights_hbm,
    plan_ref, weights_ref, tile_row_ref, tile_col_ref, sems,
):
    load = pltpu.make_async_copy(weights_hbm, weights_ref, sems.at[0])
    lists = (
        pltpu.make_async_copy(tile_row_hbm, tile_row_ref, sems.at[1]),
        pltpu.make_async_copy(tile_col_hbm, tile_col_ref, sems.at[2]),
    )
    for copy in lists:
        copy.start()
    load.start()
    for copy in lists:
        copy.wait()
    slots = tile_row_ref.shape[1]
    length = plan_ref.shape[1]
    my_row, my_col = lax.axis_index("row"), lax.axis_index("col")
    chunk_tiles = row_tiles // CHUNKS
    per_half = per_group // HALVES
    row = tile_row_ref[...]
    rel = (row // per_group) ^ my_col
    chunk = (1 - rel % 2) * HALVES + (row % per_group) // per_half
    order = chunk * chunk_tiles + (rel // 2) * per_half + row % per_half
    order = jnp.where(iota((1, slots), 1) < count_ref[0, 0], order, row_tiles).astype(jnp.float32)
    col = tile_col_ref[...]
    source = ((col // per_group) ^ my_row) * per_group + col % per_group
    entry = (iota((1, slots), 1) * SHIFT + source).astype(jnp.float32)
    order_c = to_column(order)
    entry_c = to_column(entry)
    same = jnp.where((order_c == order) & (iota((slots, slots), 1) < iota((slots, slots), 0)), 1.0, 0.0)
    within = jnp.sum(same, axis=1, keepdims=True)
    tiles_r = iota((row_tiles, slots), 0).astype(jnp.float32)
    held = jnp.sum(jnp.where(tiles_r == order, 1.0, 0.0), axis=1, keepdims=True).astype(jnp.int32)
    steps = (held + GROUP - 1) // GROUP
    steps_f = steps.astype(jnp.float32)
    square = (row_tiles, row_tiles)
    first = jnp.sum(jnp.where(iota(square, 1) < iota(square, 0), to_row(steps_f), 0.0), axis=1, keepdims=True)
    tile_no, step_no = iota((row_tiles, 1), 0), iota((1, length), 1)
    raw, begin, ends = jnp.int32(0), jnp.int32(0), []
    limit = jnp.full((1, length), row_tiles - 1, jnp.int32)
    shift = jnp.zeros((row_tiles, 1), jnp.int32)
    for c in range(CHUNKS):
        mine = (tile_no >= c * chunk_tiles) & (tile_no < (c + 1) * chunk_tiles)
        size = jnp.sum(jnp.where(mine, steps_f, 0.0)).astype(jnp.int32)
        shift = shift + jnp.where(mine, begin - raw, 0)
        end = begin + size
        if c > 0:
            end = (end + UNROLL - 1) // UNROLL * UNROLL
        limit = jnp.where((step_no >= begin) & (step_no < end), (c + 1) * chunk_tiles - 1, limit)
        raw, begin = raw + size, end
        ends.append(end // UNROLL)
    first = first + shift.astype(jnp.float32)
    lanes = iota((slots, row_tiles), 1).astype(jnp.float32)
    start = jnp.sum(jnp.where(order_c == lanes, to_row(first), 0.0), axis=1, keepdims=True)
    place = jnp.where(order_c < row_tiles, GROUP * start + within, -1.0)
    hit = place == iota((slots, length), 1).astype(jnp.float32)
    listed = jnp.sum(jnp.where(hit, entry_c - zero_tile, 0.0), axis=0, keepdims=True) + zero_tile
    done = (first + steps_f) <= iota((row_tiles, length), 1).astype(jnp.float32)
    owner = jnp.sum(jnp.where(done, 1.0, 0.0), axis=0, keepdims=True).astype(jnp.int32)
    bounds = jnp.zeros((1, length), jnp.int32)
    for c, end in enumerate(ends):
        bounds = jnp.where(step_no == c + 1, end, bounds)
    plan_ref[0:1, :] = listed.astype(jnp.int32)
    plan_ref[1:2, :] = jnp.minimum(owner, limit)
    plan_ref[2:3, :] = bounds
    plan_ref[3:8, :] = jnp.zeros((5, length), jnp.int32)
    load.wait()


def begin_kernel(degree_hbm, embed_hbm, state_ref, *refs):
    square_refs, (degree_ref, embed_ref, sems) = refs[:HALVES], refs[HALVES:]
    half = embed_ref.shape[0] // HALVES
    copies = (
        pltpu.make_async_copy(degree_hbm, degree_ref, sems.at[0]),
        pltpu.make_async_copy(embed_hbm, embed_ref, sems.at[1]),
    )
    for copy in copies:
        copy.start()
    for copy in copies:
        copy.wait()
    lanes = degree_ref.shape[1]
    for i in range(degree_ref.shape[0]):
        scale = to_column(lax.rsqrt(degree_ref[i : i + 1, :].astype(jnp.float32)))
        at = slice(i * lanes, (i + 1) * lanes)
        state_ref[at, :] = (scale * embed_ref[at, :].astype(jnp.float32)).astype(state_ref.dtype)
        inside = i * lanes % half
        square = jnp.broadcast_to(scale * scale, (lanes, embed_ref.shape[1]))
        square_refs[i * lanes // half][inside : inside + lanes, :] = square


def fill_state(pieces, state, halves, tile):
    rows = pieces[0].shape[0]
    devices = (state.shape[0] - tile) // (rows * halves)
    for i, piece in enumerate(pieces):
        half, device = halves - 1 - i // devices, i % devices
        at = (device * halves + half) * rows
        state[at : at + rows, :] = piece[...]
    state[len(pieces) * rows :, :] = jnp.zeros((tile, state.shape[1]), state.dtype)


def multiply(plan_ref, weights_ref, state, total, chunk, chunks, chunk_tiles):
    tile = weights_ref.shape[1]
    total[...] = jnp.zeros_like(total)

    def turn(i, carry):
        prods = []
        for u in range(UNROLL):
            left, right = [], []
            for j in range(GROUP):
                entry = plan_ref[0, (i * UNROLL + u) * GROUP + j]
                left.append(weights_ref[entry >> BITS])
                right.append(state[pl.ds(pl.multiple_of((entry & (SHIFT - 1)) * tile, tile), tile), :])
            prods.append(
                jnp.dot(
                    jnp.concatenate(left, axis=1),
                    jnp.concatenate(right, axis=0),
                    preferred_element_type=jnp.float32,
                )
            )
        for u in range(UNROLL):
            row = plan_ref[1, i * UNROLL + u] - chunk * chunk_tiles
            at = pl.ds(pl.multiple_of(row * tile, tile), tile)
            total[at, :] += prods[u]
        return carry

    lax.fori_loop(plan_ref[2, chunk], plan_ref[2, chunk + chunks], turn, 0)


def odd_kernel(pieces, halves, plan_ref, *refs):
    weights_ref, extra_refs = refs[pieces], refs[pieces + 1 : -3]
    odd_ref, state, total = refs[-3:]
    rows = total.shape[0]
    fill_state(refs[:pieces], state, halves, weights_ref.shape[1])
    multiply(plan_ref, weights_ref, state, total, 0, HALVES, 0)
    odd_ref[0:rows, :] = total[...].astype(odd_ref.dtype)
    for extra in extra_refs:
        odd_ref[rows:, :] = extra[...]


def even0_kernel(plan_ref, state, weights_ref, even_ref):
    multiply(plan_ref, weights_ref, state, even_ref, HALVES, 1, even_ref.shape[0] // weights_ref.shape[1])


def even1_kernel(chips, plan_ref, state, weights_ref, after_ref, other_ref, *refs):
    extra_refs, own_ref, sent_refs, total = refs[: -chips - 1], refs[-chips - 1], refs[-chips:-1], refs[-1]
    rows = total.shape[0]
    multiply(plan_ref, weights_ref, state, total, HALVES + 1, 1, rows // weights_ref.shape[1])
    add_cores(chips, rows, total, other_ref, own_ref, sent_refs)
    for extra in extra_refs:
        size = extra.shape[0]
        far = other_ref[other_ref.shape[0] - size :, :].astype(jnp.float32)
        both = (extra[...].astype(jnp.float32) + pltpu.roll(far, size // 2, 0)).astype(extra.dtype)
        for sent in sent_refs:
            sent[own_ref.shape[0] :, :] = both


def add_cores(chips, offset, even_ref, other_ref, own_ref, sent_refs):
    rows = own_ref.shape[0]
    for k, out in enumerate((own_ref, *sent_refs)):
        other = other_ref[pl.ds(offset + k * rows, rows), :].astype(jnp.float32)
        out[0:rows, :] = (even_ref[pl.ds(k * rows, rows), :] + other).astype(out.dtype)


def merge_kernel(chips, even_ref, other_ref, own_ref, *sent_refs):
    add_cores(chips, 0, even_ref, other_ref, own_ref, sent_refs)


def state_kernel(parts, square_ref, own_ref, *refs):
    state_ref = refs[-1]
    total = own_ref[...]
    for ref in refs[:parts]:
        total = total + ref[0 : total.shape[0], :].astype(jnp.float32)
    state_ref[...] = (square_ref[...] * total).astype(state_ref.dtype)


def place_kernel(chips, rows_here, block_rows, id_rows, mine_ref, other_ref, *refs):
    far_refs, place_ref = refs[:-1], refs[-1]
    my_col = lax.axis_index("col")
    half = rows_here // HALVES
    chunk_rows = block_rows // CHUNKS
    extra = mine_ref.shape[0]

    def places(rows):
        ids = (rows[:id_rows] * BYTE + rows[id_rows : 2 * id_rows]).astype(jnp.int32)
        rel = (ids // rows_here) ^ my_col
        chunk = (1 - rel % 2) * HALVES + ids % rows_here // half
        return chunk * chunk_rows + rel // 2 * half + ids % half

    def tail(ref):
        return ref[ref.shape[0] - extra :, :].astype(jnp.float32)

    even, odd = [mine_ref[...].astype(jnp.float32)], [tail(other_ref)]
    for ref in far_refs:
        rows = tail(ref)
        even.append(rows)
        odd.append(pltpu.roll(rows, extra - extra // 2, 0))
    for k in range(chips):
        for part, rows in enumerate((places(odd[k]), places(even[k]))):
            for r in range(id_rows):
                at = ((part * chips + k) * id_rows + r) * LANES
                place_ref[0:1, at : at + LANES] = rows[r : r + 1, :]


def pick_rows(place_ref, first, total, picked):
    def some(i, carry):
        for j in range(UNPICK):
            at = i * UNPICK + j
            picked[pl.ds(at, 1), :] = total[pl.ds(place_ref[0, first + at], 1), :]
        return carry

    lax.fori_loop(0, picked.shape[0] // UNPICK, some, 0)


def last_kernel(pieces, halves, plan_ref, place_ref, *refs):
    weights_ref = refs[pieces]
    odd_ref, total, state, picked = refs[pieces + 1 :]
    fill_state(refs[:pieces], state, halves, weights_ref.shape[1])
    multiply(plan_ref, weights_ref, state, total, 0, CHUNKS, 0)
    pick_rows(place_ref, 0, total, picked)
    odd_ref[...] = picked[...].astype(odd_ref.dtype)


def pick_kernel(place_ref, total, even_ref):
    pick_rows(place_ref, even_ref.shape[0], total, even_ref)


def local(
    embed, degree, tile_row, tile_col, tile_count, tile_values, new_rows, new_bucket, bucket_norm
):
    rows_here, width = embed.shape
    ncols, nrows = lax.axis_size("col"), lax.axis_size("row")
    weights = tile_values[0, 0]
    slots, tile = weights.shape[:2]
    chips = ncols // 2
    block_rows = ncols * rows_here
    row_tiles = block_rows // tile
    per_group = rows_here // tile
    half_here = rows_here // HALVES
    chunk_rows = block_rows // CHUNKS
    zero_tile = nrows * per_group
    new_here = new_rows.shape[0]
    id_rows = new_here // LANES
    id_block = -(-4 * id_rows // PACK) * PACK
    length = -(-(slots + GROUP * (row_tiles + CHUNKS * UNROLL)) // LANES) * LANES
    f32, bf16 = jnp.float32, jnp.bfloat16
    array = jax.ShapeDtypeStruct
    in_hbm = lambda x: pltpu.with_memory_space_constraint(x, pltpu.HBM)
    in_vmem = lambda x: pltpu.with_memory_space_constraint(x, pltpu.VMEM)

    def call(kernel, name, out_shape, args, scalars=0, in_specs=None, scratch=(), turns=0.0):
        many = isinstance(out_shape, (list, tuple))
        cost = pl.CostEstimate(
            flops=int(turns * 2 * slots * tile * tile * width),
            bytes_accessed=int(turns * 2 * slots * tile * tile),
            transcendentals=0,
        )
        return pl.pallas_call(
            kernel,
            out_shape=out_shape,
            grid_spec=pltpu.PrefetchScalarGridSpec(
                num_scalar_prefetch=scalars,
                grid=(),
                in_specs=in_specs or [VMEM_SPEC] * (len(args) - scalars),
                out_specs=[VMEM_SPEC] * len(out_shape) if many else VMEM_SPEC,
                scratch_shapes=list(scratch),
            ),
            compiler_params=PARAMS,
            cost_estimate=cost if turns else None,
            name=name,
        )(*args)

    def swap(array, axis, size, mask):
        return lax.ppermute(array, axis, [(i, i ^ mask) for i in range(size)])

    def swap_cores(odd):
        return swap(odd, "col", ncols, 1)

    def spread(state):
        return [state] + [swap(state, "row", nrows, k) for k in range(1, nrows)]

    state, *squares = call(
        begin_kernel,
        "begin",
        [array(embed.shape, bf16)] + [array((half_here, width), f32)] * HALVES,
        (in_hbm(degree.reshape(rows_here // LANES, LANES)), in_hbm(embed)),
        in_specs=[HBM_SPEC, HBM_SPEC],
        scratch=[
            pltpu.VMEM((rows_here // LANES, LANES), jnp.int32),
            pltpu.VMEM(embed.shape, bf16),
            pltpu.SemaphoreType.DMA((2,)),
        ],
    )
    pieces = spread(state)

    plan, weights = call(
        functools.partial(plan_kernel, row_tiles, per_group, zero_tile),
        "plan",
        [array((8, length), jnp.int32), pltpu.VMEM(weights.shape, weights.dtype)],
        (tile_count, in_hbm(tile_row[0]), in_hbm(tile_col[0]), in_hbm(weights)),
        in_specs=[SMEM_SPEC, HBM_SPEC, HBM_SPEC, HBM_SPEC],
        scratch=[
            pltpu.VMEM((1, slots), jnp.int32),
            pltpu.VMEM((1, slots), jnp.int32),
            pltpu.SemaphoreType.DMA((3,)),
        ],
    )
    weights = in_vmem(weights)

    inside = (new_rows - lax.axis_index("row") * block_rows).reshape(id_rows, LANES)
    mine = jnp.concatenate([inside // BYTE, inside % BYTE]).astype(bf16)
    mine = jnp.pad(mine, ((0, id_block - 2 * id_rows), (0, 0)))

    state_shape = ((zero_tile + 1) * tile, width)

    def sums_shape(rows, more=0):
        return [array((rows, width), f32)] + [array((rows + more, width), bf16)] * (chips - 1)

    def send(sent):
        return [swap(part, "col", ncols, 2 * k) for k, part in enumerate(sent, 1)]

    def merge(even, other):
        own, *sent = call(
            functools.partial(merge_kernel, chips), "merge", sums_shape(even.shape[0] // chips), (even, other)
        )
        return own, send(sent)

    def add(own, came):
        for part in came:
            own = own + part[: own.shape[0]].astype(f32)
        return own

    for hop in range(HOPS - 1):
        extra = (mine,)
        odd, held = call(
            functools.partial(odd_kernel, len(pieces), len(pieces) // nrows),
            "odd",
            [
                array((HALVES * chunk_rows + len(extra) * id_block, width), bf16),
                array(state_shape, bf16),
            ],
            (plan, *pieces, weights, *extra),
            scalars=1,
            scratch=[pltpu.VMEM((HALVES * chunk_rows, width), f32)],
            turns=0.5,
        )
        other = swap_cores(odd)
        even0 = call(
            even0_kernel, "even0", array((chunk_rows, width), f32), (plan, held, weights), scalars=1, turns=0.25
        )
        own0, came0 = merge(even0, other)
        own1, *sent1 = call(
            functools.partial(even1_kernel, chips),
            "even1",
            sums_shape(half_here, len(extra) * id_block),
            (plan, held, weights, own0, other, *extra),
            scalars=1,
            scratch=[pltpu.VMEM((chunk_rows, width), f32)],
            turns=0.25,
        )
        came1 = send(sent1)
        if hop == 0:
            place = call(
                functools.partial(place_kernel, chips, rows_here, block_rows, id_rows),
                "place",
                array((1, ncols * new_here), jnp.int32),
                (mine, other, *came1),
            )
        parts, after = [], ()
        for square, own, came in zip(squares, (own0, own1), (came0, came1)):
            half_state = call(
                functools.partial(state_kernel, len(came)),
                "state",
                array(square.shape, bf16),
                (square, own, *came, *after),
            )
            parts.append(spread(half_state))
            after = (half_state,)
        pieces = [parts[half][r] for half in reversed(range(HALVES)) for r in range(nrows)]

    odd, total = call(
        functools.partial(last_kernel, len(pieces), len(pieces) // nrows),
        "last",
        [array((chips * new_here, width), bf16), array((block_rows, width), f32)],
        (plan, place, *pieces, weights),
        scalars=2,
        scratch=[pltpu.VMEM(state_shape, bf16), pltpu.VMEM((chips * new_here, width), f32)],
        turns=1.0,
    )
    other = swap_cores(odd)
    even = call(pick_kernel, "pick", array((chips * new_here, width), f32), (place, total), scalars=1, turns=0.2)
    picked = add(*merge(even, other))
    buckets = jnp.arange(bucket_norm.shape[0], dtype=jnp.int32)
    target = jnp.sum(
        jnp.where(new_bucket[:, None] == buckets[None, :], bucket_norm[None, :], jnp.float32(0.0)),
        axis=1,
    )
    return (
        target[:, None]
        * picked
        * lax.rsqrt(jnp.sum(picked * picked, axis=1, keepdims=True) + 1e-06)
    )


def solution(mesh):
    in_specs = (
        P(("row", "col"), None),
        P(("row", "col")),
        P("row", "col", None),
        P("row", "col", None),
        P("row", "col"),
        P("row", "col", None, None, None),
        P(("row", "col")),
        P(("row", "col")),
        P(),
    )
    out_specs = P(("row", "col"), None)
    return jax.shard_map(local, mesh=mesh, in_specs=in_specs, out_specs=out_specs, check_vma=False)
```

```python
import functools

import jax
import jax.numpy as jnp
from jax import lax
from jax.experimental import pallas as pl
from jax.experimental.pallas import tpu as pltpu
from jax.sharding import PartitionSpec as P

HOPS = 3
HALVES = 2
CHUNKS = 2 * HALVES
GROUP = 4
UNROLL = 8
UNPICK = 16
BITS = 8
SHIFT = 1 << BITS
BYTE = 256
LANES = 128
PACK = 16
MIB = 1024 * 1024

VMEM_SPEC = pl.BlockSpec(memory_space=pltpu.VMEM)
SMEM_SPEC = pl.BlockSpec(memory_space=pltpu.SMEM)
HBM_SPEC = pl.BlockSpec(memory_space=pltpu.HBM)
PARAMS = pltpu.CompilerParams(vmem_limit_bytes=16 * MIB)


def chip_slot(k, core, chips):
    return jnp.where(core == 0, k, (chips - k) % chips)


def row_slot(k, core, nrows):
    return jnp.where(core == 0, k, k // 2 + k % 2 * (nrows // 2))


def row_mask(slot, core, nrows):
    return slot if core == 0 else slot * 2 % nrows + slot * 2 // nrows


def iota(shape, dim):
    return lax.broadcasted_iota(jnp.int32, shape, dim)


def to_column(row):
    n = row.shape[1]
    return jnp.sum(jnp.where(iota((n, n), 0) == iota((n, n), 1), row, 0.0), axis=1, keepdims=True)


def to_row(column):
    n = column.shape[0]
    return jnp.sum(jnp.where(iota((n, n), 0) == iota((n, n), 1), column, 0.0), axis=0, keepdims=True)


def plan_kernel(
    row_tiles, per_group, nrows, count_ref, tile_row_hbm, tile_col_hbm, weights_hbm,
    plan_ref, weights_ref, tile_row_ref, tile_col_ref, sems,
):
    load = pltpu.make_async_copy(weights_hbm, weights_ref, sems.at[0])
    lists = (
        pltpu.make_async_copy(tile_row_hbm, tile_row_ref, sems.at[1]),
        pltpu.make_async_copy(tile_col_hbm, tile_col_ref, sems.at[2]),
    )
    for copy in lists:
        copy.start()
    load.start()
    for copy in lists:
        copy.wait()
    slots = tile_row_ref.shape[1]
    length = plan_ref.shape[1]
    my_row, my_col = lax.axis_index("row"), lax.axis_index("col")
    zero_tile = nrows * per_group
    chunk_tiles = row_tiles // CHUNKS
    per_half = per_group // HALVES
    row = tile_row_ref[...]
    rel = (row // per_group) ^ my_col
    chunk = (1 - rel % 2) * HALVES + (row % per_group) // per_half
    slot = chip_slot(rel // 2, (my_col + rel) % 2, chunk_tiles // per_half)
    order = chunk * chunk_tiles + slot * per_half + row % per_half
    order = jnp.where(iota((1, slots), 1) < count_ref[0, 0], order, row_tiles).astype(jnp.float32)
    col = tile_col_ref[...]
    source = row_slot((col // per_group) ^ my_row, my_col % 2, nrows) * per_group + col % per_group
    entry = (iota((1, slots), 1) * SHIFT + source).astype(jnp.float32)
    order_c = to_column(order)
    entry_c = to_column(entry)
    same = jnp.where((order_c == order) & (iota((slots, slots), 1) < iota((slots, slots), 0)), 1.0, 0.0)
    within = jnp.sum(same, axis=1, keepdims=True)
    tiles_r = iota((row_tiles, slots), 0).astype(jnp.float32)
    held = jnp.sum(jnp.where(tiles_r == order, 1.0, 0.0), axis=1, keepdims=True).astype(jnp.int32)
    steps = (held + GROUP - 1) // GROUP
    steps_f = steps.astype(jnp.float32)
    square = (row_tiles, row_tiles)
    first = jnp.sum(jnp.where(iota(square, 1) < iota(square, 0), to_row(steps_f), 0.0), axis=1, keepdims=True)
    tile_no, step_no = iota((row_tiles, 1), 0), iota((1, length), 1)
    raw, begin, ends = jnp.int32(0), jnp.int32(0), []
    limit = jnp.full((1, length), row_tiles - 1, jnp.int32)
    shift = jnp.zeros((row_tiles, 1), jnp.int32)
    for c in range(CHUNKS):
        mine = (tile_no >= c * chunk_tiles) & (tile_no < (c + 1) * chunk_tiles)
        size = jnp.sum(jnp.where(mine, steps_f, 0.0)).astype(jnp.int32)
        shift = shift + jnp.where(mine, begin - raw, 0)
        end = begin + size
        if c > 0:
            end = (end + UNROLL - 1) // UNROLL * UNROLL
        limit = jnp.where((step_no >= begin) & (step_no < end), (c + 1) * chunk_tiles - 1, limit)
        raw, begin = raw + size, end
        ends.append(end // UNROLL)
    first = first + shift.astype(jnp.float32)
    lanes = iota((slots, row_tiles), 1).astype(jnp.float32)
    start = jnp.sum(jnp.where(order_c == lanes, to_row(first), 0.0), axis=1, keepdims=True)
    place = jnp.where(order_c < row_tiles, GROUP * start + within, -1.0)
    hit = place == iota((slots, length), 1).astype(jnp.float32)
    listed = jnp.sum(jnp.where(hit, entry_c - zero_tile, 0.0), axis=0, keepdims=True) + zero_tile
    done = (first + steps_f) <= iota((row_tiles, length), 1).astype(jnp.float32)
    owner = jnp.sum(jnp.where(done, 1.0, 0.0), axis=0, keepdims=True).astype(jnp.int32)
    bounds = jnp.zeros((1, length), jnp.int32)
    for c, end in enumerate(ends):
        bounds = jnp.where(step_no == c + 1, end, bounds)
    plan_ref[0:1, :] = listed.astype(jnp.int32)
    plan_ref[1:2, :] = jnp.minimum(owner, limit)
    plan_ref[2:3, :] = bounds
    plan_ref[3:8, :] = jnp.zeros((5, length), jnp.int32)
    load.wait()


def begin_kernel(degree_hbm, embed_hbm, state_ref, *refs):
    square_refs, (degree_ref, embed_ref, sems) = refs[:HALVES], refs[HALVES:]
    half = embed_ref.shape[0] // HALVES
    copies = (
        pltpu.make_async_copy(degree_hbm, degree_ref, sems.at[0]),
        pltpu.make_async_copy(embed_hbm, embed_ref, sems.at[1]),
    )
    for copy in copies:
        copy.start()
    for copy in copies:
        copy.wait()
    lanes = degree_ref.shape[1]
    for i in range(degree_ref.shape[0]):
        scale = to_column(lax.rsqrt(degree_ref[i : i + 1, :].astype(jnp.float32)))
        at = slice(i * lanes, (i + 1) * lanes)
        state_ref[at, :] = (scale * embed_ref[at, :].astype(jnp.float32)).astype(state_ref.dtype)
        inside = i * lanes % half
        square = jnp.broadcast_to(scale * scale, (lanes, embed_ref.shape[1]))
        square_refs[i * lanes // half][inside : inside + lanes, :] = square


def fill_state(pieces, state, halves, tile):
    rows = pieces[0].shape[0]
    devices = (state.shape[0] - tile) // (rows * halves)
    for i, piece in enumerate(pieces):
        half, device = halves - 1 - i // devices, i % devices
        at = (device * halves + half) * rows
        state[at : at + rows, :] = piece[...]
    state[len(pieces) * rows :, :] = jnp.zeros((tile, state.shape[1]), state.dtype)


def multiply(plan_ref, weights_ref, state, total, chunk, chunks, chunk_tiles):
    tile = weights_ref.shape[1]
    total[...] = jnp.zeros_like(total)

    def turn(i, carry):
        prods = []
        for u in range(UNROLL):
            left, right = [], []
            for j in range(GROUP):
                entry = plan_ref[0, (i * UNROLL + u) * GROUP + j]
                left.append(weights_ref[entry >> BITS])
                right.append(state[pl.ds(pl.multiple_of((entry & (SHIFT - 1)) * tile, tile), tile), :])
            prods.append(
                jnp.dot(
                    jnp.concatenate(left, axis=1),
                    jnp.concatenate(right, axis=0),
                    preferred_element_type=jnp.float32,
                )
            )
        for u in range(UNROLL):
            row = plan_ref[1, i * UNROLL + u] - chunk * chunk_tiles
            at = pl.ds(pl.multiple_of(row * tile, tile), tile)
            total[at, :] += prods[u]
        return carry

    lax.fori_loop(plan_ref[2, chunk], plan_ref[2, chunk + chunks], turn, 0)


def odd_kernel(pieces, halves, plan_ref, *refs):
    weights_ref, extra_refs = refs[pieces], refs[pieces + 1 : -3]
    odd_ref, state, total = refs[-3:]
    rows = total.shape[0]
    fill_state(refs[:pieces], state, halves, weights_ref.shape[1])
    multiply(plan_ref, weights_ref, state, total, 0, HALVES, 0)
    odd_ref[0:rows, :] = total[...].astype(odd_ref.dtype)
    for extra in extra_refs:
        odd_ref[rows:, :] = extra[...]


def even0_kernel(plan_ref, state, weights_ref, even_ref):
    multiply(plan_ref, weights_ref, state, even_ref, HALVES, 1, even_ref.shape[0] // weights_ref.shape[1])


def even1_kernel(chips, plan_ref, state, weights_ref, after_ref, other_ref, *refs):
    extra_refs, own_ref, sent_refs, total = refs[: -chips - 1], refs[-chips - 1], refs[-chips:-1], refs[-1]
    rows = total.shape[0]
    multiply(plan_ref, weights_ref, state, total, HALVES + 1, 1, rows // weights_ref.shape[1])
    add_cores(chips, rows, total, other_ref, own_ref, sent_refs)
    for extra in extra_refs:
        size = extra.shape[0]
        far = other_ref[other_ref.shape[0] - size :, :].astype(jnp.float32)
        both = (extra[...].astype(jnp.float32) + pltpu.roll(far, size // 2, 0)).astype(extra.dtype)
        for sent in sent_refs:
            sent[own_ref.shape[0] :, :] = both


def add_cores(chips, offset, even_ref, other_ref, own_ref, sent_refs):
    rows = own_ref.shape[0]
    for k, out in enumerate((own_ref, *sent_refs)):
        other = other_ref[pl.ds(offset + k * rows, rows), :].astype(jnp.float32)
        out[0:rows, :] = (even_ref[pl.ds(k * rows, rows), :] + other).astype(out.dtype)


def merge_kernel(chips, even_ref, other_ref, own_ref, *sent_refs):
    add_cores(chips, 0, even_ref, other_ref, own_ref, sent_refs)


def state_kernel(parts, square_ref, own_ref, *refs):
    state_ref = refs[-1]
    total = own_ref[...]
    for ref in refs[:parts]:
        total = total + ref[0 : total.shape[0], :].astype(jnp.float32)
    state_ref[...] = (square_ref[...] * total).astype(state_ref.dtype)


def place_kernel(chips, rows_here, block_rows, id_rows, mine_ref, other_ref, *refs):
    far_refs, place_ref = refs[:-1], refs[-1]
    my_col = lax.axis_index("col")
    half = rows_here // HALVES
    chunk_rows = block_rows // CHUNKS
    extra = mine_ref.shape[0]

    def places(rows):
        ids = (rows[:id_rows] * BYTE + rows[id_rows : 2 * id_rows]).astype(jnp.int32)
        rel = (ids // rows_here) ^ my_col
        chunk = (1 - rel % 2) * HALVES + ids % rows_here // half
        slot = chip_slot(rel // 2, (my_col + rel) % 2, chips)
        return chunk * chunk_rows + slot * half + ids % half

    def tail(ref):
        return ref[ref.shape[0] - extra :, :].astype(jnp.float32)

    even, odd = [mine_ref[...].astype(jnp.float32)], [tail(other_ref)]
    for ref in far_refs:
        rows = tail(ref)
        even.append(rows)
        odd.append(pltpu.roll(rows, extra - extra // 2, 0))
    for k in range(chips):
        for place, rows in (((chips - k) % chips, places(odd[k])), (chips + k, places(even[k]))):
            for r in range(id_rows):
                at = (place * id_rows + r) * LANES
                place_ref[0:1, at : at + LANES] = rows[r : r + 1, :]


def pick_rows(place_ref, first, total, picked):
    def some(i, carry):
        for j in range(UNPICK):
            at = i * UNPICK + j
            picked[pl.ds(at, 1), :] = total[pl.ds(place_ref[0, first + at], 1), :]
        return carry

    lax.fori_loop(0, picked.shape[0] // UNPICK, some, 0)


def last_kernel(pieces, halves, plan_ref, place_ref, *refs):
    weights_ref = refs[pieces]
    odd_ref, total, state, picked = refs[pieces + 1 :]
    fill_state(refs[:pieces], state, halves, weights_ref.shape[1])
    multiply(plan_ref, weights_ref, state, total, 0, CHUNKS, 0)
    pick_rows(place_ref, 0, total, picked)
    odd_ref[...] = picked[...].astype(odd_ref.dtype)


def pick_kernel(place_ref, total, even_ref):
    pick_rows(place_ref, even_ref.shape[0], total, even_ref)


def local(
    embed, degree, tile_row, tile_col, tile_count, tile_values, new_rows, new_bucket, bucket_norm
):
    rows_here, width = embed.shape
    ncols, nrows = lax.axis_size("col"), lax.axis_size("row")
    weights = tile_values[0, 0]
    slots, tile = weights.shape[:2]
    chips = ncols // 2
    block_rows = ncols * rows_here
    row_tiles = block_rows // tile
    per_group = rows_here // tile
    half_here = rows_here // HALVES
    chunk_rows = block_rows // CHUNKS
    zero_tile = nrows * per_group
    new_here = new_rows.shape[0]
    id_rows = new_here // LANES
    id_block = -(-4 * id_rows // PACK) * PACK
    length = -(-(slots + GROUP * (row_tiles + CHUNKS * UNROLL)) // LANES) * LANES
    f32, bf16 = jnp.float32, jnp.bfloat16
    array = jax.ShapeDtypeStruct
    in_hbm = lambda x: pltpu.with_memory_space_constraint(x, pltpu.HBM)
    in_vmem = lambda x: pltpu.with_memory_space_constraint(x, pltpu.VMEM)

    def call(kernel, name, out_shape, args, scalars=0, in_specs=None, scratch=(), turns=0.0):
        many = isinstance(out_shape, (list, tuple))
        cost = pl.CostEstimate(
            flops=int(turns * 2 * slots * tile * tile * width),
            bytes_accessed=int(turns * 2 * slots * tile * tile),
            transcendentals=0,
        )
        return pl.pallas_call(
            kernel,
            out_shape=out_shape,
            grid_spec=pltpu.PrefetchScalarGridSpec(
                num_scalar_prefetch=scalars,
                grid=(),
                in_specs=in_specs or [VMEM_SPEC] * (len(args) - scalars),
                out_specs=[VMEM_SPEC] * len(out_shape) if many else VMEM_SPEC,
                scratch_shapes=list(scratch),
            ),
            compiler_params=PARAMS,
            cost_estimate=cost if turns else None,
            name=name,
        )(*args)

    def swap_cores(odd):
        return lax.ppermute(odd, "col", [(i, i ^ 1) for i in range(ncols)])

    def send(sent):
        came = []
        for slot, part in enumerate(sent, 1):
            masks = (2 * slot, 2 * (chips - slot))
            came.append(lax.ppermute(part, "col", [(i, i ^ masks[i % 2]) for i in range(ncols)]))
        return came

    def spread(state):
        pieces = [state]
        for slot in range(1, nrows):
            masks = [row_mask(slot, core, nrows) for core in range(2)]
            pairs = [
                (r * ncols + c, (r ^ masks[c % 2]) * ncols + c) for r in range(nrows) for c in range(ncols)
            ]
            pieces.append(lax.ppermute(state, ("row", "col"), pairs))
        return pieces

    state, *squares = call(
        begin_kernel,
        "begin",
        [array(embed.shape, bf16)] + [array((half_here, width), f32)] * HALVES,
        (in_hbm(degree.reshape(rows_here // LANES, LANES)), in_hbm(embed)),
        in_specs=[HBM_SPEC, HBM_SPEC],
        scratch=[
            pltpu.VMEM((rows_here // LANES, LANES), jnp.int32),
            pltpu.VMEM(embed.shape, bf16),
            pltpu.SemaphoreType.DMA((2,)),
        ],
    )
    pieces = spread(state)

    plan, weights = call(
        functools.partial(plan_kernel, row_tiles, per_group, nrows),
        "plan",
        [array((8, length), jnp.int32), pltpu.VMEM(weights.shape, weights.dtype)],
        (tile_count, in_hbm(tile_row[0]), in_hbm(tile_col[0]), in_hbm(weights)),
        in_specs=[SMEM_SPEC, HBM_SPEC, HBM_SPEC, HBM_SPEC],
        scratch=[
            pltpu.VMEM((1, slots), jnp.int32),
            pltpu.VMEM((1, slots), jnp.int32),
            pltpu.SemaphoreType.DMA((3,)),
        ],
    )
    weights = in_vmem(weights)

    inside = (new_rows - lax.axis_index("row") * block_rows).reshape(id_rows, LANES)
    mine = jnp.concatenate([inside // BYTE, inside % BYTE]).astype(bf16)
    mine = jnp.pad(mine, ((0, id_block - 2 * id_rows), (0, 0)))

    state_shape = ((zero_tile + 1) * tile, width)

    def sums_shape(rows, more=0):
        return [array((rows, width), f32)] + [array((rows + more, width), bf16)] * (chips - 1)

    def merge(even, other):
        own, *sent = call(
            functools.partial(merge_kernel, chips), "merge", sums_shape(even.shape[0] // chips), (even, other)
        )
        return own, send(sent)

    def add(own, came):
        for part in came:
            own = own + part[: own.shape[0]].astype(f32)
        return own

    for hop in range(HOPS - 1):
        extra = (mine,)
        odd, held = call(
            functools.partial(odd_kernel, len(pieces), len(pieces) // nrows),
            "odd",
            [
                array((HALVES * chunk_rows + len(extra) * id_block, width), bf16),
                array(state_shape, bf16),
            ],
            (plan, *pieces, weights, *extra),
            scalars=1,
            scratch=[pltpu.VMEM((HALVES * chunk_rows, width), f32)],
            turns=0.5,
        )
        other = swap_cores(odd)
        even0 = call(
            even0_kernel, "even0", array((chunk_rows, width), f32), (plan, held, weights), scalars=1, turns=0.25
        )
        own0, came0 = merge(even0, other)
        own1, *sent1 = call(
            functools.partial(even1_kernel, chips),
            "even1",
            sums_shape(half_here, len(extra) * id_block),
            (plan, held, weights, own0, other, *extra),
            scalars=1,
            scratch=[pltpu.VMEM((chunk_rows, width), f32)],
            turns=0.25,
        )
        came1 = send(sent1)
        if hop == 0:
            place = call(
                functools.partial(place_kernel, chips, rows_here, block_rows, id_rows),
                "place",
                array((1, ncols * new_here), jnp.int32),
                (mine, other, *came1),
            )
        parts, after = [], ()
        for square, own, came in zip(squares, (own0, own1), (came0, came1)):
            half_state = call(
                functools.partial(state_kernel, len(came)),
                "state",
                array(square.shape, bf16),
                (square, own, *came, *after),
            )
            parts.append(spread(half_state))
            after = (half_state,)
        pieces = [parts[half][r] for half in reversed(range(HALVES)) for r in range(nrows)]

    odd, total = call(
        functools.partial(last_kernel, len(pieces), len(pieces) // nrows),
        "last",
        [array((chips * new_here, width), bf16), array((block_rows, width), f32)],
        (plan, place, *pieces, weights),
        scalars=2,
        scratch=[pltpu.VMEM(state_shape, bf16), pltpu.VMEM((chips * new_here, width), f32)],
        turns=1.0,
    )
    other = swap_cores(odd)
    even = call(pick_kernel, "pick", array((chips * new_here, width), f32), (place, total), scalars=1, turns=0.2)
    picked = add(*merge(even, other))
    buckets = jnp.arange(bucket_norm.shape[0], dtype=jnp.int32)
    target = jnp.sum(
        jnp.where(new_bucket[:, None] == buckets[None, :], bucket_norm[None, :], jnp.float32(0.0)),
        axis=1,
    )
    return (
        target[:, None]
        * picked
        * lax.rsqrt(jnp.sum(picked * picked, axis=1, keepdims=True) + 1e-06)
    )


def solution(mesh):
    in_specs = (
        P(("row", "col"), None),
        P(("row", "col")),
        P("row", "col", None),
        P("row", "col", None),
        P("row", "col"),
        P("row", "col", None, None, None),
        P(("row", "col")),
        P(("row", "col")),
        P(),
    )
    out_specs = P(("row", "col"), None)
    return jax.shard_map(local, mesh=mesh, in_specs=in_specs, out_specs=out_specs, check_vma=False)
```

```python
import functools

import jax
import jax.numpy as jnp
from jax import lax
from jax.experimental import pallas as pl
from jax.experimental.pallas import tpu as pltpu
from jax.sharding import PartitionSpec as P

HOPS = 3
HALVES = 2
CHUNKS = 2 * HALVES
GROUP = 4
UNROLL = 8
UNPICK = 16
BITS = 8
SHIFT = 1 << BITS
BYTE = 256
LANES = 128
PACK = 16
MIB = 1024 * 1024

VMEM_SPEC = pl.BlockSpec(memory_space=pltpu.VMEM)
SMEM_SPEC = pl.BlockSpec(memory_space=pltpu.SMEM)
HBM_SPEC = pl.BlockSpec(memory_space=pltpu.HBM)
PARAMS = pltpu.CompilerParams(vmem_limit_bytes=16 * MIB)


def chip_slot(k, core, chips):
    return jnp.where(core == 0, k, (chips - k) % chips)


def row_slot(k, core, nrows):
    return jnp.where(core == 0, k, k // 2 + k % 2 * (nrows // 2))


def row_mask(slot, core, nrows):
    return slot if core == 0 else slot * 2 % nrows + slot * 2 // nrows


def iota(shape, dim):
    return lax.broadcasted_iota(jnp.int32, shape, dim)


def to_column(row):
    n = row.shape[1]
    return jnp.sum(jnp.where(iota((n, n), 0) == iota((n, n), 1), row, 0.0), axis=1, keepdims=True)


def to_row(column):
    n = column.shape[0]
    return jnp.sum(jnp.where(iota((n, n), 0) == iota((n, n), 1), column, 0.0), axis=0, keepdims=True)


def plan_kernel(
    row_tiles, per_group, nrows, count_ref, tile_row_hbm, tile_col_hbm, weights_hbm,
    plan_ref, weights_ref, tile_row_ref, tile_col_ref, sems,
):
    load = pltpu.make_async_copy(weights_hbm, weights_ref, sems.at[0])
    lists = (
        pltpu.make_async_copy(tile_row_hbm, tile_row_ref, sems.at[1]),
        pltpu.make_async_copy(tile_col_hbm, tile_col_ref, sems.at[2]),
    )
    for copy in lists:
        copy.start()
    load.start()
    for copy in lists:
        copy.wait()
    slots = tile_row_ref.shape[1]
    length = plan_ref.shape[1]
    my_row, my_col = lax.axis_index("row"), lax.axis_index("col")
    zero_tile = nrows * per_group
    chunk_tiles = row_tiles // CHUNKS
    per_half = per_group // HALVES
    row = tile_row_ref[...]
    rel = (row // per_group) ^ my_col
    chunk = (1 - rel % 2) * HALVES + (row % per_group) // per_half
    slot = chip_slot(rel // 2, (my_col + rel) % 2, chunk_tiles // per_half)
    order = chunk * chunk_tiles + slot * per_half + row % per_half
    order = jnp.where(iota((1, slots), 1) < count_ref[0, 0], order, row_tiles).astype(jnp.float32)
    col = tile_col_ref[...]
    source = row_slot((col // per_group) ^ my_row, my_col % 2, nrows) * per_group + col % per_group
    entry = (iota((1, slots), 1) * SHIFT + source).astype(jnp.float32)
    order_c = to_column(order)
    entry_c = to_column(entry)
    same = jnp.where((order_c == order) & (iota((slots, slots), 1) < iota((slots, slots), 0)), 1.0, 0.0)
    within = jnp.sum(same, axis=1, keepdims=True)
    tiles_r = iota((row_tiles, slots), 0).astype(jnp.float32)
    held = jnp.sum(jnp.where(tiles_r == order, 1.0, 0.0), axis=1, keepdims=True).astype(jnp.int32)
    steps = (held + GROUP - 1) // GROUP
    steps_f = steps.astype(jnp.float32)
    square = (row_tiles, row_tiles)
    first = jnp.sum(jnp.where(iota(square, 1) < iota(square, 0), to_row(steps_f), 0.0), axis=1, keepdims=True)
    tile_no, step_no = iota((row_tiles, 1), 0), iota((1, length), 1)
    raw, begin, ends = jnp.int32(0), jnp.int32(0), []
    limit = jnp.full((1, length), row_tiles - 1, jnp.int32)
    shift = jnp.zeros((row_tiles, 1), jnp.int32)
    for c in range(CHUNKS):
        mine = (tile_no >= c * chunk_tiles) & (tile_no < (c + 1) * chunk_tiles)
        size = jnp.sum(jnp.where(mine, steps_f, 0.0)).astype(jnp.int32)
        shift = shift + jnp.where(mine, begin - raw, 0)
        end = begin + size
        if c > 0:
            end = (end + UNROLL - 1) // UNROLL * UNROLL
        limit = jnp.where((step_no >= begin) & (step_no < end), (c + 1) * chunk_tiles - 1, limit)
        raw, begin = raw + size, end
        ends.append(end // UNROLL)
    first = first + shift.astype(jnp.float32)
    lanes = iota((slots, row_tiles), 1).astype(jnp.float32)
    start = jnp.sum(jnp.where(order_c == lanes, to_row(first), 0.0), axis=1, keepdims=True)
    place = jnp.where(order_c < row_tiles, GROUP * start + within, -1.0)
    hit = place == iota((slots, length), 1).astype(jnp.float32)
    listed = jnp.sum(jnp.where(hit, entry_c - zero_tile, 0.0), axis=0, keepdims=True) + zero_tile
    done = (first + steps_f) <= iota((row_tiles, length), 1).astype(jnp.float32)
    owner = jnp.sum(jnp.where(done, 1.0, 0.0), axis=0, keepdims=True).astype(jnp.int32)
    bounds = jnp.zeros((1, length), jnp.int32)
    for c, end in enumerate(ends):
        bounds = jnp.where(step_no == c + 1, end, bounds)
    plan_ref[0:1, :] = listed.astype(jnp.int32)
    plan_ref[1:2, :] = jnp.minimum(owner, limit)
    plan_ref[2:3, :] = bounds
    plan_ref[3:8, :] = jnp.zeros((5, length), jnp.int32)
    load.wait()


def begin_kernel(degree_hbm, embed_hbm, state_ref, *refs):
    square_refs, (degree_ref, embed_ref, sems) = refs[:HALVES], refs[HALVES:]
    half = embed_ref.shape[0] // HALVES
    copies = (
        pltpu.make_async_copy(degree_hbm, degree_ref, sems.at[0]),
        pltpu.make_async_copy(embed_hbm, embed_ref, sems.at[1]),
    )
    for copy in copies:
        copy.start()
    for copy in copies:
        copy.wait()
    lanes = degree_ref.shape[1]
    for i in range(degree_ref.shape[0]):
        scale = to_column(lax.rsqrt(degree_ref[i : i + 1, :].astype(jnp.float32)))
        at = slice(i * lanes, (i + 1) * lanes)
        state_ref[at, :] = (scale * embed_ref[at, :].astype(jnp.float32)).astype(state_ref.dtype)
        inside = i * lanes % half
        square = jnp.broadcast_to(scale * scale, (lanes, embed_ref.shape[1]))
        square_refs[i * lanes // half][inside : inside + lanes, :] = square


def fill_state(pieces, state, halves, tile):
    rows = pieces[0].shape[0]
    each = len(pieces) // halves
    for i in range(halves):
        slot = 0
        for piece in pieces[i * each : (i + 1) * each]:
            for j in range(piece.shape[0] // rows):
                at = (slot * halves + halves - 1 - i) * rows
                state[at : at + rows, :] = piece[j * rows : (j + 1) * rows, :]
                slot += 1
    filled = state.shape[0] - tile
    state[filled:, :] = jnp.zeros((tile, state.shape[1]), state.dtype)


def multiply(plan_ref, weights_ref, state, total, chunk, chunks, chunk_tiles):
    tile = weights_ref.shape[1]
    total[...] = jnp.zeros_like(total)

    def turn(i, carry):
        prods = []
        for u in range(UNROLL):
            left, right = [], []
            for j in range(GROUP):
                entry = plan_ref[0, (i * UNROLL + u) * GROUP + j]
                left.append(weights_ref[entry >> BITS])
                right.append(state[pl.ds(pl.multiple_of((entry & (SHIFT - 1)) * tile, tile), tile), :])
            prods.append(
                jnp.dot(
                    jnp.concatenate(left, axis=1),
                    jnp.concatenate(right, axis=0),
                    preferred_element_type=jnp.float32,
                )
            )
        for u in range(UNROLL):
            row = plan_ref[1, i * UNROLL + u] - chunk * chunk_tiles
            at = pl.ds(pl.multiple_of(row * tile, tile), tile)
            total[at, :] += prods[u]
        return carry

    lax.fori_loop(plan_ref[2, chunk], plan_ref[2, chunk + chunks], turn, 0)


def odd_kernel(pieces, halves, plan_ref, *refs):
    weights_ref, extra_refs = refs[pieces], refs[pieces + 1 : -3]
    odd_ref, state, total = refs[-3:]
    rows = total.shape[0]
    fill_state(refs[:pieces], state, halves, weights_ref.shape[1])
    multiply(plan_ref, weights_ref, state, total, 0, HALVES, 0)
    odd_ref[0:rows, :] = total[...].astype(odd_ref.dtype)
    for extra in extra_refs:
        odd_ref[rows:, :] = extra[...]


def even0_kernel(plan_ref, state, weights_ref, even_ref):
    multiply(plan_ref, weights_ref, state, even_ref, HALVES, 1, even_ref.shape[0] // weights_ref.shape[1])


def even1_kernel(chips, plan_ref, state, weights_ref, after_ref, other_ref, *refs):
    extra_refs, own_ref, sent_refs, total = refs[: -chips - 1], refs[-chips - 1], refs[-chips:-1], refs[-1]
    rows = total.shape[0]
    multiply(plan_ref, weights_ref, state, total, HALVES + 1, 1, rows // weights_ref.shape[1])
    add_cores(chips, rows, total, other_ref, own_ref, sent_refs)
    for extra in extra_refs:
        size = extra.shape[0]
        far = other_ref[other_ref.shape[0] - size :, :].astype(jnp.float32)
        both = (extra[...].astype(jnp.float32) + pltpu.roll(far, size // 2, 0)).astype(extra.dtype)
        for sent in sent_refs:
            sent[own_ref.shape[0] :, :] = both


def add_cores(chips, offset, even_ref, other_ref, own_ref, sent_refs):
    rows = own_ref.shape[0]
    for k, out in enumerate((own_ref, *sent_refs)):
        other = other_ref[pl.ds(offset + k * rows, rows), :].astype(jnp.float32)
        out[0:rows, :] = (even_ref[pl.ds(k * rows, rows), :] + other).astype(out.dtype)


def merge_kernel(chips, even_ref, other_ref, own_ref, *sent_refs):
    add_cores(chips, 0, even_ref, other_ref, own_ref, sent_refs)


def state_kernel(parts, square_ref, own_ref, *refs):
    state_ref = refs[-1]
    total = own_ref[...]
    for ref in refs[:parts]:
        total = total + ref[0 : total.shape[0], :].astype(jnp.float32)
    state_ref[...] = (square_ref[...] * total).astype(state_ref.dtype)


def place_kernel(chips, rows_here, block_rows, id_rows, mine_ref, other_ref, *refs):
    far_refs, place_ref = refs[:-1], refs[-1]
    my_col = lax.axis_index("col")
    half = rows_here // HALVES
    chunk_rows = block_rows // CHUNKS
    extra = mine_ref.shape[0]

    def places(rows):
        ids = (rows[:id_rows] * BYTE + rows[id_rows : 2 * id_rows]).astype(jnp.int32)
        rel = (ids // rows_here) ^ my_col
        chunk = (1 - rel % 2) * HALVES + ids % rows_here // half
        slot = chip_slot(rel // 2, (my_col + rel) % 2, chips)
        return chunk * chunk_rows + slot * half + ids % half

    def tail(ref):
        return ref[ref.shape[0] - extra :, :].astype(jnp.float32)

    even, odd = [mine_ref[...].astype(jnp.float32)], [tail(other_ref)]
    for ref in far_refs:
        rows = tail(ref)
        even.append(rows)
        odd.append(pltpu.roll(rows, extra - extra // 2, 0))
    for k in range(chips):
        for place, rows in (((chips - k) % chips, places(odd[k])), (chips + k, places(even[k]))):
            for r in range(id_rows):
                at = (place * id_rows + r) * LANES
                place_ref[0:1, at : at + LANES] = rows[r : r + 1, :]


def pick_rows(place_ref, first, total, picked):
    def some(i, carry):
        for j in range(UNPICK):
            at = i * UNPICK + j
            picked[pl.ds(at, 1), :] = total[pl.ds(place_ref[0, first + at], 1), :]
        return carry

    lax.fori_loop(0, picked.shape[0] // UNPICK, some, 0)


def last_kernel(pieces, halves, plan_ref, place_ref, *refs):
    weights_ref = refs[pieces]
    odd_ref, total, state, picked = refs[pieces + 1 :]
    fill_state(refs[:pieces], state, halves, weights_ref.shape[1])
    multiply(plan_ref, weights_ref, state, total, 0, CHUNKS, 0)
    pick_rows(place_ref, 0, total, picked)
    odd_ref[...] = picked[...].astype(odd_ref.dtype)


def pick_kernel(place_ref, total, even_ref):
    pick_rows(place_ref, even_ref.shape[0], total, even_ref)


def local(
    embed, degree, tile_row, tile_col, tile_count, tile_values, new_rows, new_bucket, bucket_norm
):
    rows_here, width = embed.shape
    ncols, nrows = lax.axis_size("col"), lax.axis_size("row")
    weights = tile_values[0, 0]
    slots, tile = weights.shape[:2]
    chips = ncols // 2
    block_rows = ncols * rows_here
    row_tiles = block_rows // tile
    per_group = rows_here // tile
    half_here = rows_here // HALVES
    chunk_rows = block_rows // CHUNKS
    zero_tile = nrows * per_group
    new_here = new_rows.shape[0]
    id_rows = new_here // LANES
    id_block = -(-4 * id_rows // PACK) * PACK
    length = -(-(slots + GROUP * (row_tiles + CHUNKS * UNROLL)) // LANES) * LANES
    f32, bf16 = jnp.float32, jnp.bfloat16
    array = jax.ShapeDtypeStruct
    in_hbm = lambda x: pltpu.with_memory_space_constraint(x, pltpu.HBM)
    in_vmem = lambda x: pltpu.with_memory_space_constraint(x, pltpu.VMEM)

    def call(kernel, name, out_shape, args, scalars=0, in_specs=None, scratch=(), turns=0.0):
        many = isinstance(out_shape, (list, tuple))
        cost = pl.CostEstimate(
            flops=int(turns * 2 * slots * tile * tile * width),
            bytes_accessed=int(turns * 2 * slots * tile * tile),
            transcendentals=0,
        )
        return pl.pallas_call(
            kernel,
            out_shape=out_shape,
            grid_spec=pltpu.PrefetchScalarGridSpec(
                num_scalar_prefetch=scalars,
                grid=(),
                in_specs=in_specs or [VMEM_SPEC] * (len(args) - scalars),
                out_specs=[VMEM_SPEC] * len(out_shape) if many else VMEM_SPEC,
                scratch_shapes=list(scratch),
            ),
            compiler_params=PARAMS,
            cost_estimate=cost if turns else None,
            name=name,
        )(*args)

    def swap_cores(odd):
        return lax.ppermute(odd, "col", [(i, i ^ 1) for i in range(ncols)])

    def send(sent):
        came = []
        for slot, part in enumerate(sent, 1):
            masks = (2 * slot, 2 * (chips - slot))
            came.append(lax.ppermute(part, "col", [(i, i ^ masks[i % 2]) for i in range(ncols)]))
        return came

    row_bits = nrows.bit_length() - 1

    def swap_rows(sent, slot):
        masks = [row_mask(slot, core, nrows) for core in range(2)]
        pairs = [(r * ncols + c, (r ^ masks[c % 2]) * ncols + c) for r in range(nrows) for c in range(ncols)]
        return lax.ppermute(sent, ("row", "col"), pairs)

    def spread(state):
        held = [state]
        while 1 << (len(held) - 1) < nrows:
            sent = jnp.concatenate(held) if len(held) > 1 else state
            held.append(swap_rows(sent, 1 << (len(held) - 1)))
        return held

    state, *squares = call(
        begin_kernel,
        "begin",
        [array(embed.shape, bf16)] + [array((half_here, width), f32)] * HALVES,
        (in_hbm(degree.reshape(rows_here // LANES, LANES)), in_hbm(embed)),
        in_specs=[HBM_SPEC, HBM_SPEC],
        scratch=[
            pltpu.VMEM((rows_here // LANES, LANES), jnp.int32),
            pltpu.VMEM(embed.shape, bf16),
            pltpu.SemaphoreType.DMA((2,)),
        ],
    )
    pieces = [state] + [swap_rows(state, slot) for slot in range(1, nrows)]

    plan, weights = call(
        functools.partial(plan_kernel, row_tiles, per_group, nrows),
        "plan",
        [array((8, length), jnp.int32), pltpu.VMEM(weights.shape, weights.dtype)],
        (tile_count, in_hbm(tile_row[0]), in_hbm(tile_col[0]), in_hbm(weights)),
        in_specs=[SMEM_SPEC, HBM_SPEC, HBM_SPEC, HBM_SPEC],
        scratch=[
            pltpu.VMEM((1, slots), jnp.int32),
            pltpu.VMEM((1, slots), jnp.int32),
            pltpu.SemaphoreType.DMA((3,)),
        ],
    )
    weights = in_vmem(weights)

    inside = (new_rows - lax.axis_index("row") * block_rows).reshape(id_rows, LANES)
    mine = jnp.concatenate([inside // BYTE, inside % BYTE]).astype(bf16)
    mine = jnp.pad(mine, ((0, id_block - 2 * id_rows), (0, 0)))

    state_shape = ((zero_tile + 1) * tile, width)

    def sums_shape(rows, more=0):
        return [array((rows, width), f32)] + [array((rows + more, width), bf16)] * (chips - 1)

    def merge(even, other):
        own, *sent = call(
            functools.partial(merge_kernel, chips), "merge", sums_shape(even.shape[0] // chips), (even, other)
        )
        return own, send(sent)

    def add(own, came):
        for part in came:
            own = own + part[: own.shape[0]].astype(f32)
        return own

    for hop in range(HOPS - 1):
        extra = (mine,)
        odd, held = call(
            functools.partial(odd_kernel, len(pieces), HALVES if hop else 1),
            "odd",
            [
                array((HALVES * chunk_rows + len(extra) * id_block, width), bf16),
                array(state_shape, bf16),
            ],
            (plan, *pieces, weights, *extra),
            scalars=1,
            scratch=[pltpu.VMEM((HALVES * chunk_rows, width), f32)],
            turns=0.5,
        )
        other = swap_cores(odd)
        even0 = call(
            even0_kernel, "even0", array((chunk_rows, width), f32), (plan, held, weights), scalars=1, turns=0.25
        )
        own0, came0 = merge(even0, other)
        own1, *sent1 = call(
            functools.partial(even1_kernel, chips),
            "even1",
            sums_shape(half_here, len(extra) * id_block),
            (plan, held, weights, own0, other, *extra),
            scalars=1,
            scratch=[pltpu.VMEM((chunk_rows, width), f32)],
            turns=0.25,
        )
        came1 = send(sent1)
        if hop == 0:
            place = call(
                functools.partial(place_kernel, chips, rows_here, block_rows, id_rows),
                "place",
                array((1, ncols * new_here), jnp.int32),
                (mine, other, *came1),
            )
        parts, after = [], ()
        for square, own, came in zip(squares, (own0, own1), (came0, came1)):
            half_state = call(
                functools.partial(state_kernel, len(came)),
                "state",
                array(square.shape, bf16),
                (square, own, *came, *after),
            )
            parts.append(spread(half_state))
            after = (half_state,)
        pieces = [piece for half in reversed(range(HALVES)) for piece in parts[half]]

    odd, total = call(
        functools.partial(last_kernel, len(pieces), HALVES),
        "last",
        [array((chips * new_here, width), bf16), array((block_rows, width), f32)],
        (plan, place, *pieces, weights),
        scalars=2,
        scratch=[pltpu.VMEM(state_shape, bf16), pltpu.VMEM((chips * new_here, width), f32)],
        turns=1.0,
    )
    other = swap_cores(odd)
    even = call(pick_kernel, "pick", array((chips * new_here, width), f32), (place, total), scalars=1, turns=0.2)
    picked = add(*merge(even, other))
    buckets = jnp.arange(bucket_norm.shape[0], dtype=jnp.int32)
    target = jnp.sum(
        jnp.where(new_bucket[:, None] == buckets[None, :], bucket_norm[None, :], jnp.float32(0.0)),
        axis=1,
    )
    return (
        target[:, None]
        * picked
        * lax.rsqrt(jnp.sum(picked * picked, axis=1, keepdims=True) + 1e-06)
    )


def solution(mesh):
    in_specs = (
        P(("row", "col"), None),
        P(("row", "col")),
        P("row", "col", None),
        P("row", "col", None),
        P("row", "col"),
        P("row", "col", None, None, None),
        P(("row", "col")),
        P(("row", "col")),
        P(),
    )
    out_specs = P(("row", "col"), None)
    return jax.shard_map(local, mesh=mesh, in_specs=in_specs, out_specs=out_specs, check_vma=False)
```

```python
import functools

import jax
import jax.numpy as jnp
from jax import lax
from jax.experimental import pallas as pl
from jax.experimental.pallas import tpu as pltpu
from jax.sharding import PartitionSpec as P

HOPS = 3
HALVES = 2
CHUNKS = 2 * HALVES
GROUP = 4
UNROLL = 8
UNPICK = 16
BITS = 8
SHIFT = 1 << BITS
BYTE = 256
LANES = 128
PACK = 16
MIB = 1024 * 1024

VMEM_SPEC = pl.BlockSpec(memory_space=pltpu.VMEM)
SMEM_SPEC = pl.BlockSpec(memory_space=pltpu.SMEM)
HBM_SPEC = pl.BlockSpec(memory_space=pltpu.HBM)
PARAMS = pltpu.CompilerParams(vmem_limit_bytes=16 * MIB)


def row_slot(k, core, nrows):
    return jnp.where(core == 0, k, k // 2 + k % 2 * (nrows // 2))


def row_mask(slot, core, nrows):
    return slot if core == 0 else slot * 2 % nrows + slot * 2 // nrows


def iota(shape, dim):
    return lax.broadcasted_iota(jnp.int32, shape, dim)


def to_column(row):
    n = row.shape[1]
    return jnp.sum(jnp.where(iota((n, n), 0) == iota((n, n), 1), row, 0.0), axis=1, keepdims=True)


def to_row(column):
    n = column.shape[0]
    return jnp.sum(jnp.where(iota((n, n), 0) == iota((n, n), 1), column, 0.0), axis=0, keepdims=True)


def plan_kernel(
    row_tiles, per_group, nrows, count_ref, tile_row_hbm, tile_col_hbm, weights_hbm,
    plan_ref, weights_ref, tile_row_ref, tile_col_ref, sems,
):
    load = pltpu.make_async_copy(weights_hbm, weights_ref, sems.at[0])
    lists = (
        pltpu.make_async_copy(tile_row_hbm, tile_row_ref, sems.at[1]),
        pltpu.make_async_copy(tile_col_hbm, tile_col_ref, sems.at[2]),
    )
    for copy in lists:
        copy.start()
    load.start()
    for copy in lists:
        copy.wait()
    slots = tile_row_ref.shape[1]
    length = plan_ref.shape[1]
    my_row, my_col = lax.axis_index("row"), lax.axis_index("col")
    zero_tile = nrows * per_group
    chunk_tiles = row_tiles // CHUNKS
    per_half = per_group // HALVES
    row = tile_row_ref[...]
    rel = (row // per_group) ^ my_col
    chunk = (1 - rel % 2) * HALVES + (row % per_group) // per_half
    order = chunk * chunk_tiles + rel // 2 * per_half + row % per_half
    order = jnp.where(iota((1, slots), 1) < count_ref[0, 0], order, row_tiles).astype(jnp.float32)
    col = tile_col_ref[...]
    source = row_slot((col // per_group) ^ my_row, my_col % 2, nrows) * per_group + col % per_group
    entry = (iota((1, slots), 1) * SHIFT + source).astype(jnp.float32)
    order_c = to_column(order)
    entry_c = to_column(entry)
    same = jnp.where((order_c == order) & (iota((slots, slots), 1) < iota((slots, slots), 0)), 1.0, 0.0)
    within = jnp.sum(same, axis=1, keepdims=True)
    tiles_r = iota((row_tiles, slots), 0).astype(jnp.float32)
    held = jnp.sum(jnp.where(tiles_r == order, 1.0, 0.0), axis=1, keepdims=True).astype(jnp.int32)
    steps = (held + GROUP - 1) // GROUP
    steps_f = steps.astype(jnp.float32)
    square = (row_tiles, row_tiles)
    first = jnp.sum(jnp.where(iota(square, 1) < iota(square, 0), to_row(steps_f), 0.0), axis=1, keepdims=True)
    tile_no, step_no = iota((row_tiles, 1), 0), iota((1, length), 1)
    raw, begin, ends = jnp.int32(0), jnp.int32(0), []
    limit = jnp.full((1, length), row_tiles - 1, jnp.int32)
    shift = jnp.zeros((row_tiles, 1), jnp.int32)
    for c in range(CHUNKS):
        mine = (tile_no >= c * chunk_tiles) & (tile_no < (c + 1) * chunk_tiles)
        size = jnp.sum(jnp.where(mine, steps_f, 0.0)).astype(jnp.int32)
        shift = shift + jnp.where(mine, begin - raw, 0)
        end = begin + size
        if c > 0:
            end = (end + UNROLL - 1) // UNROLL * UNROLL
        limit = jnp.where((step_no >= begin) & (step_no < end), (c + 1) * chunk_tiles - 1, limit)
        raw, begin = raw + size, end
        ends.append(end // UNROLL)
    first = first + shift.astype(jnp.float32)
    lanes = iota((slots, row_tiles), 1).astype(jnp.float32)
    start = jnp.sum(jnp.where(order_c == lanes, to_row(first), 0.0), axis=1, keepdims=True)
    place = jnp.where(order_c < row_tiles, GROUP * start + within, -1.0)
    hit = place == iota((slots, length), 1).astype(jnp.float32)
    listed = jnp.sum(jnp.where(hit, entry_c - zero_tile, 0.0), axis=0, keepdims=True) + zero_tile
    done = (first + steps_f) <= iota((row_tiles, length), 1).astype(jnp.float32)
    owner = jnp.sum(jnp.where(done, 1.0, 0.0), axis=0, keepdims=True).astype(jnp.int32)
    bounds = jnp.zeros((1, length), jnp.int32)
    for c, end in enumerate(ends):
        bounds = jnp.where(step_no == c + 1, end, bounds)
    plan_ref[0:1, :] = listed.astype(jnp.int32)
    plan_ref[1:2, :] = jnp.minimum(owner, limit)
    plan_ref[2:3, :] = bounds
    plan_ref[3:8, :] = jnp.zeros((5, length), jnp.int32)
    load.wait()


def begin_kernel(degree_hbm, embed_hbm, state_ref, *refs):
    square_refs, (degree_ref, embed_ref, sems) = refs[:HALVES], refs[HALVES:]
    half = embed_ref.shape[0] // HALVES
    copies = (
        pltpu.make_async_copy(degree_hbm, degree_ref, sems.at[0]),
        pltpu.make_async_copy(embed_hbm, embed_ref, sems.at[1]),
    )
    for copy in copies:
        copy.start()
    for copy in copies:
        copy.wait()
    lanes = degree_ref.shape[1]
    for i in range(degree_ref.shape[0]):
        scale = to_column(lax.rsqrt(degree_ref[i : i + 1, :].astype(jnp.float32)))
        at = slice(i * lanes, (i + 1) * lanes)
        state_ref[at, :] = (scale * embed_ref[at, :].astype(jnp.float32)).astype(state_ref.dtype)
        inside = i * lanes % half
        square = jnp.broadcast_to(scale * scale, (lanes, embed_ref.shape[1]))
        square_refs[i * lanes // half][inside : inside + lanes, :] = square


def fill_state(pieces, state, halves, tile):
    rows = pieces[0].shape[0]
    devices = (state.shape[0] - tile) // (rows * halves)
    for i, piece in enumerate(pieces):
        half, device = halves - 1 - i // devices, i % devices
        at = (device * halves + half) * rows
        state[at : at + rows, :] = piece[...]
    state[len(pieces) * rows :, :] = jnp.zeros((tile, state.shape[1]), state.dtype)


def multiply(plan_ref, weights_ref, state, total, chunk, chunks, chunk_tiles):
    tile = weights_ref.shape[1]
    total[...] = jnp.zeros_like(total)

    def turn(i, carry):
        prods = []
        for u in range(UNROLL):
            left, right = [], []
            for j in range(GROUP):
                entry = plan_ref[0, (i * UNROLL + u) * GROUP + j]
                left.append(weights_ref[entry >> BITS])
                right.append(state[pl.ds(pl.multiple_of((entry & (SHIFT - 1)) * tile, tile), tile), :])
            prods.append(
                jnp.dot(
                    jnp.concatenate(left, axis=1),
                    jnp.concatenate(right, axis=0),
                    preferred_element_type=jnp.float32,
                )
            )
        for u in range(UNROLL):
            row = plan_ref[1, i * UNROLL + u] - chunk * chunk_tiles
            at = pl.ds(pl.multiple_of(row * tile, tile), tile)
            total[at, :] += prods[u]
        return carry

    lax.fori_loop(plan_ref[2, chunk], plan_ref[2, chunk + chunks], turn, 0)


def odd_kernel(pieces, halves, plan_ref, *refs):
    weights_ref, extra_refs = refs[pieces], refs[pieces + 1 : -3]
    odd_ref, state, total = refs[-3:]
    rows = total.shape[0]
    fill_state(refs[:pieces], state, halves, weights_ref.shape[1])
    multiply(plan_ref, weights_ref, state, total, 0, HALVES, 0)
    odd_ref[0:rows, :] = total[...].astype(odd_ref.dtype)
    for extra in extra_refs:
        odd_ref[rows:, :] = extra[...]


def even0_kernel(plan_ref, state, weights_ref, even_ref):
    multiply(plan_ref, weights_ref, state, even_ref, HALVES, 1, even_ref.shape[0] // weights_ref.shape[1])


def even1_kernel(chips, plan_ref, state, weights_ref, after_ref, other_ref, *refs):
    extra_refs, own_ref, sent_refs, total = refs[: -chips - 1], refs[-chips - 1], refs[-chips:-1], refs[-1]
    rows = total.shape[0]
    multiply(plan_ref, weights_ref, state, total, HALVES + 1, 1, rows // weights_ref.shape[1])
    add_cores(chips, rows, total, other_ref, own_ref, sent_refs)
    for extra in extra_refs:
        size = extra.shape[0]
        far = other_ref[other_ref.shape[0] - size :, :].astype(jnp.float32)
        both = (extra[...].astype(jnp.float32) + pltpu.roll(far, size // 2, 0)).astype(extra.dtype)
        for sent in sent_refs:
            sent[own_ref.shape[0] :, :] = both


def add_cores(chips, offset, even_ref, other_ref, own_ref, sent_refs):
    rows = own_ref.shape[0]
    for k, out in enumerate((own_ref, *sent_refs)):
        other = other_ref[pl.ds(offset + k * rows, rows), :].astype(jnp.float32)
        out[0:rows, :] = (even_ref[pl.ds(k * rows, rows), :] + other).astype(out.dtype)


def merge_kernel(chips, even_ref, other_ref, own_ref, *sent_refs):
    add_cores(chips, 0, even_ref, other_ref, own_ref, sent_refs)


def state_kernel(parts, square_ref, own_ref, *refs):
    state_ref = refs[-1]
    total = own_ref[...]
    for ref in refs[:parts]:
        total = total + ref[0 : total.shape[0], :].astype(jnp.float32)
    state_ref[...] = (square_ref[...] * total).astype(state_ref.dtype)


def place_kernel(chips, rows_here, block_rows, id_rows, mine_ref, other_ref, *refs):
    far_refs, place_ref = refs[:-1], refs[-1]
    my_col = lax.axis_index("col")
    half = rows_here // HALVES
    chunk_rows = block_rows // CHUNKS
    extra = mine_ref.shape[0]

    def places(rows):
        ids = (rows[:id_rows] * BYTE + rows[id_rows : 2 * id_rows]).astype(jnp.int32)
        rel = (ids // rows_here) ^ my_col
        chunk = (1 - rel % 2) * HALVES + ids % rows_here // half
        return chunk * chunk_rows + rel // 2 * half + ids % half

    def tail(ref):
        return ref[ref.shape[0] - extra :, :].astype(jnp.float32)

    even, odd = [mine_ref[...].astype(jnp.float32)], [tail(other_ref)]
    for ref in far_refs:
        rows = tail(ref)
        even.append(rows)
        odd.append(pltpu.roll(rows, extra - extra // 2, 0))
    for k in range(chips):
        for place, rows in ((k, places(odd[k])), (chips + k, places(even[k]))):
            for r in range(id_rows):
                at = (place * id_rows + r) * LANES
                place_ref[0:1, at : at + LANES] = rows[r : r + 1, :]


def pick_rows(place_ref, first, total, picked):
    def some(i, carry):
        for j in range(UNPICK):
            at = i * UNPICK + j
            picked[pl.ds(at, 1), :] = total[pl.ds(place_ref[0, first + at], 1), :]
        return carry

    lax.fori_loop(0, picked.shape[0] // UNPICK, some, 0)


def last_kernel(pieces, halves, plan_ref, place_ref, *refs):
    weights_ref = refs[pieces]
    odd_ref, total, state, picked = refs[pieces + 1 :]
    fill_state(refs[:pieces], state, halves, weights_ref.shape[1])
    multiply(plan_ref, weights_ref, state, total, 0, CHUNKS, 0)
    pick_rows(place_ref, 0, total, picked)
    odd_ref[...] = picked[...].astype(odd_ref.dtype)


def pick_kernel(place_ref, total, even_ref):
    pick_rows(place_ref, even_ref.shape[0], total, even_ref)


def local(
    embed, degree, tile_row, tile_col, tile_count, tile_values, new_rows, new_bucket, bucket_norm
):
    rows_here, width = embed.shape
    ncols, nrows = lax.axis_size("col"), lax.axis_size("row")
    weights = tile_values[0, 0]
    slots, tile = weights.shape[:2]
    chips = ncols // 2
    block_rows = ncols * rows_here
    row_tiles = block_rows // tile
    per_group = rows_here // tile
    half_here = rows_here // HALVES
    chunk_rows = block_rows // CHUNKS
    zero_tile = nrows * per_group
    new_here = new_rows.shape[0]
    id_rows = new_here // LANES
    id_block = -(-4 * id_rows // PACK) * PACK
    length = -(-(slots + GROUP * (row_tiles + CHUNKS * UNROLL)) // LANES) * LANES
    f32, bf16 = jnp.float32, jnp.bfloat16
    array = jax.ShapeDtypeStruct
    in_hbm = lambda x: pltpu.with_memory_space_constraint(x, pltpu.HBM)
    in_vmem = lambda x: pltpu.with_memory_space_constraint(x, pltpu.VMEM)

    def call(kernel, name, out_shape, args, scalars=0, in_specs=None, scratch=(), turns=0.0):
        many = isinstance(out_shape, (list, tuple))
        cost = pl.CostEstimate(
            flops=int(turns * 2 * slots * tile * tile * width),
            bytes_accessed=int(turns * 2 * slots * tile * tile),
            transcendentals=0,
        )
        return pl.pallas_call(
            kernel,
            out_shape=out_shape,
            grid_spec=pltpu.PrefetchScalarGridSpec(
                num_scalar_prefetch=scalars,
                grid=(),
                in_specs=in_specs or [VMEM_SPEC] * (len(args) - scalars),
                out_specs=[VMEM_SPEC] * len(out_shape) if many else VMEM_SPEC,
                scratch_shapes=list(scratch),
            ),
            compiler_params=PARAMS,
            cost_estimate=cost if turns else None,
            name=name,
        )(*args)

    def swap_cores(odd):
        return lax.ppermute(odd, "col", [(i, i ^ 1) for i in range(ncols)])

    def send(sent):
        return [
            lax.ppermute(part, "col", [(i, i ^ (2 * k)) for i in range(ncols)]) for k, part in enumerate(sent, 1)
        ]

    def spread(state):
        pieces = [state]
        for slot in range(1, nrows):
            masks = [row_mask(slot, core, nrows) for core in range(2)]
            pairs = [
                (r * ncols + c, (r ^ masks[c % 2]) * ncols + c) for r in range(nrows) for c in range(ncols)
            ]
            pieces.append(lax.ppermute(state, ("row", "col"), pairs))
        return pieces

    state, *squares = call(
        begin_kernel,
        "begin",
        [array(embed.shape, bf16)] + [array((half_here, width), f32)] * HALVES,
        (in_hbm(degree.reshape(rows_here // LANES, LANES)), in_hbm(embed)),
        in_specs=[HBM_SPEC, HBM_SPEC],
        scratch=[
            pltpu.VMEM((rows_here // LANES, LANES), jnp.int32),
            pltpu.VMEM(embed.shape, bf16),
            pltpu.SemaphoreType.DMA((2,)),
        ],
    )
    pieces = spread(state)

    plan, weights = call(
        functools.partial(plan_kernel, row_tiles, per_group, nrows),
        "plan",
        [array((8, length), jnp.int32), pltpu.VMEM(weights.shape, weights.dtype)],
        (tile_count, in_hbm(tile_row[0]), in_hbm(tile_col[0]), in_hbm(weights)),
        in_specs=[SMEM_SPEC, HBM_SPEC, HBM_SPEC, HBM_SPEC],
        scratch=[
            pltpu.VMEM((1, slots), jnp.int32),
            pltpu.VMEM((1, slots), jnp.int32),
            pltpu.SemaphoreType.DMA((3,)),
        ],
    )
    weights = in_vmem(weights)

    inside = (new_rows - lax.axis_index("row") * block_rows).reshape(id_rows, LANES)
    mine = jnp.concatenate([inside // BYTE, inside % BYTE]).astype(bf16)
    mine = jnp.pad(mine, ((0, id_block - 2 * id_rows), (0, 0)))

    state_shape = ((zero_tile + 1) * tile, width)

    def sums_shape(rows, more=0):
        return [array((rows, width), f32)] + [array((rows + more, width), bf16)] * (chips - 1)

    def merge(even, other):
        own, *sent = call(
            functools.partial(merge_kernel, chips), "merge", sums_shape(even.shape[0] // chips), (even, other)
        )
        return own, send(sent)

    def add(own, came):
        for part in came:
            own = own + part[: own.shape[0]].astype(f32)
        return own

    for hop in range(HOPS - 1):
        extra = (mine,)
        odd, held = call(
            functools.partial(odd_kernel, len(pieces), len(pieces) // nrows),
            "odd",
            [
                array((HALVES * chunk_rows + len(extra) * id_block, width), bf16),
                array(state_shape, bf16),
            ],
            (plan, *pieces, weights, *extra),
            scalars=1,
            scratch=[pltpu.VMEM((HALVES * chunk_rows, width), f32)],
            turns=0.5,
        )
        other = swap_cores(odd)
        even0 = call(
            even0_kernel, "even0", array((chunk_rows, width), f32), (plan, held, weights), scalars=1, turns=0.25
        )
        own0, came0 = merge(even0, other)
        own1, *sent1 = call(
            functools.partial(even1_kernel, chips),
            "even1",
            sums_shape(half_here, len(extra) * id_block),
            (plan, held, weights, own0, other, *extra),
            scalars=1,
            scratch=[pltpu.VMEM((chunk_rows, width), f32)],
            turns=0.25,
        )
        came1 = send(sent1)
        if hop == 0:
            place = call(
                functools.partial(place_kernel, chips, rows_here, block_rows, id_rows),
                "place",
                array((1, ncols * new_here), jnp.int32),
                (mine, other, *came1),
            )
        parts, after = [], ()
        for square, own, came in zip(squares, (own0, own1), (came0, came1)):
            half_state = call(
                functools.partial(state_kernel, len(came)),
                "state",
                array(square.shape, bf16),
                (square, own, *came, *after),
            )
            parts.append(spread(half_state))
            after = (half_state,)
        pieces = [parts[half][r] for half in reversed(range(HALVES)) for r in range(nrows)]

    odd, total = call(
        functools.partial(last_kernel, len(pieces), len(pieces) // nrows),
        "last",
        [array((chips * new_here, width), bf16), array((block_rows, width), f32)],
        (plan, place, *pieces, weights),
        scalars=2,
        scratch=[pltpu.VMEM(state_shape, bf16), pltpu.VMEM((chips * new_here, width), f32)],
        turns=1.0,
    )
    other = swap_cores(odd)
    even = call(pick_kernel, "pick", array((chips * new_here, width), f32), (place, total), scalars=1, turns=0.2)
    picked = add(*merge(even, other))
    buckets = jnp.arange(bucket_norm.shape[0], dtype=jnp.int32)
    target = jnp.sum(
        jnp.where(new_bucket[:, None] == buckets[None, :], bucket_norm[None, :], jnp.float32(0.0)),
        axis=1,
    )
    return (
        target[:, None]
        * picked
        * lax.rsqrt(jnp.sum(picked * picked, axis=1, keepdims=True) + 1e-06)
    )


def solution(mesh):
    in_specs = (
        P(("row", "col"), None),
        P(("row", "col")),
        P("row", "col", None),
        P("row", "col", None),
        P("row", "col"),
        P("row", "col", None, None, None),
        P(("row", "col")),
        P(("row", "col")),
        P(),
    )
    out_specs = P(("row", "col"), None)
    return jax.shard_map(local, mesh=mesh, in_specs=in_specs, out_specs=out_specs, check_vma=False)
```
